32 devices in a mesh: ctx: 8 (over y, x, core), exp: 4 (over z).
Axes of the slice: x: 2, y: 2, z: 4, core: 2. Of those that a mesh axis runs over, the one named last changes fastest.
Arguments:
- queries: bfloat16 [2048, 4096], P('ctx', 'exp'), may hold values from -6 to 6
- key_rows: bfloat16 [2048, 4096], P('ctx', 'exp'), may hold values from -6 to 6
- value_rows: bfloat16 [2048, 4096], P('ctx', 'exp'), may hold values from -6 to 6
- decay_rate: float32 [32], P('exp'), may hold values from 1.953125e-05 to 0.06
- out_weight: bfloat16 [4096, 3072], P('exp', 'ctx'), may hold values from -0.09375 to 0.09375
- residual: bfloat16 [2048, 3072], P(('ctx', 'exp')), may hold values from -6 to 6
- moe_gain: float32 [3072], replicated, may hold values from 0.1 to 1.9
- expert_ids: int32 [2048, 2], P(('ctx', 'exp')), may hold values from 0 to 3, all different within a row; in each aligned block of 64 rows (0 to 63, 64 to 127, ...) at most 48 rows name the same one
- gate_weight: bfloat16 [4, 4608, 3072], P('exp', 'ctx'), may hold values from -0.109375 to 0.109375
- up_weight: bfloat16 [4, 4608, 3072], P('exp', 'ctx'), may hold values from -0.109375 to 0.109375
Outputs:
- mixed: bfloat16 [2048, 3072], P(('ctx', 'exp'))
- expert_hidden: bfloat16 [4, 4608, 1536], P('exp', 'ctx')
The draws below stay inside these ranges and needn't reach their ends.
Inputs may be any that keep to these rules, and one draw needn't show every extreme that they name: `expert_ids`: in each aligned block of 64 tokens (the rows of one device) no expert is named by more than 48 of the block's routes; some block names some expert exactly 48 times; a token's two ids differ.
All inputs are finite; a program needn't handle non-finite values.
Results may differ from the reference program's by a relative error of at most 0.0079.
Values may be sent and summed in bfloat16 or wider, within the bound.
No kernel may reach another device: no remote copies, remote signals or barrier semaphores. Data moves between devices by JAX's collectives and lax.ppermute only.
A program may use at most 64 MiB of HBM per device.

```python
import math
import jax
import jax.numpy as jnp
import numpy as np
from jax import lax

D = 3072
HEAD_DIM = 128
HEADS = 32
HID = 4608
SPAN = 256
SEQ = 2048
TOK_DEV = 64
EXPERTS = 4
CAP = 48
SLOTS = 1536


def levels(rng, extent, shards, smallest, top_value):
    factor_of, own = 1.0, jax.random.fold_in(rng, 6)
    for dim, shards_of in shards:
        steps = jnp.exp(jax.random.uniform(jax.random.fold_in(own, dim), (shards_of,), jnp.float32, smallest / len(shards), top_value / len(shards)))
        factor_of = factor_of * jnp.repeat(steps, extent[dim] // shards_of).reshape([-1 if axis == dim else 1 for axis in range(len(extent))])
    return factor_of


def routed_block(own_key, own, number, rows, amount, top, bound, skew):
    ranking = jax.random.permutation(own_key, amount)
    heavy_load, ordinary = load_shares(amount, rows * top, bound, skew, True), load_shares(amount, rows * top, bound, skew, False)
    places = jnp.arange(amount)

    def named(sizes, offset_by):
        used = int((sizes > 0).sum())
        fixed = max(1, used // 4)
        passed = fixed + (places - fixed + offset_by * (used - fixed)) % max(1, amount - fixed)
        return jnp.zeros((amount,), jnp.int32).at[ranking[jnp.where(places < fixed, places, passed)]].set(jnp.asarray(sizes, jnp.int32))

    sizes = jnp.where(number % 4 == 0, named(heavy_load, number // 4), named(ordinary, number - number // 4 - 1))
    mixed = jax.random.permutation(jax.random.fold_in(own, 3), amount)
    source_of, sink = mixed[0:amount // 2 * 2:2], mixed[1:amount // 2 * 2:2]
    margin = jnp.minimum(sizes[source_of] - 1, bound - sizes[sink]) // 2
    margin = jnp.where((source_of == ranking[0]) | (sink == ranking[0]) | (sizes[sink] == 0), 0, jnp.maximum(margin, 0))
    passed = jax.random.randint(jax.random.fold_in(own, 4), (amount // 2,), 0, 1 << 20) % (margin + 1)
    sizes = sizes.at[source_of].add(-passed).at[sink].add(passed)
    members = jnp.searchsorted(jnp.cumsum(sizes), jnp.arange(rows * top), side="right").astype(jnp.int32)
    table = members.reshape(top, rows).T
    table = table[jax.random.permutation(jax.random.fold_in(own, 1), rows)]
    offset_by = jax.random.randint(jax.random.fold_in(own, 2), (rows, 1), 0, top)
    return jnp.take_along_axis(table, (jnp.arange(top)[None, :] + offset_by) % top, axis=1)


def load_shares(number_of, total, bound, skew, full):
    loads = [(1 << 20) // math.isqrt(rank ** skew) + 1 for rank in range(1, number_of + 1)]
    largest = bound if full else min(bound, max(-(-total // number_of), total * loads[0] // sum(loads)))
    least = 1 if total - largest >= number_of - 1 else 0
    holding, surplus = [largest] + [least] * (number_of - 1), total - largest - least * (number_of - 1)
    while surplus > 0:
        candidates = [i for i in range(1, number_of) if holding[i] < largest] or [i for i in range(1, number_of) if holding[i] < bound]
        pool, remaining = sum([loads[i] for i in candidates]), surplus
        for i in candidates:
            addition = min(bound - holding[i], max(1, remaining * loads[i] // pool), surplus)
            holding[i] = holding[i] + addition
            surplus = surplus - addition
    return np.array(holding)


def gaussian(rng, shape, spread, reach, split=(), kind=jnp.bfloat16):
    array = jax.random.normal(rng, shape, jnp.float32) * spread
    if len(split) > 0:
        array = levels(rng, shape, split, -0.22, 0.18) * array
    return jnp.clip(array, min=-reach, max=reach).astype(kind)


def setup_inputs(seed: int = 0) -> dict:
    splits = jax.random.split(jax.random.key(seed), 11)
    queries = gaussian(splits[0], (SEQ, HEADS * HEAD_DIM), 1.0, 6.0, ((0, 8), (1, 4)))
    key_rows = gaussian(splits[1], (SEQ, HEADS * HEAD_DIM), 1.0, 6.0, ((0, 8), (1, 4)))
    value_rows = gaussian(splits[2], (SEQ, HEADS * HEAD_DIM), 1.0, 6.0, ((0, 8), (1, 4)))
    decay_rate = jnp.clip(jnp.exp(math.log(0.06) - 8.030084 * jax.random.uniform(splits[3], (HEADS,), jnp.float32) ** levels(splits[3], (HEADS,), ((0, 4),), -0.2, 0.2)), 1.9531249563442543e-05, 0.06)
    out_weight = gaussian(splits[4], (HEADS * HEAD_DIM, D), (HEADS * HEAD_DIM) ** -0.5, 0.09375, ((0, 4), (1, 8)))
    residual = gaussian(splits[5], (SEQ, D), 1.0, 6.0, ((0, 32),))
    moe_gain = jnp.clip(1.0 + 0.18 * jax.random.normal(splits[6], (D,), jnp.float32), 0.1, 1.9)
    expert_ids_keys = jax.random.split(jax.random.fold_in(splits[7], 1), SEQ // TOK_DEV)
    expert_ids_turns = jax.random.permutation(jax.random.fold_in(splits[7], 3), SEQ // TOK_DEV)
    expert_ids = jax.vmap(lambda own, number: routed_block(jax.random.fold_in(splits[7], 2), own, number, TOK_DEV, EXPERTS, 2, CAP, 2))(expert_ids_keys, expert_ids_turns).reshape((SEQ, 2))
    gate_weight = gaussian(splits[8], (EXPERTS, HID, D), D ** -0.5, 0.109375, ((0, 4), (1, 8)))
    up_weight = gaussian(splits[9], (EXPERTS, HID, D), D ** -0.5, 0.109375, ((0, 4), (1, 8)))
    return dict(queries=queries, key_rows=key_rows, value_rows=value_rows, decay_rate=decay_rate, out_weight=out_weight, residual=residual, moe_gain=moe_gain, expert_ids=expert_ids, gate_weight=gate_weight, up_weight=up_weight)


def route_slots(id_rows):
    count = id_rows.shape[1]
    same = id_rows[:, :, None] == id_rows[:, None, :]
    before = lax.broadcasted_iota(jnp.int32, (count, count), 1) < lax.broadcasted_iota(jnp.int32, (count, count), 0)
    return lax.optimization_barrier(jnp.sum((same & before[None]).astype(jnp.int32), axis=2)).astype(jnp.int32)

def select_matrix(id_rows, slot_rows, owners, capacity):
    routes = id_rows.shape[1]
    places = jnp.arange(capacity, dtype=jnp.int32)
    hits = (id_rows[:, None, None, :] == owners[None, :, None, None]) & (slot_rows[:, None, None, :] == places[None, None, :, None])
    to_token = (jnp.arange(routes, dtype=jnp.int32)[:, None] // 2 == jnp.arange(routes // 2, dtype=jnp.int32)[None, :]).astype(jnp.float32)
    return jnp.einsum('bepr,rt->bept', hits.astype(jnp.float32), to_token)

def reference(queries, key_rows, value_rows, decay_rate, out_weight, residual, moe_gain, expert_ids, gate_weight, up_weight):
    highest = lax.Precision.HIGHEST
    blocks = SEQ // SPAN
    query_blk = queries.reshape(blocks, SPAN, HEADS, HEAD_DIM)
    key_blk = key_rows.reshape(blocks, SPAN, HEADS, HEAD_DIM)
    value_blk = value_rows.reshape(blocks, SPAN, HEADS, HEAD_DIM)
    position = jnp.arange(SPAN, dtype=jnp.float32)
    offset = position[:, None] - position[None, :]
    masked = jnp.where((offset >= 0)[None], jnp.exp(-decay_rate[:, None, None] * jnp.maximum(offset, 0.0)[None]), 0.0)
    inner = jnp.exp(-decay_rate[None, :] * position[:, None])
    tail = jnp.exp(-decay_rate[None, :] * (SPAN - position[:, None]))
    whole = jnp.exp(-decay_rate * SPAN)

    def advance(state, pieces):
        query_f = pieces[0].astype(jnp.float32)
        key_f = pieces[1].astype(jnp.float32)
        value_f = pieces[2].astype(jnp.float32)
        scores = jnp.einsum('ihd,jhd->hij', query_f, key_f, precision=highest)
        weighted = (scores * masked).astype(jnp.bfloat16)
        local_part = jnp.einsum('hij,jhd->ihd', weighted.astype(jnp.float32), value_f, precision=highest)
        carried = jnp.einsum('ihd,hde->ihe', query_f, state, precision=highest) * inner[:, :, None]
        fresh = jnp.einsum('jhd,jhe->hde', key_f * tail[:, :, None], value_f, precision=highest)
        return (whole[:, None, None] * state + fresh, local_part + carried)
    start_state = jnp.zeros((HEADS, HEAD_DIM, HEAD_DIM), jnp.float32)
    unused, attended = lax.scan(advance, start_state, (query_blk, key_blk, value_blk))
    scale_rows = lax.rsqrt(lax.optimization_barrier(jnp.mean(attended * attended, axis=-1, keepdims=True)) + 1e-05)
    head_out = (attended * scale_rows).astype(jnp.bfloat16).reshape(SEQ, HEADS * HEAD_DIM)
    attn = jnp.dot(head_out, out_weight, preferred_element_type=jnp.float32)
    mixed = (residual.astype(jnp.float32) + attn).astype(jnp.bfloat16)
    mixed_f = mixed.astype(jnp.float32)
    normed = (mixed_f * lax.rsqrt(lax.optimization_barrier(jnp.mean(mixed_f * mixed_f, axis=-1, keepdims=True)) + 1e-05) * moe_gain).astype(jnp.bfloat16)
    groups = SEQ // TOK_DEV
    id_rows = expert_ids.reshape(groups, 2 * TOK_DEV).astype(jnp.int32)
    slot_rows = route_slots(id_rows)
    normed_blk = normed.reshape(groups, TOK_DEV, D).astype(jnp.float32)
    contract = (((1,), (1,)), ((), ()))

    def one_expert(items):
        owner, gate_here, up_here = items
        picks = select_matrix(id_rows, slot_rows, jnp.reshape(owner, (1,)), CAP)[:, 0]
        rows = jnp.einsum('bpt,btd->bpd', picks, normed_blk).reshape(SLOTS, D).astype(jnp.bfloat16)
        gated = lax.dot_general(gate_here, rows, contract, preferred_element_type=jnp.float32)
        lifted = lax.dot_general(up_here, rows, contract, preferred_element_type=jnp.float32)
        return (jax.nn.silu(gated) * lifted).astype(jnp.bfloat16)
    expert_hidden = lax.map(one_expert, (jnp.arange(EXPERTS, dtype=jnp.int32), gate_weight, up_weight))
    return (mixed, expert_hidden)
```

```python
import functools

import jax
import jax.numpy as jnp
from jax import lax
from jax.experimental import pallas as pl
from jax.experimental.pallas import tpu as pltpu
from jax.sharding import PartitionSpec as P

GROUPS = 4
VMEM_LIMIT = 48 * 1024 * 1024
BF16 = jnp.bfloat16
F32 = jnp.float32
NT = (((1,), (1,)), ((), ()))
TN = (((0,), (0,)), ((), ()))
NN = (((1,), (0,)), ((), ()))


def dot(a, b, dims):
    return lax.dot_general(a, b, dims, preferred_element_type=F32)


def halves(x):
    high = x.astype(BF16)
    return high, (x - high.astype(F32)).astype(BF16)


def call(kernel, out_shape, flops, nbytes, exps=0, **kwargs):
    return pl.pallas_call(
        kernel,
        out_shape=out_shape,
        compiler_params=pltpu.CompilerParams(vmem_limit_bytes=VMEM_LIMIT),
        cost_estimate=pl.CostEstimate(
            flops=int(flops), bytes_accessed=int(nbytes), transcendentals=int(exps)
        ),
        **kwargs,
    )


VM = pl.BlockSpec(memory_space=pltpu.VMEM)
SM = pl.BlockSpec(memory_space=pltpu.SMEM)


def fresh_kernel(rate_ref, k_ref, v_ref, out_ref):
    heads, size = out_ref.shape[0], out_ref.shape[1]
    length = k_ref.shape[0]
    left = length - lax.broadcasted_iota(jnp.int32, (length, size), 0).astype(F32)
    for h in range(heads):
        cols = slice(h * size, (h + 1) * size)
        tail = jnp.exp(-rate_ref[h] * left)
        high, low = halves(k_ref[:, cols].astype(F32) * tail)
        v = v_ref[:, cols]
        out_ref[h] = dot(high, v, TN) + dot(low, v, TN)


def local_kernel(rate_ref, q_ref, k_ref, v_ref, out_ref):
    heads = rate_ref.shape[0]
    length = k_ref.shape[0]
    size = k_ref.shape[1] // heads
    rows = lax.broadcasted_iota(jnp.int32, (length, length), 0)
    cols = lax.broadcasted_iota(jnp.int32, (length, length), 1)
    offset = (rows - cols).astype(F32)
    keep = offset >= 0
    offset = jnp.maximum(offset, 0.0)
    for h in range(heads):
        at = slice(h * size, (h + 1) * size)
        masked = jnp.where(keep, jnp.exp(-rate_ref[h] * offset), 0.0)
        weighted = (dot(q_ref[:, at], k_ref[:, at], NT) * masked).astype(BF16)
        out_ref[:, at] = dot(weighted, v_ref[:, at], NN)


def head_kernel(rate_ref, coef_ref, q_ref, local_ref, state_ref, got_ref, out_ref):
    heads, size = state_ref.shape[0], state_ref.shape[1]
    length = q_ref.shape[0]
    pos = lax.broadcasted_iota(jnp.int32, (length, size), 0).astype(F32)
    for h in range(heads):
        at = slice(h * size, (h + 1) * size)
        state = state_ref[h] + coef_ref[h] * got_ref[h].astype(F32)
        high, low = halves(state)
        q = q_ref[:, at]
        carried = (dot(q, high, NN) + dot(q, low, NN)) * jnp.exp(-rate_ref[h] * pos)
        attended = local_ref[:, at] + carried
        scale = lax.rsqrt(jnp.mean(attended * attended, axis=-1, keepdims=True) + 1e-05)
        out_ref[:, at] = (attended * scale).astype(BF16)


def xor_permute(x, step):
    n = lax.axis_size("ctx")
    return lax.ppermute(x, "ctx", [(d, d ^ step) for d in range(n)])


def across_groups(x):
    low = lax.axis_size("ctx") // GROUPS
    cut = x.shape[0] // 2
    one = xor_permute(x, low)
    two = xor_permute(x, 2 * low)
    top = xor_permute(one[:cut], 2 * low)
    bottom = xor_permute(two[cut:], low)
    return [x, one, two, jnp.concatenate([top, bottom], axis=0)]


def within_group(x):
    n = lax.axis_size("ctx")
    low = n // GROUPS
    got = [x]
    for step in range(1, low):
        got.append(
            lax.ppermute(
                x, "ctx", [(d, d // low * low + (d % low - step) % low) for d in range(n)]
            )
        )
    return got


def in_order(pieces, member, axis):
    low, width = len(pieces), pieces[0].shape[axis]
    ring = jnp.concatenate(pieces + pieces[:-1], axis=axis)
    return lax.dynamic_slice_in_dim(ring, lax.rem(low - member, low) * width, low * width, axis)


def line_sum(part, place):
    n = lax.axis_size("exp")
    half = n // 2
    for hop in range(half - 1):
        got = lax.ppermute(part.astype(BF16), "exp", [(hop, hop + 1), (n - 1 - hop, n - 2 - hop)])
        part = part + got.astype(F32)
    mine = part.astype(BF16)
    other = lax.ppermute(mine, "exp", [(half - 1, half), (half, half - 1)])
    total = (mine.astype(F32) + other.astype(F32)).astype(BF16)
    for hop in range(half - 1):
        here, there = half - 1 - hop, half + hop
        got = lax.ppermute(total, "exp", [(here, here - 1), (there, there + 1)])
        total = jnp.where((place == here - 1) | (place == there + 1), got, total)
    return total


def expert_kernel(chunks, low, final, has_acc, place_ref, *refs):
    refs = list(refs)
    pieces = [[refs.pop(0) for _ in range(low)] for _ in range(chunks)]
    gates = [refs.pop(0) for _ in range(chunks)]
    ups = [refs.pop(0) for _ in range(chunks)]
    sums = [refs.pop(0), refs.pop(0)] if has_acc else None
    if final and final != "first":
        refs.pop(0)
    outs = [refs.pop(0)] if final else [refs.pop(0), refs.pop(0)]
    held = refs
    rows = pieces[0][0].shape[0]

    @pl.when(pl.program_id(0) == 0)
    def _():
        for t in range(chunks):
            for a in range(low):
                member = lax.rem(place_ref[1] + a, low)
                held[t][pl.ds(pl.multiple_of(member * rows, rows), rows), :] = pieces[t][a][...]

    width = gates[0].shape[1]
    gated, lifted = (sums[0][...], sums[1][...]) if has_acc else (0.0, 0.0)
    for t in range(chunks):
        x = held[t][:, :width]
        gated = gated + dot(gates[t][...], x, NT)
        lifted = lifted + dot(ups[t][...], x, NT)
    if final:
        extra = held[chunks - 1][:, width:]
        pick = (lax.broadcasted_iota(jnp.int32, (8, extra.shape[1]), 1) < 3).astype(BF16)
        scale = dot(pick, extra, NT)[0:1, :]
        gated, lifted = gated * scale, lifted * scale
        outs[0][...] = (gated / (1.0 + jnp.exp(-gated)) * lifted).astype(BF16)
    else:
        outs[0][...] = gated
        outs[1][...] = lifted


def expert_step(place, s, chunk_ids, pieces, gate, up, sums, hidden, final, width):
    hid = gate.shape[0]
    low, rows = len(pieces[0]), pieces[0][0].shape[0]
    slots = low * rows
    block = max(b for b in range(16, min(hid, 192) + 1, 16) if hid % b == 0)
    chunks = len(chunk_ids)
    has_acc = sums is not None

    def whole(x):
        return pl.BlockSpec(x.shape, lambda r, p: (0, 0))

    def weight(t):
        return pl.BlockSpec((block, width), lambda r, p: (r, p[0] ^ (s ^ t)))

    acc_spec = pl.BlockSpec((block, slots), lambda r, p: (r, 0))
    operands = [x for per in pieces for x in per]
    specs = [whole(x) for x in operands]
    operands += [gate] * chunks + [up] * chunks
    specs += [weight(t) for t in chunk_ids] * 2
    if has_acc:
        operands += list(sums)
        specs += [acc_spec] * 2
    aliases = {}
    if final:
        out_shape = jax.ShapeDtypeStruct((hid, slots * GROUPS), BF16)
        out_specs = pl.BlockSpec((block, slots), lambda r, p: (r, p[0] ^ s))
        if hidden is not None:
            operands.append(hidden)
            specs.append(pl.BlockSpec(memory_space=pl.ANY))
            aliases = {len(operands): 0}
        mode = "first" if hidden is None else "next"
    else:
        out_shape = [jax.ShapeDtypeStruct((hid, slots), F32)] * 2
        out_specs = [acc_spec] * 2
        mode = None
    return call(
        functools.partial(expert_kernel, chunks, low, mode, has_acc),
        out_shape,
        4 * hid * slots * width * chunks,
        4 * hid * width * chunks + 8 * hid * slots * (1 + has_acc) + 2 * slots * width * chunks,
        hid * slots if final else 0,
        grid_spec=pltpu.PrefetchScalarGridSpec(
            num_scalar_prefetch=1,
            grid=(hid // block,),
            in_specs=specs,
            out_specs=out_specs,
            scratch_shapes=[pltpu.VMEM((slots, per[0].shape[1]), BF16) for per in pieces],
        ),
        input_output_aliases=aliases,
    )(place, *operands)


def per_device(
    queries,
    key_rows,
    value_rows,
    decay_rate,
    out_weight,
    residual,
    moe_gain,
    expert_ids,
    gate_weight,
    up_weight,
):
    n_ctx, n_exp = lax.axis_size("ctx"), lax.axis_size("exp")
    low = n_ctx // GROUPS
    ctx, exp = lax.axis_index("ctx"), lax.axis_index("exp")
    group, member = ctx // low, lax.rem(ctx, low)
    place = jnp.stack([group, member]).astype(jnp.int32)
    length, here = queries.shape
    heads = decay_rate.shape[0]
    size = here // heads
    model = residual.shape[1]
    width = model // GROUPS
    tokens = length // n_exp
    capacity = max(2, 3 * tokens // n_exp)

    state_type = jax.ShapeDtypeStruct((heads, size, size), F32)
    total = call(
        fresh_kernel,
        state_type,
        4 * heads * length * size * size,
        4 * length * here + 4 * heads * size * size,
        heads * length * size,
        in_specs=[SM, VM, VM],
        out_specs=VM,
    )(decay_rate, key_rows, value_rows)
    local = call(
        local_kernel,
        jax.ShapeDtypeStruct((length, here), F32),
        4 * heads * length * length * size,
        10 * length * here,
        heads * length * length,
        in_specs=[SM, VM, VM, VM],
        out_specs=VM,
    )(decay_rate, queries, key_rows, value_rows)

    def fade(blocks):
        return jnp.exp(-decay_rate * (length * blocks))

    state = jnp.zeros_like(total)
    got, coef = jnp.zeros(total.shape, BF16), jnp.zeros_like(decay_rate)
    step = 1
    while step < n_ctx:
        upper = (ctx & step) != 0
        coef = jnp.where(upper, fade((ctx & (step - 1)).astype(F32)), 0.0)
        if 2 * step < n_ctx:
            got = xor_permute(total.astype(BF16), step)
            gotten = got.astype(F32)
            state = state + coef[:, None, None] * gotten
            span = fade(float(step))[:, None, None]
            total = jnp.where(upper, span * gotten + total, span * total + gotten)
        else:
            got = lax.ppermute(total.astype(BF16), "ctx", [(d, d + step) for d in range(step)])
        step *= 2
    head_out = call(
        head_kernel,
        jax.ShapeDtypeStruct((length, here), BF16),
        4 * heads * length * size * size,
        8 * length * here + 6 * heads * size * size,
        heads * length * size,
        in_specs=[SM, SM, VM, VM, VM, VM],
        out_specs=VM,
    )(decay_rate, coef, queries, local, state, got)

    columns = [in_order(within_group(w), member, 1) for w in across_groups(out_weight)]

    ids = expert_ids.T
    id_parts = [ids]
    for shift in range(1, n_exp):
        id_parts.append(
            lax.ppermute(ids, "exp", [(d, (d - shift) % n_exp) for d in range(n_exp)])
        )
    all_ids = in_order_ring(id_parts, exp)
    named = (all_ids[0] == exp) | (all_ids[1] == exp)
    token = jnp.arange(length, dtype=jnp.int32)
    earlier = (token[:, None] < token[None, :]) & (
        token[:, None] // tokens == token[None, :] // tokens
    )
    rank = jnp.sum((earlier & named[:, None]).astype(jnp.int32), axis=0)
    row = jnp.where(named & (rank < capacity), token // tokens * capacity + rank, -1)
    slots = jnp.arange(n_exp * capacity, dtype=jnp.int32)
    picks = slots[:, None] == row[None, :]

    own_rows = (exp * tokens).astype(jnp.int32)
    mixed_out = jnp.zeros((tokens, model), BF16)
    squares = jnp.zeros((length,), F32)
    received = []
    for t in range(GROUPS):
        start = ((group ^ t) * width).astype(jnp.int32)
        part = dot(head_out, columns[t], NN)
        own = lax.dynamic_slice(residual, (jnp.int32(0), start), (tokens, width)).astype(F32)
        tiled = jnp.tile(own, (n_exp, 1))
        part = part + jnp.where((token // tokens == exp)[:, None], tiled, 0.0)
        mixed = line_sum(part, exp)
        mixed_out = lax.dynamic_update_slice(
            mixed_out,
            lax.dynamic_slice(mixed, (own_rows, jnp.int32(0)), (tokens, width)),
            (jnp.int32(0), start),
        )
        mixed_f = mixed.astype(F32)
        squares = squares + jnp.sum(mixed_f * mixed_f, axis=1)
        gain = lax.dynamic_slice(moe_gain, (start,), (width,))
        rows = dot(picks.astype(BF16), (mixed_f * gain).astype(BF16), NN).astype(BF16)
        if t == GROUPS - 1:
            scale = lax.rsqrt(squares / model + 1e-05)
            scale = jnp.sum(jnp.where(picks, scale[None, :], 0.0), axis=1)
            high, rest = scale.astype(BF16), scale
            parts = []
            for _ in range(3):
                high = rest.astype(BF16)
                rest = rest - high.astype(F32)
                parts.append(high)
            extra = jnp.stack(parts, axis=1)
            rows = jnp.concatenate(
                [rows, jnp.pad(extra, ((0, 0), (0, 128 - extra.shape[1])))], axis=1
            )
        received.append([within_group(x) for x in across_groups(rows)])

    gate, up = gate_weight[0], up_weight[0]
    sums = [None] * GROUPS
    early = list(range(GROUPS - 1))
    for s in range(GROUPS):
        sums[s] = expert_step(
            place, s, early, [received[t][s] for t in early], gate, up, None, None, False, width
        )
    hidden = None
    for s in range(GROUPS):
        last = GROUPS - 1
        hidden = expert_step(
            place, s, [last], [received[last][s]], gate, up, sums[s], hidden, True, width
        )
    return (mixed_out, hidden[None])


def in_order_ring(parts, first):
    n, width = len(parts), parts[0].shape[1]
    ring = jnp.concatenate(parts + parts[:-1], axis=1)
    return lax.dynamic_slice_in_dim(ring, lax.rem(n - first, n) * width, n * width, 1)


def solution(mesh):
    in_specs = (
        P("ctx", "exp"),
        P("ctx", "exp"),
        P("ctx", "exp"),
        P("exp"),
        P("exp", "ctx"),
        P(("ctx", "exp"), None),
        P(),
        P(("ctx", "exp"), None),
        P("exp", "ctx", None),
        P("exp", "ctx", None),
    )
    out_specs = (P(("ctx", "exp"), None), P("exp", "ctx", None))
    return jax.shard_map(
        per_device, mesh=mesh, in_specs=in_specs, out_specs=out_specs, check_vma=False
    )
```

```python
import functools

import jax
import jax.numpy as jnp
from jax import lax
from jax.experimental import pallas as pl
from jax.experimental.pallas import tpu as pltpu
from jax.sharding import PartitionSpec as P

GROUPS = 4
VMEM_LIMIT = 48 * 1024 * 1024
BF16 = jnp.bfloat16
F32 = jnp.float32
NT = (((1,), (1,)), ((), ()))
TN = (((0,), (0,)), ((), ()))
NN = (((1,), (0,)), ((), ()))


def dot(a, b, dims):
    return lax.dot_general(a, b, dims, preferred_element_type=F32)


def halves(x):
    high = x.astype(BF16)
    return high, (x - high.astype(F32)).astype(BF16)


def call(kernel, out_shape, flops, nbytes, exps=0, **kwargs):
    return pl.pallas_call(
        kernel,
        out_shape=out_shape,
        compiler_params=pltpu.CompilerParams(vmem_limit_bytes=VMEM_LIMIT),
        cost_estimate=pl.CostEstimate(
            flops=int(flops), bytes_accessed=int(nbytes), transcendentals=int(exps)
        ),
        **kwargs,
    )


VM = pl.BlockSpec(memory_space=pltpu.VMEM)
SM = pl.BlockSpec(memory_space=pltpu.SMEM)


def fresh_kernel(place_ref, rate_ref, k_ref, v_ref, *outs):
    part, size = outs[0].shape[0], outs[0].shape[1]
    length = k_ref.shape[0]
    left = length - lax.broadcasted_iota(jnp.int32, (length, size), 0).astype(F32)
    for a, out_ref in enumerate(outs):
        first = lax.rem(place_ref[1] + a, len(outs)) * part
        for j in range(part):
            cols = pl.ds(pl.multiple_of((first + j) * size, size), size)
            tail = jnp.exp(-rate_ref[first + j] * left)
            high, low = halves(k_ref[:, cols].astype(F32) * tail)
            v = v_ref[:, cols]
            out_ref[j] = dot(high, v, TN) + dot(low, v, TN)


def local_kernel(rate_ref, q_ref, k_ref, v_ref, out_ref):
    heads = rate_ref.shape[0]
    length = k_ref.shape[0]
    size = k_ref.shape[1] // heads
    rows = lax.broadcasted_iota(jnp.int32, (length, length), 0)
    cols = lax.broadcasted_iota(jnp.int32, (length, length), 1)
    offset = (rows - cols).astype(F32)
    keep = offset >= 0
    offset = jnp.maximum(offset, 0.0)
    for h in range(heads):
        at = slice(h * size, (h + 1) * size)
        masked = jnp.where(keep, jnp.exp(-rate_ref[h] * offset), 0.0)
        weighted = (dot(q_ref[:, at], k_ref[:, at], NT) * masked).astype(BF16)
        out_ref[:, at] = dot(weighted, v_ref[:, at], NN)


def head_kernel(place_ref, rate_ref, q_ref, local_ref, *refs):
    states, out_ref = refs[:-1], refs[-1]
    part, size = states[0].shape[0], states[0].shape[1]
    length = q_ref.shape[0]
    pos = lax.broadcasted_iota(jnp.int32, (length, size), 0).astype(F32)
    for a, state_ref in enumerate(states):
        first = lax.rem(place_ref[1] + a, len(states)) * part
        for j in range(part):
            at = pl.ds(pl.multiple_of((first + j) * size, size), size)
            high, low = halves(state_ref[j])
            q = q_ref[:, at]
            carried = dot(q, high, NN) + dot(q, low, NN)
            carried = carried * jnp.exp(-rate_ref[first + j] * pos)
            attended = local_ref[:, at] + carried
            scale = lax.rsqrt(jnp.mean(attended * attended, axis=-1, keepdims=True) + 1e-05)
            out_ref[:, at] = (attended * scale).astype(BF16)


def xor_permute(x, step):
    n = lax.axis_size("ctx")
    return lax.ppermute(x, "ctx", [(d, d ^ step) for d in range(n)])


def after(x, *others):
    return lax.optimization_barrier((x,) + others)[0]


def within_group(x):
    n = lax.axis_size("ctx")
    low = n // GROUPS
    got = [x]
    for step in range(1, low):
        got.append(
            lax.ppermute(
                x, "ctx", [(d, d // low * low + (d % low - step) % low) for d in range(n)]
            )
        )
    return got


def in_order(pieces, first, axis):
    n, width = len(pieces), pieces[0].shape[axis]
    ring = jnp.concatenate(pieces + pieces[:-1], axis=axis)
    return lax.dynamic_slice_in_dim(ring, lax.rem(n - first, n) * width, n * width, axis)


def gather_doubling(x, axis, count, place):
    n = lax.axis_size(axis)
    step = 1
    while step < count:
        got = lax.ppermute(x, axis, [(d, d ^ step) for d in range(n)])
        upper = (place & step) != 0
        x = jnp.where(
            upper, jnp.concatenate([got, x], axis=1), jnp.concatenate([x, got], axis=1)
        )
        step *= 2
    return x


def line_sum(part, sent, place):
    n = lax.axis_size("exp")
    half = n // 2
    for hop in range(half - 1):
        got = lax.ppermute(sent, "exp", [(hop, hop + 1), (n - 1 - hop, n - 2 - hop)])
        part = part + got.astype(F32)
        sent = part.astype(BF16)
    other = lax.ppermute(sent, "exp", [(half - 1, half), (half, half - 1)])
    total = (part + other.astype(F32)).astype(BF16)
    for hop in range(half - 1):
        here, there = half - 1 - hop, half + hop
        got = lax.ppermute(total, "exp", [(here, here - 1), (there, there + 1)])
        total = jnp.where((place == here - 1) | (place == there + 1), got, total)
    return total


def project_kernel(low, place_ref, *refs):
    heads, (w_ref,), rests = refs[:low], refs[low : low + 1], refs[low + 1 : 2 * low + 1]
    sum_ref, sent_ref = refs[2 * low + 1 :]
    length, tokens = heads[0].shape[0], rests[0].shape[0]
    for a in range(low):
        first = lax.rem(place_ref[1] + a, low) * length
        at = pl.ds(pl.multiple_of(first, length), length)
        sum_ref[at, :] = dot(heads[a][...], w_ref[...], NN)
        own = pl.ds(pl.multiple_of(first + place_ref[2] * tokens, tokens), tokens)
        sum_ref[own, :] += rests[a][...].astype(F32)
        sent_ref[at, :] = sum_ref[at, :].astype(BF16)


def dispatch_kernel(count, *refs):
    mixed, gain_ref, picks_ref, out_ref = refs[:count], refs[count], refs[count + 1], refs[count + 2]
    cols = gain_ref.shape[1]
    value = mixed[-1][...].astype(F32)
    rows = (value * gain_ref[...]).astype(BF16)
    out_ref[:, :cols] = dot(picks_ref[...], rows, NN).astype(BF16)
    if count > 1:
        squares = jnp.sum(value * value, axis=1, keepdims=True)
        for ref in mixed[:-1]:
            value = ref[...].astype(F32)
            squares = squares + jnp.sum(value * value, axis=1, keepdims=True)
        lane = lax.broadcasted_iota(jnp.int32, (squares.shape[0], 128), 1)
        rest, extra = squares, jnp.zeros((squares.shape[0], 128), F32)
        for place in range(3):
            high = rest.astype(BF16).astype(F32)
            extra = jnp.where(lane == place, high, extra)
            rest = rest - high
        extra = dot(picks_ref[...], extra.astype(BF16), NN).astype(BF16)
        out_ref[:, out_ref.shape[1] - 128 :] = extra


def mixed_kernel(low, place_ref, *refs):
    out_ref = refs[-1]
    cols = refs[0].shape[1]
    tokens = out_ref.shape[0]
    length = refs[0].shape[0] // low
    for t in range(GROUPS):
        block = (place_ref[0] ^ t) * low
        own = pl.ds(pl.multiple_of(place_ref[1] * length + place_ref[2] * tokens, tokens), tokens)
        at = pl.multiple_of((block + place_ref[1]) * cols, cols)
        out_ref[:, pl.ds(at, cols)] = refs[t][own, :]
        for a in range(1, low):
            at = pl.multiple_of((block + lax.rem(place_ref[1] + a, low)) * cols, cols)
            got = refs[GROUPS + a - 1]
            out_ref[:, pl.ds(at, cols)] = got[:, t * cols : (t + 1) * cols]


def expert_kernel(count, mode, has_acc, model, place_ref, *refs):
    refs = list(refs)
    pieces, gates, ups = refs[:count], refs[count : 2 * count], refs[2 * count : 3 * count]
    refs = refs[3 * count :]
    gated, lifted = (refs.pop(0)[...], refs.pop(0)[...]) if has_acc else (0.0, 0.0)
    outs = refs[1:] if mode == "next" else refs
    squares = 0.0
    for piece, gate, up in zip(pieces, gates, ups):
        width = gate.shape[1]
        x = piece[:, :width]
        gated = gated + dot(gate[...], x, NT)
        lifted = lifted + dot(up[...], x, NT)
        if piece.shape[1] > width:
            extra = piece[:, width:]
            lane = lax.broadcasted_iota(jnp.int32, (8, extra.shape[1]), 1)
            squares = squares + dot((lax.rem(lane, 128) < 3).astype(BF16), extra, NT)[0:1, :]
    if mode is None:
        outs[0][...] = gated
        outs[1][...] = lifted
    else:
        scale = lax.rsqrt(squares / model + 1e-05)
        gated, lifted = gated * scale, lifted * scale
        outs[0][...] = (gated / (1.0 + jnp.exp(-gated)) * lifted).astype(BF16)


def expert_step(place, s, chunk_ids, pieces, gate, up, sums, hidden, final):
    hid, model = gate.shape
    low = len(pieces[0])
    slots = pieces[0][0].shape[0]
    width = model // GROUPS // low
    has_acc = sums is not None
    count = low * len(chunk_ids)

    def whole(x):
        return pl.BlockSpec(x.shape, lambda r, p: (0, 0))

    def weight(t, a):
        return pl.BlockSpec(
            (hid, width), lambda r, p: (0, (p[0] ^ (s ^ t)) * low + lax.rem(p[1] + a, low))
        )

    acc_spec = pl.BlockSpec((hid, slots), lambda r, p: (0, 0))
    operands = [x for per in pieces for x in per]
    specs = [whole(x) for x in operands]
    operands += [gate] * count + [up] * count
    specs += [weight(t, a) for t in chunk_ids for a in range(low)] * 2
    if has_acc:
        operands += list(sums)
        specs += [acc_spec] * 2
    aliases = {}
    if final:
        out_shape = jax.ShapeDtypeStruct((hid, slots * GROUPS), BF16)
        out_specs = pl.BlockSpec((hid, slots), lambda r, p: (0, p[0] ^ s))
        if hidden is not None:
            operands.append(hidden)
            specs.append(pl.BlockSpec(memory_space=pl.ANY))
            aliases = {len(operands): 0}
        mode = "first" if hidden is None else "next"
    else:
        out_shape = [jax.ShapeDtypeStruct((hid, slots), F32)] * 2
        out_specs = [acc_spec] * 2
        mode = None
    return call(
        functools.partial(expert_kernel, count, mode, has_acc, model),
        out_shape,
        4 * hid * slots * width * count,
        4 * hid * width * count + 8 * hid * slots * (1 + has_acc) + 2 * slots * width * count,
        hid * slots if final else 0,
        grid_spec=pltpu.PrefetchScalarGridSpec(
            num_scalar_prefetch=1, grid=(1,), in_specs=specs, out_specs=out_specs
        ),
        input_output_aliases=aliases,
    )(place, *operands)


def states_by_pairs(place, decay_rate, key_rows, value_rows, length, size):
    heads = decay_rate.shape[0]
    half = heads // 2
    mine, theirs = call(
        fresh_kernel,
        [jax.ShapeDtypeStruct((half, size, size), F32)] * 2,
        4 * heads * length * size * size,
        4 * length * heads * size + 4 * heads * size * size,
        heads * length * size,
        in_specs=[SM, SM, VM, VM],
        out_specs=[VM, VM],
    )(place, decay_rate, key_rows, value_rows)
    group, first = place[0], place[1] == 0
    rates = lax.dynamic_slice(decay_rate, (place[1] * half,), (half,))

    def fade(blocks):
        return jnp.exp(-rates * (length * blocks))[:, None, None]

    got = xor_permute(theirs, 1)
    early = jnp.where(first, mine, got)
    total = fade(1.0) * early + jnp.where(first, got, mine)
    state, marks = jnp.zeros_like(total), [got]
    step = 1
    while step < GROUPS:
        upper = (group & step) != 0
        coef = jnp.where(upper, fade(2.0 * (group & (step - 1)).astype(F32)), 0.0)
        if 2 * step < GROUPS:
            got = xor_permute(total, 2 * step)
            state = state + coef * got
            span = fade(2.0 * step)
            total = jnp.where(upper, span * got + total, span * total + got)
        else:
            got = lax.ppermute(total, "ctx", [(d, d + 2 * step) for d in range(2 * step)])
            state = state + coef * got
        marks.append(got)
        step *= 2
    late = fade(1.0) * state + early
    return [
        jnp.where(first, state, late),
        xor_permute(jnp.where(first, late, state), 1),
    ], marks


def states_by_steps(place, ctx, decay_rate, key_rows, value_rows, length, size):
    n_ctx, heads = lax.axis_size("ctx"), decay_rate.shape[0]
    (total,) = call(
        fresh_kernel,
        [jax.ShapeDtypeStruct((heads, size, size), F32)],
        4 * heads * length * size * size,
        4 * length * heads * size + 4 * heads * size * size,
        heads * length * size,
        in_specs=[SM, SM, VM, VM],
        out_specs=[VM],
    )(place, decay_rate, key_rows, value_rows)

    def fade(blocks):
        return jnp.exp(-decay_rate * (length * blocks))[:, None, None]

    state, step, got = jnp.zeros_like(total), 1, total
    while step < n_ctx:
        upper = (ctx & step) != 0
        got = xor_permute(total, step)
        state = state + jnp.where(upper, fade((ctx & (step - 1)).astype(F32)), 0.0) * got
        span = fade(float(step))
        total = jnp.where(upper, span * got + total, span * total + got)
        step *= 2
    return [state], [got] * 3


def per_device(
    queries,
    key_rows,
    value_rows,
    decay_rate,
    out_weight,
    residual,
    moe_gain,
    expert_ids,
    gate_weight,
    up_weight,
):
    n_ctx, n_exp = lax.axis_size("ctx"), lax.axis_size("exp")
    low = n_ctx // GROUPS
    ctx, exp = lax.axis_index("ctx"), lax.axis_index("exp")
    group, member = ctx // low, lax.rem(ctx, low)
    place = jnp.stack([group, member, exp]).astype(jnp.int32)
    length, here = queries.shape
    heads = decay_rate.shape[0]
    size = here // heads
    model = residual.shape[1]
    cols = model // n_ctx
    tokens = length // n_exp
    capacity = max(2, 3 * tokens // n_exp)
    aligned = cols % 128 == 0

    local = call(
        local_kernel,
        jax.ShapeDtypeStruct((length, here), F32),
        4 * heads * length * length * size,
        10 * length * here,
        heads * length * length,
        in_specs=[SM, VM, VM, VM],
        out_specs=VM,
    )(decay_rate, queries, key_rows, value_rows)
    if low == 2 and heads % 2 == 0:
        states, marks = states_by_pairs(place, decay_rate, key_rows, value_rows, length, size)
    else:
        states, marks = states_by_steps(
            place, ctx, decay_rate, key_rows, value_rows, length, size
        )

    rest_rows = within_group(after(residual, marks[0]))
    ids = gather_doubling(after(expert_ids.T, marks[0]), "exp", n_exp, exp)
    ids = gather_doubling(ids, "ctx", low, member)
    cut = out_weight.shape[0] // 2
    w_one = xor_permute(after(out_weight, marks[1]), low)
    w_two = xor_permute(after(out_weight, marks[2]), 2 * low)
    w_top = xor_permute(w_one[:cut], 2 * low)
    w_bottom = xor_permute(w_two[cut:], low)
    columns = [out_weight, w_one, w_two, jnp.concatenate([w_top, w_bottom], axis=0)]

    named = (ids[0] == exp) | (ids[1] == exp)
    every = low * length
    token = jnp.arange(every, dtype=jnp.int32)
    earlier = (token[:, None] < token[None, :]) & (
        token[:, None] // tokens == token[None, :] // tokens
    )
    rank = jnp.sum((earlier & named[:, None]).astype(jnp.int32), axis=0)
    row = jnp.where(named & (rank < capacity), token // tokens * capacity + rank, -1)
    slots = low * n_exp * capacity
    picks = (jnp.arange(slots, dtype=jnp.int32)[:, None] == row[None, :]).astype(BF16)

    head_out = call(
        head_kernel,
        jax.ShapeDtypeStruct((length, here), BF16),
        4 * heads * length * size * size,
        8 * length * here + 4 * heads * size * size,
        heads * length * size,
        in_specs=[SM, SM, VM, VM] + [VM] * len(states),
        out_specs=VM,
    )(place, decay_rate, queries, local, *states)
    group_heads = within_group(head_out)

    gains, rests = [], []
    for t in range(GROUPS):
        start = (((group ^ t) * low + member) * cols).astype(jnp.int32)
        gains.append(lax.dynamic_slice(moe_gain, (start,), (cols,))[None])
        rests.append(
            [lax.dynamic_slice(r, (jnp.int32(0), start), (tokens, cols)) for r in rest_rows]
        )

    mixed, received = [], []
    for t in range(GROUPS):
        part, sent = call(
            functools.partial(project_kernel, low),
            [jax.ShapeDtypeStruct((every, cols), F32), jax.ShapeDtypeStruct((every, cols), BF16)],
            2 * every * here * cols,
            2 * every * here + 2 * here * cols + 6 * every * cols,
            in_specs=[SM] + [VM] * (2 * low + 1),
            out_specs=[VM, VM],
        )(place, *group_heads, columns[t], *rests[t])
        mixed.append(line_sum(part, sent, exp))
        last = t == GROUPS - 1
        wide = (cols + 127) // 128 * 128 + 128 if last else cols
        x = call(
            functools.partial(dispatch_kernel, GROUPS if last else 1),
            jax.ShapeDtypeStruct((slots, wide), BF16),
            2 * slots * every * wide,
            2 * every * (slots + cols) + 2 * slots * wide,
            in_specs=[VM] * ((GROUPS if last else 1) + 2),
            out_specs=VM,
        )(*(mixed if last else mixed[-1:]), gains[t], picks)
        one, two = xor_permute(x, low), xor_permute(x, 2 * low)
        three = xor_permute(one, 2 * low) if t % 2 == 0 else xor_permute(two, low)
        got = [within_group(y) for y in (x, one, two, three)]
        if not aligned:
            joined = []
            for per in got:
                whole = in_order([y[:, :cols] for y in per], member, 1)
                if last:
                    whole = jnp.concatenate([whole] + [y[:, wide - 128 :] for y in per], axis=1)
                joined.append([whole])
            got = joined
        received.append(got)

    own = exp * tokens
    gotten = []
    for a in range(1, low):
        first = lax.rem(member + a, low) * length + own
        rows = [lax.dynamic_slice_in_dim(m, first, tokens, 0) for m in mixed]
        gotten.append(
            lax.ppermute(
                jnp.concatenate(rows, axis=1),
                "ctx",
                [(d, d // low * low + (d % low + a) % low) for d in range(n_ctx)],
            )
        )
    gotten = gotten[::-1]
    if aligned:
        mixed_out = call(
            functools.partial(mixed_kernel, low),
            jax.ShapeDtypeStruct((tokens, model), BF16),
            0,
            6 * tokens * model,
            in_specs=[SM] + [VM] * (GROUPS + low - 1),
            out_specs=VM,
        )(place, *mixed, *gotten)
    else:
        rows = [lax.dynamic_slice_in_dim(m, member * length + own, tokens, 0) for m in mixed]
        parts = [jnp.concatenate(rows, axis=1)] + gotten
        mixed_out = jnp.zeros((tokens, model), BF16)
        for a, part in enumerate(parts):
            for t in range(GROUPS):
                start = ((group ^ t) * low + lax.rem(member + a, low)) * cols
                mixed_out = lax.dynamic_update_slice_in_dim(
                    mixed_out, part[:, t * cols : (t + 1) * cols], start, 1
                )

    gate, up = gate_weight[0], up_weight[0]
    sums = [None] * GROUPS
    for chunk_ids in ([0, 1], [2]):
        for s in range(GROUPS):
            sums[s] = expert_step(
                place, s, chunk_ids, [received[t][s] for t in chunk_ids], gate, up, sums[s], None, False
            )
    hidden = None
    for s in range(GROUPS):
        last = GROUPS - 1
        hidden = expert_step(
            place, s, [last], [received[last][s]], gate, up, sums[s], hidden, True
        )
    return (mixed_out, hidden[None])


def solution(mesh):
    in_specs = (
        P("ctx", "exp"),
        P("ctx", "exp"),
        P("ctx", "exp"),
        P("exp"),
        P("exp", "ctx"),
        P(("ctx", "exp"), None),
        P(),
        P(("ctx", "exp"), None),
        P("exp", "ctx", None),
        P("exp", "ctx", None),
    )
    out_specs = (P(("ctx", "exp"), None), P("exp", "ctx", None))
    return jax.shard_map(
        per_device, mesh=mesh, in_specs=in_specs, out_specs=out_specs, check_vma=False
    )
```

```python
import functools

import jax
import jax.numpy as jnp
from jax import lax
from jax.experimental import pallas as pl
from jax.experimental.pallas import tpu as pltpu
from jax.sharding import PartitionSpec as P

GROUPS = 4
BF16 = jnp.bfloat16
F32 = jnp.float32
NT = (((1,), (1,)), ((), ()))
TN = (((0,), (0,)), ((), ()))
NN = (((1,), (0,)), ((), ()))


def dot(a, b, dims):
    return lax.dot_general(a, b, dims, preferred_element_type=F32)


def halves(x):
    high = x.astype(BF16)
    return high, (x - high.astype(F32)).astype(BF16)


def call(kernel, out_shape, operands, flops, exps=0, deps=(), specs=None, limit=12, **kwargs):
    count, extra = len(operands), len(deps)

    def body(*refs):
        kernel(*refs[:count], *refs[count + extra :])

    shapes = out_shape if isinstance(out_shape, (list, tuple)) else [out_shape]
    nbytes = sum(x.size * x.dtype.itemsize for x in list(operands) + list(shapes))
    kwargs.setdefault("out_specs", jax.tree.map(lambda _: VM, out_shape))
    return pl.pallas_call(
        body,
        out_shape=out_shape,
        in_specs=list(specs or [VM] * count) + [ANY] * extra,
        compiler_params=pltpu.CompilerParams(vmem_limit_bytes=limit * 1024 * 1024),
        cost_estimate=pl.CostEstimate(
            flops=int(flops), bytes_accessed=int(nbytes), transcendentals=int(exps)
        ),
        **kwargs,
    )(*operands, *deps)


VM = pl.BlockSpec(memory_space=pltpu.VMEM)
SM = pl.BlockSpec(memory_space=pltpu.SMEM)
ANY = pl.BlockSpec(memory_space=pl.ANY)


def fresh_kernel(place_ref, rate_ref, k_ref, v_ref, *outs):
    part, size = outs[0].shape[0], outs[0].shape[1]
    length = k_ref.shape[0]
    left = length - lax.broadcasted_iota(jnp.int32, (length, size), 0).astype(F32)
    for a, out_ref in enumerate(outs):
        first = lax.rem(place_ref[1] + a, len(outs)) * part
        for j in range(part):
            cols = pl.ds(pl.multiple_of((first + j) * size, size), size)
            tail = jnp.exp(-rate_ref[first + j] * left)
            high, low = halves(k_ref[:, cols].astype(F32) * tail)
            v = v_ref[:, cols]
            out_ref[j] = dot(high, v, TN) + dot(low, v, TN)


def local_kernel(rate_ref, q_ref, k_ref, v_ref, out_ref):
    heads = rate_ref.shape[0]
    length = k_ref.shape[0]
    size = k_ref.shape[1] // heads
    rows = lax.broadcasted_iota(jnp.int32, (length, length), 0)
    cols = lax.broadcasted_iota(jnp.int32, (length, length), 1)
    offset = (rows - cols).astype(F32)
    keep = offset >= 0
    offset = jnp.maximum(offset, 0.0)
    for h in range(heads):
        at = slice(h * size, (h + 1) * size)
        masked = jnp.where(keep, jnp.exp(-rate_ref[h] * offset), 0.0)
        weighted = (dot(q_ref[:, at], k_ref[:, at], NT) * masked).astype(BF16)
        out_ref[:, at] = dot(weighted, v_ref[:, at], NN)


def fade(rate_ref, head, positions):
    return jnp.exp(-(rate_ref[head] * positions) + jnp.zeros((1, 128), F32))


def pair_kernel(length, place_ref, rate_ref, mine_ref, got_ref, early_ref, total_ref):
    part = mine_ref.shape[0]
    first = place_ref[1] == 0
    for j in range(part):
        mine, got = mine_ref[j], got_ref[j]
        early = jnp.where(first, mine, got)
        early_ref[j] = early
        late = jnp.where(first, got, mine)
        total_ref[j] = fade(rate_ref, place_ref[1] * part + j, float(length)) * early + late


def scan_kernel(length, step, place_ref, rate_ref, *refs):
    old_ref = refs[0] if step > 1 else None
    total_ref, got_ref, state_ref, out_ref = refs[-4:]
    part = total_ref.shape[0]
    upper = (place_ref[0] & step) != 0
    behind = (place_ref[0] & (step - 1)).astype(F32) * (2.0 * length)
    for j in range(part):
        head = place_ref[1] * part + j
        got, total = got_ref[j], total_ref[j]
        state = jnp.where(upper, fade(rate_ref, head, behind) * got, 0.0)
        state_ref[j] = state if old_ref is None else old_ref[j] + state
        span = fade(rate_ref, head, 2.0 * length * step)
        out_ref[j] = jnp.where(upper, span * got + total, span * total + got)


def final_scan_kernel(length, step, place_ref, rate_ref, old_ref, got_ref, early_ref, keep_ref, give_ref):
    part = old_ref.shape[0]
    first = place_ref[1] == 0
    upper = (place_ref[0] & step) != 0
    behind = (place_ref[0] & (step - 1)).astype(F32) * (2.0 * length)
    for j in range(part):
        head = place_ref[1] * part + j
        state = old_ref[j] + jnp.where(upper, fade(rate_ref, head, behind) * got_ref[j], 0.0)
        late = fade(rate_ref, head, float(length)) * state + early_ref[j]
        keep_ref[j] = jnp.where(first, state, late)
        give_ref[j] = jnp.where(first, late, state)


def head_kernel(place_ref, rate_ref, q_ref, local_ref, *refs):
    states, out_ref = refs[:-1], refs[-1]
    part, size = states[0].shape[0], states[0].shape[1]
    length = q_ref.shape[0]
    pos = lax.broadcasted_iota(jnp.int32, (length, size), 0).astype(F32)
    for a, state_ref in enumerate(states):
        first = lax.rem(place_ref[1] + a, len(states)) * part
        for j in range(part):
            at = pl.ds(pl.multiple_of((first + j) * size, size), size)
            high, low = halves(state_ref[j])
            q = q_ref[:, at]
            carried = dot(q, high, NN) + dot(q, low, NN)
            carried = carried * jnp.exp(-rate_ref[first + j] * pos)
            attended = local_ref[:, at] + carried
            scale = lax.rsqrt(jnp.mean(attended * attended, axis=-1, keepdims=True) + 1e-05)
            out_ref[:, at] = (attended * scale).astype(BF16)


def xor_permute(x, step):
    n = lax.axis_size("ctx")
    return lax.ppermute(x, "ctx", [(d, d ^ step) for d in range(n)])


def within_group(x):
    n = lax.axis_size("ctx")
    low = n // GROUPS
    got = [x]
    for step in range(1, low):
        got.append(
            lax.ppermute(
                x, "ctx", [(d, d // low * low + (d % low - step) % low) for d in range(n)]
            )
        )
    return got


def in_order(pieces, first, axis):
    n, width = len(pieces), pieces[0].shape[axis]
    ring = jnp.concatenate(pieces + pieces[:-1], axis=axis)
    return lax.dynamic_slice_in_dim(ring, lax.rem(n - first, n) * width, n * width, axis)


def gather_doubling(x, axis, count, place):
    n = lax.axis_size(axis)
    step = 1
    while step < count:
        got = lax.ppermute(x, axis, [(d, d ^ step) for d in range(n)])
        upper = (place & step) != 0
        x = jnp.where(
            upper, jnp.concatenate([got, x], axis=1), jnp.concatenate([x, got], axis=1)
        )
        step *= 2
    return x


def project_kernel(low, halves_of_w, place_ref, *refs):
    heads, rests = refs[:low], refs[low + halves_of_w : 2 * low + halves_of_w]
    weights = refs[low : low + halves_of_w]
    sum_ref, sent_ref = refs[2 * low + halves_of_w :]
    length, tokens = heads[0].shape[0], rests[0].shape[0]
    for a in range(low):
        first = lax.rem(place_ref[1] + a, low) * length
        at = pl.ds(pl.multiple_of(first, length), length)
        total, start = 0.0, 0
        for w_ref in weights:
            depth = w_ref.shape[0]
            total = total + dot(heads[a][:, start : start + depth], w_ref[...], NN)
            start += depth
        sum_ref[at, :] = total
        own = pl.ds(pl.multiple_of(first + place_ref[2] * tokens, tokens), tokens)
        sum_ref[own, :] += rests[a][...].astype(F32)
        sent_ref[at, :] = sum_ref[at, :].astype(BF16)


def add_kernel(part_ref, got_ref, *outs):
    total = part_ref[...] + got_ref[...].astype(F32)
    for out_ref in outs:
        out_ref[...] = total.astype(out_ref.dtype)


def dispatch_kernel(count, others, edges, place_ref, got_ref, *refs):
    mixed, (gain_ref, picks_ref, out_ref, mixed_ref), gives = (
        refs[:count],
        refs[count : count + 4],
        refs[count + 4 :],
    )
    cols = gain_ref.shape[1]
    if edges is None:
        mixed_ref[...] = mixed[-1][...]
    else:
        outer = (place_ref[2] == edges[0]) | (place_ref[2] == edges[1])
        mixed_ref[...] = jnp.where(outer, got_ref[...], mixed[-1][...])
    value = mixed_ref[...].astype(F32)
    rows = (value * gain_ref[...]).astype(BF16)
    out_ref[:, :cols] = dot(picks_ref[...], rows, NN).astype(BF16)
    if count == 1:
        return
    mixed = list(mixed[:-1]) + [mixed_ref]
    squares = jnp.sum(value * value, axis=1, keepdims=True)
    for ref in mixed[:-1]:
        value = ref[...].astype(F32)
        squares = squares + jnp.sum(value * value, axis=1, keepdims=True)
    lane = lax.broadcasted_iota(jnp.int32, (squares.shape[0], 128), 1)
    rest, extra = squares, jnp.zeros((squares.shape[0], 128), F32)
    for place in range(3):
        high = rest.astype(BF16).astype(F32)
        extra = jnp.where(lane == place, high, extra)
        rest = rest - high
    extra = dot(picks_ref[...], extra.astype(BF16), NN).astype(BF16)
    out_ref[:, out_ref.shape[1] - 128 :] = extra
    for a, give_ref in enumerate(gives, 1):
        tokens = give_ref.shape[0]
        first = lax.rem(place_ref[1] + a, others + 1) * (mixed_ref.shape[0] // (others + 1))
        rows = pl.ds(pl.multiple_of(first + place_ref[2] * tokens, tokens), tokens)
        for t, ref in enumerate(mixed):
            give_ref[:, t * cols : (t + 1) * cols] = ref[rows, :]


def mixed_kernel(low, place_ref, *refs):
    out_ref = refs[-1]
    cols = refs[0].shape[1]
    tokens = out_ref.shape[0]
    length = refs[0].shape[0] // low
    for t in range(GROUPS):
        block = (place_ref[0] ^ t) * low
        own = pl.ds(pl.multiple_of(place_ref[1] * length + place_ref[2] * tokens, tokens), tokens)
        at = pl.multiple_of((block + place_ref[1]) * cols, cols)
        out_ref[:, pl.ds(at, cols)] = refs[t][own, :]
        for a in range(1, low):
            at = pl.multiple_of((block + lax.rem(place_ref[1] + a, low)) * cols, cols)
            got = refs[GROUPS + a - 1]
            out_ref[:, pl.ds(at, cols)] = got[:, t * cols : (t + 1) * cols]


def expert_kernel(t, spans, count, mode, model, place_ref, gate_ref, up_ref, *refs):
    refs = list(refs)
    pieces = [[refs.pop(0) for _ in range(count)] for _ in spans]
    sums = [[refs.pop(0), refs.pop(0)] for _ in spans] if t > 0 else None
    if mode == "next":
        refs.pop(0)
    outs, scratch = (refs[0], refs[1:]) if mode else (refs[: 2 * len(spans)], refs[2 * len(spans) :])
    width = scratch[0].shape[2]
    part = width // count
    copies = []
    for n, s in enumerate(spans):
        extras, held = [], scratch[0].at[n]
        for a, piece in enumerate(pieces[n]):
            member = lax.rem(place_ref[1] + a, count) if count > 1 else 0
            at = pl.multiple_of(member * part, part) if count > 1 else 0
            held[:, pl.ds(at, part)] = piece[:, :part]
            if mode:
                extras.append(piece[:, part:])
        x = held[...]
        cols = pl.ds(pl.multiple_of((place_ref[0] ^ (s ^ t)) * width, width), width)
        gated = dot(gate_ref[:, cols], x, NT)
        lifted = dot(up_ref[:, cols], x, NT)
        if sums is not None:
            gated = gated + sums[n][0][...]
            lifted = lifted + sums[n][1][...]
        if mode is None:
            outs[2 * n][...] = gated
            outs[2 * n + 1][...] = lifted
            continue
        squares = 0.0
        for extra in extras:
            lane = lax.broadcasted_iota(jnp.int32, (8, extra.shape[1]), 1)
            squares = squares + dot((lax.rem(lane, 128) < 3).astype(BF16), extra, NT)[0:1, :]
        scale = lax.rsqrt(squares / model + 1e-05)
        gated, lifted = gated * scale, lifted * scale
        ready, sems = scratch[1], scratch[2]
        ready[n] = (gated / (1.0 + jnp.exp(-gated)) * lifted).astype(BF16)
        slots = ready.shape[2]
        at = pl.ds(pl.multiple_of((place_ref[0] ^ s) * slots, slots), slots)
        copies.append(pltpu.make_async_copy(ready.at[n], outs.at[:, at], sems.at[n]))
        copies[-1].start()
    for copy in copies:
        copy.wait()


def expert_step(place, t, spans, pieces, gate, up, sums, hidden, final, deps):
    hid, model = gate.shape
    count, slots = len(pieces[0]), pieces[0][0].shape[0]
    width = model // GROUPS
    operands = [place, gate, up] + [x for per in pieces for x in per]
    if t > 0:
        operands += [x for s in spans for x in sums[s]]
    specs = [SM] + [VM] * (len(operands) - 1)
    scratch = [pltpu.VMEM((len(spans), slots, width), BF16)]
    kwargs, mode = {}, None
    if final:
        mode = "first" if hidden is None else "next"
        if hidden is not None:
            kwargs["input_output_aliases"] = {len(operands): 0}
            operands.append(hidden)
            specs.append(ANY)
        out_shape = jax.ShapeDtypeStruct((hid, slots * GROUPS), BF16)
        kwargs["out_specs"] = ANY
        scratch += [
            pltpu.VMEM((len(spans), hid, slots), BF16),
            pltpu.SemaphoreType.DMA((len(spans),)),
        ]
    else:
        out_shape = [jax.ShapeDtypeStruct((hid, slots), F32)] * (2 * len(spans))
    return call(
        functools.partial(expert_kernel, t, spans, count, mode, model),
        out_shape,
        operands,
        4 * hid * slots * width * len(spans),
        hid * slots * len(spans) if final else 0,
        deps,
        specs,
        20,
        scratch_shapes=scratch,
        **kwargs,
    )


def exchange_states(place, rate, mine, theirs, length, deps_one, deps_two):
    like = jax.ShapeDtypeStruct(mine.shape, F32)
    got = xor_permute(theirs, 1)
    early, total = call(
        functools.partial(pair_kernel, length), [like] * 2, [place, rate, mine, got], 0,
        specs=[SM, SM, VM, VM],
    )
    marks = [total]
    state, step = [], 1
    while 2 * step < GROUPS:
        got = xor_permute(total, 2 * step)
        state, total = call(
            functools.partial(scan_kernel, length, step),
            [like] * 2,
            [place, rate] + ([state] if step > 1 else []) + [total, got],
            0,
            deps=deps_one(marks[-1]),
            specs=[SM, SM] + [VM] * (3 if step > 1 else 2),
        )
        marks.append(total)
        step *= 2
    got = lax.ppermute(total, "ctx", [(d, d + 2 * step) for d in range(2 * step)])
    keep, give = call(
        functools.partial(final_scan_kernel, length, step),
        [like] * 2,
        [place, rate, state, got, early],
        0,
        deps=deps_two(marks[-1]),
        specs=[SM, SM, VM, VM, VM],
    )
    return [keep, xor_permute(give, 1)], keep


def states_by_steps(ctx, decay_rate, total, length):
    n_ctx = lax.axis_size("ctx")

    def faded(blocks):
        return jnp.exp(-decay_rate * (length * blocks))[:, None, None]

    state, step = jnp.zeros_like(total), 1
    while step < n_ctx:
        upper = (ctx & step) != 0
        got = xor_permute(total, step)
        state = state + jnp.where(upper, faded((ctx & (step - 1)).astype(F32)), 0.0) * got
        span = faded(float(step))
        total = jnp.where(upper, span * got + total, span * total + got)
        step *= 2
    return [state]


def tie(x, *deps):
    return call(
        lambda i, o: None, jax.ShapeDtypeStruct(x.shape, x.dtype), [x], 0,
        deps=deps, specs=[ANY], out_specs=ANY, input_output_aliases={0: 0},
    )


def per_device(
    queries,
    key_rows,
    value_rows,
    decay_rate,
    out_weight,
    residual,
    moe_gain,
    expert_ids,
    gate_weight,
    up_weight,
):
    n_ctx, n_exp = lax.axis_size("ctx"), lax.axis_size("exp")
    low = n_ctx // GROUPS
    ctx, exp = lax.axis_index("ctx"), lax.axis_index("exp")
    group, member = ctx // low, lax.rem(ctx, low)
    place = jnp.stack([group, member, exp]).astype(jnp.int32)
    length, here = queries.shape
    heads = decay_rate.shape[0]
    size = here // heads
    model = residual.shape[1]
    cols = model // n_ctx
    tokens = length // n_exp
    capacity = max(2, 3 * tokens // n_exp)
    aligned = cols % 128 == 0
    pairs = low == 2 and heads % 2 == 0
    every = low * length
    slots = low * n_exp * capacity

    cut = out_weight.shape[0] // 2
    w_top, w_bottom = out_weight[:cut], out_weight[cut:]
    two_top, two_bottom = xor_permute(w_top, 2 * low), xor_permute(w_bottom, 2 * low)
    one_top = xor_permute(w_top, low)
    ids = expert_ids.T

    fresh = call(
        fresh_kernel,
        [jax.ShapeDtypeStruct((heads // 2, size, size), F32)] * 2
        if pairs
        else [jax.ShapeDtypeStruct((heads, size, size), F32)],
        [place, decay_rate, key_rows, value_rows],
        4 * heads * length * size * size,
        heads * length * size,
        specs=[SM, SM, VM, VM],
    )

    def run_local(*deps):
        return call(
            local_kernel,
            jax.ShapeDtypeStruct((length, here), F32),
            [decay_rate, queries, key_rows, value_rows],
            4 * heads * length * length * size,
            heads * length * length,
            deps,
            [SM, VM, VM, VM],
        )

    if pairs:
        side = {}

        def deps_one(total):
            side["ids"] = gather_doubling(ids, "exp", n_exp, exp)
            side["local"] = run_local(total)
            side["rest"] = within_group(residual)
            return [side["local"], one_top, side["rest"][1]]

        def deps_two(total):
            side["one_bottom"] = xor_permute(tie(w_bottom, total), low)
            return [side["ids"], two_top, two_bottom]

        states, kept = exchange_states(
            place, decay_rate, fresh[0], fresh[1], length, deps_one, deps_two
        )
        ids, local, rest_rows, one_bottom = (
            side["ids"], side["local"], side["rest"], side["one_bottom"]
        )
        ids = gather_doubling(tie(ids, kept), "ctx", low, member)
        three_top = xor_permute(tie(one_top, kept), 2 * low)
        deps = [ids, one_bottom]
    else:
        states = states_by_steps(ctx, decay_rate, fresh[0], length)
        local, rest_rows = run_local(), within_group(residual)
        ids = gather_doubling(gather_doubling(ids, "exp", n_exp, exp), "ctx", low, member)
        one_bottom = xor_permute(w_bottom, low)
        three_top = xor_permute(one_top, 2 * low)
        deps = []

    head_out = call(
        head_kernel,
        jax.ShapeDtypeStruct((length, here), BF16),
        [place, decay_rate, queries, local] + states,
        4 * heads * length * size * size,
        heads * length * size,
        deps,
        [SM, SM] + [VM] * (2 + len(states)),
    )
    group_heads = within_group(head_out)
    three_bottom = xor_permute(tie(two_bottom, head_out), low)
    columns = [
        [out_weight], [one_top, one_bottom], [two_top, two_bottom], [three_top, three_bottom]
    ]

    named = (ids[0] == exp) | (ids[1] == exp)
    token = jnp.arange(every, dtype=jnp.int32)
    earlier = (token[:, None] < token[None, :]) & (
        token[:, None] // tokens == token[None, :] // tokens
    )
    rank = jnp.sum((earlier & named[:, None]).astype(jnp.int32), axis=0)
    row = jnp.where(named & (rank < capacity), token // tokens * capacity + rank, -1)
    picks = (jnp.arange(slots, dtype=jnp.int32)[:, None] == row[None, :]).astype(BF16)

    gains, rests = [], []
    for t in range(GROUPS):
        start = (((group ^ t) * low + member) * cols).astype(jnp.int32)
        gains.append(lax.dynamic_slice(moe_gain, (start,), (cols,))[None])
        rests.append(
            [lax.dynamic_slice(r, (jnp.int32(0), start), (tokens, cols)) for r in rest_rows]
        )
    gate, up = gate_weight[0], up_weight[0]

    chunk_f32 = jax.ShapeDtypeStruct((every, cols), F32)
    chunk_b16 = jax.ShapeDtypeStruct((every, cols), BF16)
    half = n_exp // 2
    mixed, received = [None] * GROUPS, [None] * GROUPS
    sums, gives, hidden = [None] * GROUPS, [], None
    links, last = [None] * GROUPS, [head_out]

    def chunk(t):
        final = t == GROUPS - 1
        part, sent = call(
            functools.partial(project_kernel, low, len(columns[t])),
            [chunk_f32, chunk_b16],
            [place] + group_heads + columns[t] + rests[t],
            2 * every * here * cols,
            deps=last[:],
            specs=[SM] + [VM] * (2 * low + len(columns[t])),
        )
        last[:] = [sent]
        for hop in range(half - 1):
            got = lax.ppermute(sent, "exp", [(hop, hop + 1), (n_exp - 1 - hop, n_exp - 2 - hop)])
            yield
            part, sent = call(
                add_kernel, [chunk_f32, chunk_b16], [part, got], every * cols, deps=last[:]
            )
            last[:] = [sent]
        got = lax.ppermute(sent, "exp", [(half - 1, half), (half, half - 1)])
        yield
        total = call(add_kernel, chunk_b16, [part, got], every * cols, deps=last[:])
        last[:] = [total]
        edges = None
        for hop in range(half - 1):
            if edges is not None:
                total = jnp.where((exp == edges[0]) | (exp == edges[1]), got, total)
            here_, there = half - 1 - hop, half + hop
            got = lax.ppermute(total, "exp", [(here_, here_ - 1), (there, there + 1)])
            edges = (here_ - 1, there + 1)
            yield
        wide = (cols + 127) // 128 * 128 + 128 if final else cols
        known = mixed[:t] if final else []
        outs = [jax.ShapeDtypeStruct((slots, wide), BF16), chunk_b16]
        if final and aligned:
            outs += [jax.ShapeDtypeStruct((tokens, GROUPS * cols), BF16)] * (low - 1)
        x, mixed[t], *gives[:] = call(
            functools.partial(dispatch_kernel, len(known) + 1, low - 1, edges),
            outs,
            [place, got] + known + [total, gains[t], picks],
            2 * slots * every * wide,
            deps=last[:] + (links[t - 1] or [] if t > 0 else []),
            specs=[SM] + [VM] * (len(known) + 4),
        )
        last[:] = [x]
        one, two = xor_permute(x, low), xor_permute(x, 2 * low)
        got = [within_group(x)]
        links[t] = [one, two]
        yield
        three = xor_permute(one, 2 * low) if t % 2 == 0 else xor_permute(two, low)
        got += [within_group(one), within_group(two)]
        if final:
            last[:] = last[:] + [one, two]
        yield
        got += [within_group(three)]
        if final:
            last[:] = last[:] + [three]
        if not aligned:
            joined = []
            for per in got:
                whole = in_order([y[:, :cols] for y in per], member, 1)
                if final:
                    whole = jnp.concatenate([whole] + [y[:, wide - 128 :] for y in per], axis=1)
                joined.append([whole])
            got = joined
        received[t] = got
        yield

    def experts(t, spans):
        nonlocal hidden
        final = t == GROUPS - 1
        pieces = [received[t][s] for s in spans]
        out = expert_step(
            place, t, spans, pieces, gate, up, sums, hidden, final, last[:]
        )
        if final:
            hidden = out
            last[:] = []
        else:
            for n, s in enumerate(spans):
                sums[s] = out[2 * n : 2 * n + 2]
            last[:] = [out[0]]

    running, waiting = [], list(range(GROUPS))
    everyone = list(range(GROUPS))
    done = []
    while running or waiting:
        if waiting:
            running.insert(0, (waiting[0], chunk(waiting.pop(0))))
        for t, work in list(running):
            if next(work, "end") == "end":
                running.remove((t, work))
                if t < GROUPS - 1:
                    experts(t, everyone)

    own = exp * tokens
    gotten = []
    for a in range(1, low):
        if aligned:
            give = gives[a - 1]
        else:
            first = lax.rem(member + a, low) * length + own
            rows = [lax.dynamic_slice_in_dim(m, first, tokens, 0) for m in mixed]
            give = jnp.concatenate(rows, axis=1)
        gotten.append(
            lax.ppermute(
                give, "ctx", [(d, d // low * low + (d % low + a) % low) for d in range(n_ctx)]
            )
        )
    gotten = gotten[::-1]
    if aligned:
        mixed_out = call(
            functools.partial(mixed_kernel, low),
            jax.ShapeDtypeStruct((tokens, model), BF16),
            [place] + mixed + gotten,
            0,
            deps=last[:],
            specs=[SM] + [VM] * (GROUPS + low - 1),
        )
        last[:] = [mixed_out]
    else:
        rows = [lax.dynamic_slice_in_dim(m, member * length + own, tokens, 0) for m in mixed]
        parts = [jnp.concatenate(rows, axis=1)] + gotten
        mixed_out = jnp.zeros((tokens, model), BF16)
        for a, part in enumerate(parts):
            for t in range(GROUPS):
                start = ((group ^ t) * low + lax.rem(member + a, low)) * cols
                mixed_out = lax.dynamic_update_slice_in_dim(
                    mixed_out, part[:, t * cols : (t + 1) * cols], start, 1
                )
    experts(GROUPS - 1, everyone[:-1])
    experts(GROUPS - 1, everyone[-1:])
    return (mixed_out, hidden[None])


def solution(mesh):
    in_specs = (
        P("ctx", "exp"),
        P("ctx", "exp"),
        P("ctx", "exp"),
        P("exp"),
        P("exp", "ctx"),
        P(("ctx", "exp"), None),
        P(),
        P(("ctx", "exp"), None),
        P("exp", "ctx", None),
        P("exp", "ctx", None),
    )
    out_specs = (P(("ctx", "exp"), None), P("exp", "ctx", None))
    return jax.shard_map(
        per_device, mesh=mesh, in_specs=in_specs, out_specs=out_specs, check_vma=False
    )
```

```python
import functools

import jax
import jax.numpy as jnp
from jax import lax
from jax.experimental import pallas as pl
from jax.experimental.pallas import tpu as pltpu
from jax.sharding import PartitionSpec as P

GROUPS = 4
BF16 = jnp.bfloat16
F32 = jnp.float32
NT = (((1,), (1,)), ((), ()))
TN = (((0,), (0,)), ((), ()))
NN = (((1,), (0,)), ((), ()))


def dot(a, b, dims):
    return lax.dot_general(a, b, dims, preferred_element_type=F32)


def halves(x):
    high = x.astype(BF16)
    return high, (x - high.astype(F32)).astype(BF16)


def call(kernel, out_shape, operands, flops, exps=0, deps=(), specs=None, limit=12, **kwargs):
    count, extra = len(operands), len(deps)

    def body(*refs):
        kernel(*refs[:count], *refs[count + extra :])

    shapes = out_shape if isinstance(out_shape, (list, tuple)) else [out_shape]
    nbytes = sum(x.size * x.dtype.itemsize for x in list(operands) + list(shapes))
    kwargs.setdefault("out_specs", jax.tree.map(lambda _: VM, out_shape))
    return pl.pallas_call(
        body,
        out_shape=out_shape,
        in_specs=list(specs or [VM] * count) + [ANY] * extra,
        compiler_params=pltpu.CompilerParams(vmem_limit_bytes=limit * 1024 * 1024),
        cost_estimate=pl.CostEstimate(
            flops=int(flops), bytes_accessed=int(nbytes), transcendentals=int(exps)
        ),
        **kwargs,
    )(*operands, *deps)


VM = pl.BlockSpec(memory_space=pltpu.VMEM)
SM = pl.BlockSpec(memory_space=pltpu.SMEM)
ANY = pl.BlockSpec(memory_space=pl.ANY)


def fresh_kernel(place_ref, rate_ref, k_in, v_in, *refs):
    outs, (k_ref, v_ref, sems) = refs[:-3], refs[-3:]
    part, size = outs[0].shape[0], outs[0].shape[1]
    length = k_ref.shape[0]
    left = length - lax.broadcasted_iota(jnp.int32, (length, size), 0).astype(F32)
    waits = []
    for a in range(len(outs)):
        first = lax.rem(place_ref[1] + len(outs) - 1 - a, len(outs)) * part
        at = pl.ds(pl.multiple_of(first * size, part * size), part * size)
        pair = []
        for n, (source, target) in enumerate(((k_in, k_ref), (v_in, v_ref))):
            pair.append(pltpu.make_async_copy(source.at[:, at], target.at[:, at], sems.at[2 * a + n]))
            pair[-1].start()
        waits.append((first, pair))
    for a, out_ref in enumerate(outs[::-1]):
        first, pair = waits[a]
        for copy in pair:
            copy.wait()
        for j in range(part):
            cols = pl.ds(pl.multiple_of((first + j) * size, size), size)
            tail = jnp.exp(rate_ref[first + j][:, :size] * left)
            high, low = halves(k_ref[:, cols].astype(F32) * tail)
            v = v_ref[:, cols]
            out_ref[j] = dot(high, v, TN) + dot(low, v, TN)


def local_kernel(rate_ref, q_in, k_ref, v_ref, out_ref, q_ref, sem):
    heads = rate_ref.shape[0]
    length = k_ref.shape[0]
    size = k_ref.shape[1] // heads
    copy = pltpu.make_async_copy(q_in, q_ref, sem)
    copy.start()
    rows = lax.broadcasted_iota(jnp.int32, (length, length), 0)
    cols = lax.broadcasted_iota(jnp.int32, (length, length), 1)
    offset = (rows - cols).astype(F32)
    keep = offset >= 0
    offset = jnp.maximum(offset, 0.0)
    copy.wait()
    for h in range(heads):
        at = slice(h * size, (h + 1) * size)
        masked = jnp.where(keep, jnp.exp(rate_ref[h] * offset), 0.0)
        weighted = (dot(q_ref[:, at], k_ref[:, at], NT) * masked).astype(BF16)
        out_ref[:, at] = dot(weighted, v_ref[:, at], NN)


def mix_kernel(recipe, coef_ref, *refs):
    count = 1 + max(i for terms in recipe for i, _ in terms)
    for j in range(refs[0].shape[0]):
        values = [refs[i][j] for i in range(count)]
        for out_ref, terms in zip(refs[count:], recipe):
            out_ref[j] = sum(values[i] * coef_ref[row, j] for i, row in terms)


def head_kernel(place_ref, rate_ref, q_ref, local_ref, *refs):
    states, out_ref = refs[:-1], refs[-1]
    part, size = states[0].shape[0], states[0].shape[1]
    length = q_ref.shape[0]
    pos = lax.broadcasted_iota(jnp.int32, (length, size), 0).astype(F32)
    for a, state_ref in enumerate(states):
        first = lax.rem(place_ref[1] + a, len(states)) * part
        for j in range(part):
            at = pl.ds(pl.multiple_of((first + j) * size, size), size)
            high, low = halves(state_ref[j])
            q = q_ref[:, at]
            carried = dot(q, high, NN) + dot(q, low, NN)
            carried = carried * jnp.exp(rate_ref[first + j][:, :size] * pos)
            attended = local_ref[:, at] + carried
            scale = lax.rsqrt(jnp.mean(attended * attended, axis=-1, keepdims=True) + 1e-05)
            out_ref[:, at] = (attended * scale).astype(BF16)


def xor_permute(x, step):
    n = lax.axis_size("ctx")
    return lax.ppermute(x, "ctx", [(d, d ^ step) for d in range(n)])


def within_group(x):
    n = lax.axis_size("ctx")
    low = n // GROUPS
    got = [x]
    for step in range(1, low):
        got.append(
            lax.ppermute(
                x, "ctx", [(d, d // low * low + (d % low - step) % low) for d in range(n)]
            )
        )
    return got


def in_order(pieces, first, axis):
    n, width = len(pieces), pieces[0].shape[axis]
    ring = jnp.concatenate(pieces + pieces[:-1], axis=axis)
    return lax.dynamic_slice_in_dim(ring, lax.rem(n - first, n) * width, n * width, axis)


def gather_doubling(x, axis, count, place, step=1):
    n = lax.axis_size(axis)
    while step < count:
        got = lax.ppermute(x, axis, [(d, d ^ step) for d in range(n)])
        upper = (place & step) != 0
        x = jnp.where(
            upper, jnp.concatenate([got, x], axis=1), jnp.concatenate([x, got], axis=1)
        )
        step *= 2
    return x


def project_kernel(low, halves_of_w, place_ref, *refs):
    heads, rests = refs[:low], refs[low + halves_of_w : 2 * low + halves_of_w]
    weights = refs[low : low + halves_of_w]
    sum_ref, sent_ref = refs[2 * low + halves_of_w :]
    length, tokens = heads[0].shape[0], rests[0].shape[0]
    for a in range(low):
        first = lax.rem(place_ref[1] + a, low) * length
        at = pl.ds(pl.multiple_of(first, length), length)
        total, start = 0.0, 0
        for w_ref in weights:
            depth = w_ref.shape[0]
            total = total + dot(heads[a][:, start : start + depth], w_ref[...], NN)
            start += depth
        sum_ref[at, :] = total
        own = pl.ds(pl.multiple_of(first + place_ref[2] * tokens, tokens), tokens)
        sum_ref[own, :] += rests[a][...].astype(F32)
        sent_ref[at, :] = sum_ref[at, :].astype(BF16)


def add_kernel(part_ref, got_ref, *outs):
    total = part_ref[...] + got_ref[...].astype(F32)
    for out_ref in outs:
        out_ref[...] = total.astype(out_ref.dtype)


def dispatch_kernel(count, others, edges, place_ref, got_ref, *refs):
    mixed, (gain_ref, picks_ref, out_ref, mixed_ref), gives = (
        refs[:count],
        refs[count : count + 4],
        refs[count + 4 :],
    )
    cols = gain_ref.shape[1]
    if edges is None:
        mixed_ref[...] = mixed[-1][...]
    else:
        outer = (place_ref[2] == edges[0]) | (place_ref[2] == edges[1])
        mixed_ref[...] = jnp.where(outer, got_ref[...], mixed[-1][...])
    value = mixed_ref[...].astype(F32)
    rows = (value * gain_ref[...]).astype(BF16)
    out_ref[:, :cols] = dot(picks_ref[...], rows, NN).astype(BF16)
    if count == 1:
        return
    mixed = list(mixed[:-1]) + [mixed_ref]
    squares = jnp.sum(value * value, axis=1, keepdims=True)
    for ref in mixed[:-1]:
        value = ref[...].astype(F32)
        squares = squares + jnp.sum(value * value, axis=1, keepdims=True)
    lane = lax.broadcasted_iota(jnp.int32, (squares.shape[0], 128), 1)
    rest, extra = squares, jnp.zeros((squares.shape[0], 128), F32)
    for place in range(3):
        high = rest.astype(BF16).astype(F32)
        extra = jnp.where(lane == place, high, extra)
        rest = rest - high
    extra = dot(picks_ref[...], extra.astype(BF16), NN).astype(BF16)
    out_ref[:, out_ref.shape[1] - 128 :] = extra
    for a, give_ref in enumerate(gives, 1):
        tokens = give_ref.shape[0]
        first = lax.rem(place_ref[1] + a, others + 1) * (mixed_ref.shape[0] // (others + 1))
        rows = pl.ds(pl.multiple_of(first + place_ref[2] * tokens, tokens), tokens)
        for t, ref in enumerate(mixed):
            give_ref[:, t * cols : (t + 1) * cols] = ref[rows, :]


def mixed_kernel(low, place_ref, *refs):
    out_ref = refs[-1]
    cols = refs[0].shape[1]
    tokens = out_ref.shape[0]
    length = refs[0].shape[0] // low
    for t in range(GROUPS):
        block = (place_ref[0] ^ t) * low
        own = pl.ds(pl.multiple_of(place_ref[1] * length + place_ref[2] * tokens, tokens), tokens)
        at = pl.multiple_of((block + place_ref[1]) * cols, cols)
        out_ref[:, pl.ds(at, cols)] = refs[t][own, :]
        for a in range(1, low):
            at = pl.multiple_of((block + lax.rem(place_ref[1] + a, low)) * cols, cols)
            got = refs[GROUPS + a - 1]
            out_ref[:, pl.ds(at, cols)] = got[:, t * cols : (t + 1) * cols]


def expert_kernel(t, spans, count, mode, model, place_ref, gate_ref, up_ref, *refs):
    refs = list(refs)
    pieces = [[refs.pop(0) for _ in range(count)] for _ in spans]
    sums = [[refs.pop(0), refs.pop(0)] for _ in spans] if t > 0 else None
    if mode == "next":
        refs.pop(0)
    outs, scratch = (refs[0], refs[1:]) if mode else (refs[: 2 * len(spans)], refs[2 * len(spans) :])
    width = scratch[0].shape[2]
    part = width // count
    copies = []
    for n, s in enumerate(spans):
        extras, held = [], scratch[0].at[n]
        for a, piece in enumerate(pieces[n]):
            member = lax.rem(place_ref[1] + a, count) if count > 1 else 0
            at = pl.multiple_of(member * part, part) if count > 1 else 0
            held[:, pl.ds(at, part)] = piece[:, :part]
            if mode:
                extras.append(piece[:, part:])
        x = held[...]
        cols = pl.ds(pl.multiple_of((place_ref[0] ^ (s ^ t)) * width, width), width)
        gated = dot(gate_ref[:, cols], x, NT)
        lifted = dot(up_ref[:, cols], x, NT)
        if sums is not None:
            gated = gated + sums[n][0][...]
            lifted = lifted + sums[n][1][...]
        if mode is None:
            outs[2 * n][...] = gated
            outs[2 * n + 1][...] = lifted
            continue
        squares = 0.0
        for extra in extras:
            lane = lax.broadcasted_iota(jnp.int32, (8, extra.shape[1]), 1)
            squares = squares + dot((lax.rem(lane, 128) < 3).astype(BF16), extra, NT)[0:1, :]
        scale = lax.rsqrt(squares / model + 1e-05)
        gated, lifted = gated * scale, lifted * scale
        ready, sems = scratch[1], scratch[2]
        ready[n] = (gated / (1.0 + jnp.exp(-gated)) * lifted).astype(BF16)
        slots = ready.shape[2]
        at = pl.ds(pl.multiple_of((place_ref[0] ^ s) * slots, slots), slots)
        copies.append(pltpu.make_async_copy(ready.at[n], outs.at[:, at], sems.at[n]))
        copies[-1].start()
    for copy in copies:
        copy.wait()


def expert_step(place, t, spans, pieces, gate, up, sums, hidden, final, deps):
    hid, model = gate.shape
    count, slots = len(pieces[0]), pieces[0][0].shape[0]
    width = model // GROUPS
    operands = [place, gate, up] + [x for per in pieces for x in per]
    if t > 0:
        operands += [x for s in spans for x in sums[s]]
    specs = [SM] + [VM] * (len(operands) - 1)
    scratch = [pltpu.VMEM((len(spans), slots, width), BF16)]
    kwargs, mode = {}, None
    if final:
        mode = "first" if hidden is None else "next"
        if hidden is not None:
            kwargs["input_output_aliases"] = {len(operands): 0}
            operands.append(hidden)
            specs.append(ANY)
        out_shape = jax.ShapeDtypeStruct((hid, slots * GROUPS), BF16)
        kwargs["out_specs"] = ANY
        scratch += [
            pltpu.VMEM((len(spans), hid, slots), BF16),
            pltpu.SemaphoreType.DMA((len(spans),)),
        ]
    else:
        out_shape = [jax.ShapeDtypeStruct((hid, slots), F32)] * (2 * len(spans))
    return call(
        functools.partial(expert_kernel, t, spans, count, mode, model),
        out_shape,
        operands,
        4 * hid * slots * width * len(spans),
        hid * slots * len(spans) if final else 0,
        deps,
        specs,
        20,
        scratch_shapes=scratch,
        **kwargs,
    )


def exchange_states(ctx, rate, mine, theirs, length, deps_one, deps_two):
    like = jax.ShapeDtypeStruct(mine.shape, F32)
    group, member = ctx // 2, lax.rem(ctx, 2)
    part = mine.shape[0]
    rates = lax.dynamic_slice(rate, (member * part,), (part,))

    def fade(blocks):
        return jnp.exp(-rates * (length * blocks))

    one, none = jnp.ones_like(rates), jnp.zeros_like(rates)
    first = member == 0
    rows = [
        jnp.where(first, one, none),
        jnp.where(first, none, one),
        jnp.where(first, fade(1.0), one),
        jnp.where(first, one, fade(1.0)),
    ]
    step = 1
    while step < GROUPS:
        upper = (group & step) != 0
        span = fade(2.0 * step)
        rows += [
            jnp.where(upper, fade(2.0 * (group & (step - 1)).astype(F32)), none),
            jnp.where(upper, span, one),
            jnp.where(upper, one, span),
        ]
        step *= 2
    rows += [
        jnp.where(first, one, fade(1.0)),
        jnp.where(first, fade(1.0), one),
        jnp.where(first, none, one),
        jnp.where(first, one, none),
        one,
    ]
    size = mine.shape[2]
    coef = jnp.broadcast_to(jnp.stack(rows)[:, :, None, None], (len(rows), part, 1, size))

    def mix(recipe, values, deps=()):
        return call(
            functools.partial(mix_kernel, recipe), [like] * len(recipe), [coef] + values, 0, deps=deps
        )

    got = xor_permute(theirs, 1)
    early, total = mix([[(0, 0), (1, 1)], [(0, 2), (1, 3)]], [mine, got])
    state, step, row = None, 1, 4
    while 2 * step < GROUPS:
        mark, got = total, xor_permute(total, 2 * step)
        recipe = [[(0, row)], [(0, row + 1), (1, row + 2)]]
        values = [got, total]
        if state is not None:
            recipe[0].append((2, len(rows) - 1))
            values.append(state)
        state, total = mix(recipe, values, deps_one(mark, got))
        step, row = 2 * step, row + 3
    got = lax.ppermute(total, "ctx", [(d, d + 2 * step) for d in range(2 * step)])
    end = len(rows) - 5
    final = mix([[(0, len(rows) - 1), (1, row)]], [state, got], deps_two(total))[0]
    keep, give = mix(
        [[(0, end), (1, end + 2)], [(0, end + 1), (1, end + 3)]], [final, early]
    )
    return [keep, xor_permute(give, 1)], keep


def states_by_steps(ctx, decay_rate, total, length):
    n_ctx = lax.axis_size("ctx")

    def faded(blocks):
        return jnp.exp(-decay_rate * (length * blocks))[:, None, None]

    state, step = jnp.zeros_like(total), 1
    while step < n_ctx:
        upper = (ctx & step) != 0
        got = xor_permute(total, step)
        state = state + jnp.where(upper, faded((ctx & (step - 1)).astype(F32)), 0.0) * got
        span = faded(float(step))
        total = jnp.where(upper, span * got + total, span * total + got)
        step *= 2
    return [state]


def tie(x, *deps):
    def copy_kernel(in_ref, out_ref):
        out_ref[...] = in_ref[...]

    return call(copy_kernel, jax.ShapeDtypeStruct(x.shape, x.dtype), [x], 0, deps=deps)


def split_kernel(in_ref, *outs):
    start = 0
    for out_ref in outs:
        out_ref[...] = in_ref[start : start + out_ref.shape[0], :]
        start += out_ref.shape[0]


def per_device(
    queries,
    key_rows,
    value_rows,
    decay_rate,
    out_weight,
    residual,
    moe_gain,
    expert_ids,
    gate_weight,
    up_weight,
):
    n_ctx, n_exp = lax.axis_size("ctx"), lax.axis_size("exp")
    low = n_ctx // GROUPS
    ctx, exp = lax.axis_index("ctx"), lax.axis_index("exp")
    group, member = ctx // low, lax.rem(ctx, low)
    place = jnp.stack([group, member, exp]).astype(jnp.int32)
    length, here = queries.shape
    heads = decay_rate.shape[0]
    size = here // heads
    model = residual.shape[1]
    cols = model // n_ctx
    tokens = length // n_exp
    capacity = max(2, 3 * tokens // n_exp)
    aligned = cols % 128 == 0
    pairs = low == 2 and heads % 2 == 0
    every = low * length
    slots = low * n_exp * capacity

    cut = out_weight.shape[0] // 2
    half_w = jax.ShapeDtypeStruct((cut, cols), BF16)

    def split(*deps):
        return call(split_kernel, [half_w] * 2, [out_weight], 0, deps=deps)

    ids = expert_ids.T
    rate = jnp.broadcast_to(-decay_rate[:, None, None], (heads, 1, length))

    wide_b16 = jax.ShapeDtypeStruct((length, here), BF16)
    outs = (
        [jax.ShapeDtypeStruct((heads // 2, size, size), F32)] * 2
        if pairs
        else [jax.ShapeDtypeStruct((heads, size, size), F32)]
    )
    *fresh, keys, values = call(
        fresh_kernel,
        outs + [wide_b16] * 2,
        [place, rate, key_rows, value_rows],
        4 * heads * length * size * size,
        heads * length * size,
        specs=[SM, VM, ANY, ANY],
        scratch_shapes=[pltpu.SemaphoreType.DMA((2 * len(outs),))],
    )

    def run_local(*deps):
        return call(
            local_kernel,
            [jax.ShapeDtypeStruct((length, here), F32), wide_b16],
            [rate, queries, keys, values],
            4 * heads * length * length * size,
            heads * length * length,
            deps,
            [VM, ANY, VM, VM],
            scratch_shapes=[pltpu.SemaphoreType.DMA(())],
        )

    if pairs:
        side = {}

        def deps_one(total, got):
            side["ids"] = gather_doubling(ids, "exp", 2, exp)
            side["local"] = run_local(total)
            side["rest"] = within_group(residual)
            side["w"] = split(got)
            side["one"] = [xor_permute(w, low) for w in side["w"]]
            return [side["local"][0], side["ids"], side["rest"][1]]

        def deps_two(total):
            side["ids"] = gather_doubling(tie(side["ids"], total), "exp", n_exp, exp, 2)
            return [side["ids"]]

        states, kept = exchange_states(
            ctx, decay_rate, fresh[0], fresh[1], length, deps_one, deps_two
        )
        ids, (local, queries_here), rest_rows, one = (
            side["ids"], side["local"], side["rest"], side["one"]
        )
        deps = [one[0]]
    else:
        states = states_by_steps(ctx, decay_rate, fresh[0], length)
        (local, queries_here), rest_rows = run_local(), within_group(residual)
        ids = gather_doubling(ids, "exp", n_exp, exp)
        one = [xor_permute(w, low) for w in split()]
        deps = []

    head_out = call(
        head_kernel,
        wide_b16,
        [place, rate, queries_here, local] + states,
        4 * heads * length * size * size,
        heads * length * size,
        deps,
        [SM] + [VM] * (3 + len(states)),
    )
    group_heads = within_group(head_out)

    w_top, w_bottom = split(head_out)
    two = [xor_permute(w_top, 2 * low), None]
    columns = [[out_weight], one, two, [None, None]]
    ids = gather_doubling(tie(ids, head_out), "ctx", low, member)
    pins = {}

    def after_kernel(name, t, out):
        if (name, t) == ("project", 0):
            pins["add", 0] = [two[0], ids]
            two[1] = xor_permute(tie(w_bottom, out), 2 * low)
        if (name, t) == ("add", 0):
            columns[3][0] = xor_permute(tie(one[0], out), 2 * low)
        if (name, t) == ("project", 2):
            pins["dispatch", 0] = [columns[3][0]]
            columns[3][1] = xor_permute(tie(two[1], out), low)

    named = (ids[0] == exp) | (ids[1] == exp)
    token = jnp.arange(every, dtype=jnp.int32)
    earlier = (token[:, None] < token[None, :]) & (
        token[:, None] // tokens == token[None, :] // tokens
    )
    rank = jnp.sum((earlier & named[:, None]).astype(jnp.int32), axis=0)
    row = jnp.where(named & (rank < capacity), token // tokens * capacity + rank, -1)
    picks = (jnp.arange(slots, dtype=jnp.int32)[:, None] == row[None, :]).astype(BF16)

    gains, rests = [], []
    for t in range(GROUPS):
        start = (((group ^ t) * low + member) * cols).astype(jnp.int32)
        gains.append(lax.dynamic_slice(moe_gain, (start,), (cols,))[None])
        rests.append(
            [lax.dynamic_slice(r, (jnp.int32(0), start), (tokens, cols)) for r in rest_rows]
        )
    gate, up = gate_weight[0], up_weight[0]

    chunk_f32 = jax.ShapeDtypeStruct((every, cols), F32)
    chunk_b16 = jax.ShapeDtypeStruct((every, cols), BF16)
    half = n_exp // 2
    mixed, received = [None] * GROUPS, [None] * GROUPS
    sums, gives, hidden = [None] * GROUPS, [], None
    links, last = [None] * GROUPS, [head_out]

    def chunk(t):
        final = t == GROUPS - 1
        part, sent = call(
            functools.partial(project_kernel, low, len(columns[t])),
            [chunk_f32, chunk_b16],
            [place] + group_heads + columns[t] + rests[t],
            2 * every * here * cols,
            deps=last[:] + (one[1:] if t == 0 else []),
            specs=[SM] + [VM] * (2 * low + len(columns[t])),
        )
        last[:] = [sent]
        after_kernel("project", t, sent)
        for hop in range(half - 1):
            got = lax.ppermute(sent, "exp", [(hop, hop + 1), (n_exp - 1 - hop, n_exp - 2 - hop)])
            yield
            part, sent = call(
                add_kernel,
                [chunk_f32, chunk_b16],
                [part, got],
                every * cols,
                deps=last[:] + (pins.get(("add", t), []) if hop == 0 else []),
            )
            last[:] = [sent]
            if hop == 0:
                after_kernel("add", t, sent)
        got = lax.ppermute(sent, "exp", [(half - 1, half), (half, half - 1)])
        yield
        total = call(add_kernel, chunk_b16, [part, got], every * cols, deps=last[:])
        last[:] = [total]
        edges = None
        for hop in range(half - 1):
            if edges is not None:
                total = jnp.where((exp == edges[0]) | (exp == edges[1]), got, total)
            here_, there = half - 1 - hop, half + hop
            got = lax.ppermute(total, "exp", [(here_, here_ - 1), (there, there + 1)])
            edges = (here_ - 1, there + 1)
            yield
        wide = (cols + 127) // 128 * 128 + 128 if final else cols
        known = mixed[:t] if final else []
        outs = [jax.ShapeDtypeStruct((slots, wide), BF16), chunk_b16]
        if final and aligned:
            outs += [jax.ShapeDtypeStruct((tokens, GROUPS * cols), BF16)] * (low - 1)
        x, mixed[t], *gives[:] = call(
            functools.partial(dispatch_kernel, len(known) + 1, low - 1, edges),
            outs,
            [place, got] + known + [total, gains[t], picks],
            2 * slots * every * wide,
            deps=last[:] + (links[t - 1] if t > 0 else []) + pins.get(("dispatch", t), []),
            specs=[SM] + [VM] * (len(known) + 4),
        )
        last[:] = [x]
        near, far = xor_permute(x, low), xor_permute(x, 2 * low)
        got = [within_group(x)]
        links[t] = [near, far]
        yield
        if t % 2 == 0:
            diagonal = xor_permute(tie(near, *last) if t > 1 else near, 2 * low)
        else:
            diagonal = xor_permute(tie(far, *last) if t > 1 else far, low)
        got += [within_group(near), within_group(far)]
        received[t] = [in_columns(per, t) for per in got]
        yield
        experts(t, everyone[:-1])
        received[t].append(in_columns(within_group(tie(diagonal, *last)), t))
        yield
        experts(t, everyone[-1:])
        yield

    def in_columns(per, t):
        if aligned:
            return per
        whole = in_order([y[:, :cols] for y in per], member, 1)
        if t == GROUPS - 1:
            whole = jnp.concatenate([whole] + [y[:, -128:] for y in per], axis=1)
        return [whole]

    def experts(t, spans):
        nonlocal hidden
        final = t == GROUPS - 1
        pieces = [received[t][s] for s in spans]
        out = expert_step(
            place, t, spans, pieces, gate, up, sums, hidden, final, last[:]
        )
        if final:
            hidden = out
        else:
            for n, s in enumerate(spans):
                sums[s] = out[2 * n : 2 * n + 2]
            last[:] = [out[0]]

    everyone = list(range(GROUPS))
    running, waiting = [], everyone[:]
    while running or waiting:
        if waiting:
            running.insert(0, chunk(waiting.pop(0)))
        for work in list(running):
            if next(work, "end") == "end":
                running.remove(work)

    own = exp * tokens
    gotten = []
    for a in range(1, low):
        if aligned:
            give = gives[a - 1]
        else:
            first = lax.rem(member + a, low) * length + own
            rows = [lax.dynamic_slice_in_dim(m, first, tokens, 0) for m in mixed]
            give = jnp.concatenate(rows, axis=1)
        gotten.append(
            lax.ppermute(
                give, "ctx", [(d, d // low * low + (d % low + a) % low) for d in range(n_ctx)]
            )
        )
    gotten = gotten[::-1]
    if aligned:
        mixed_out = call(
            functools.partial(mixed_kernel, low),
            jax.ShapeDtypeStruct((tokens, model), BF16),
            [place] + mixed + gotten,
            0,
            specs=[SM] + [VM] * (GROUPS + low - 1),
        )
    else:
        rows = [lax.dynamic_slice_in_dim(m, member * length + own, tokens, 0) for m in mixed]
        parts = [jnp.concatenate(rows, axis=1)] + gotten
        mixed_out = jnp.zeros((tokens, model), BF16)
        for a, part in enumerate(parts):
            for t in range(GROUPS):
                start = ((group ^ t) * low + lax.rem(member + a, low)) * cols
                mixed_out = lax.dynamic_update_slice_in_dim(
                    mixed_out, part[:, t * cols : (t + 1) * cols], start, 1
                )
    return (mixed_out, hidden[None])


def solution(mesh):
    in_specs = (
        P("ctx", "exp"),
        P("ctx", "exp"),
        P("ctx", "exp"),
        P("exp"),
        P("exp", "ctx"),
        P(("ctx", "exp"), None),
        P(),
        P(("ctx", "exp"), None),
        P("exp", "ctx", None),
        P("exp", "ctx", None),
    )
    out_specs = (P(("ctx", "exp"), None), P("exp", "ctx", None))
    return jax.shard_map(
        per_device, mesh=mesh, in_specs=in_specs, out_specs=out_specs, check_vma=False
    )
```

```python
import functools

import jax
import jax.numpy as jnp
from jax import lax
from jax.experimental import pallas as pl
from jax.experimental.pallas import tpu as pltpu
from jax.sharding import PartitionSpec as P

GROUPS = 4
CORES = 2
LANES = 128
BF16 = jnp.bfloat16
F32 = jnp.float32
NT = (((1,), (1,)), ((), ()))
TN = (((0,), (0,)), ((), ()))
NN = (((1,), (0,)), ((), ()))
VM = pl.BlockSpec(memory_space=pltpu.VMEM)
SM = pl.BlockSpec(memory_space=pltpu.SMEM)
HBM = pl.BlockSpec(memory_space=pltpu.HBM)
ANY = pl.BlockSpec(memory_space=pl.ANY)


def dot(a, b, dims):
    return lax.dot_general(a, b, dims, preferred_element_type=F32)


def halves(x):
    high = x.astype(BF16)
    return high, (x - high.astype(F32)).astype(BF16)


def like(shape, dtype=BF16):
    return jax.ShapeDtypeStruct(tuple(shape), dtype)


def call(kernel, out_shape, operands, flops=0, exps=0, deps=(), specs=None, limit=12, **kwargs):
    count, extra = len(operands), len(deps)

    def body(*refs):
        kernel(*refs[:count], *refs[count + extra :])

    shapes = out_shape if isinstance(out_shape, (list, tuple)) else [out_shape]
    nbytes = sum(x.size * x.dtype.itemsize for x in list(operands) + list(shapes))
    kwargs.setdefault("out_specs", jax.tree.map(lambda _: VM, out_shape))
    return pl.pallas_call(
        body,
        out_shape=out_shape,
        in_specs=list(specs or [VM] * count) + [ANY] * extra,
        compiler_params=pltpu.CompilerParams(vmem_limit_bytes=limit * 1024 * 1024),
        cost_estimate=pl.CostEstimate(
            flops=int(flops), bytes_accessed=int(nbytes), transcendentals=int(exps)
        ),
        **kwargs,
    )(*operands, *deps)


def tile(index, size):
    return pl.ds(pl.multiple_of(index * size, size), size)


def fresh_kernel(place_ref, rate_ref, k_in, v_in, mine_ref, theirs_ref, k_ref, v_ref, sems):
    part, size = mine_ref.shape[0], mine_ref.shape[1]
    length = k_ref.shape[0]
    left = length - lax.broadcasted_iota(jnp.int32, (length, size), 0).astype(F32)
    order = ((theirs_ref, 1 - place_ref[1]), (mine_ref, place_ref[1]))
    copies = []
    for n, (_, half) in enumerate(order):
        at = tile(half, part * size)
        for source, target in ((k_in, k_ref), (v_in, v_ref)):
            copies.append(
                pltpu.make_async_copy(source.at[:, at], target.at[:, at], sems.at[len(copies)])
            )
            copies[-1].start()
    for n, (out_ref, half) in enumerate(order):
        copies[2 * n].wait()
        copies[2 * n + 1].wait()
        for j in range(part):
            head = half * part + j
            cols = tile(head, size)
            tail = jnp.exp(rate_ref[head][:, :size] * left)
            high, low = halves(k_ref[:, cols].astype(F32) * tail)
            v = v_ref[:, cols]
            out_ref[j] = dot(high, v, TN) + dot(low, v, TN)


def local_kernel(rate_ref, q_in, k_ref, v_ref, out_ref, q_ref, sem):
    heads = rate_ref.shape[0]
    length = k_ref.shape[0]
    size = k_ref.shape[1] // heads
    copy = pltpu.make_async_copy(q_in, q_ref, sem)
    copy.start()
    rows = lax.broadcasted_iota(jnp.int32, (length, length), 0)
    cols = lax.broadcasted_iota(jnp.int32, (length, length), 1)
    offset = (rows - cols).astype(F32)
    keep = offset >= 0
    offset = jnp.maximum(offset, 0.0)
    copy.wait()
    for h in range(heads):
        at = slice(h * size, (h + 1) * size)
        masked = jnp.where(keep, jnp.exp(rate_ref[h] * offset), 0.0)
        weighted = (dot(q_ref[:, at], k_ref[:, at], NT) * masked).astype(BF16)
        out_ref[:, at] = dot(weighted, v_ref[:, at], NN)


def mix_kernel(recipe, coef_ref, *refs):
    count = 1 + max(i for terms in recipe for i, _ in terms)
    for j in range(refs[0].shape[0]):
        values = [refs[i][j] for i in range(count)]
        for out_ref, terms in zip(refs[count:], recipe):
            out_ref[j] = sum(values[i] * coef_ref[row, j] for i, row in terms)


def scan_rows(chip, core, rate, part, length):
    rates = lax.dynamic_slice(rate, (core * part,), (part,))

    def fade(blocks):
        return jnp.exp(-rates * (length * blocks))

    one, none = jnp.ones_like(rates), jnp.zeros_like(rates)
    first, east, south = core == 0, (chip & 1) != 0, (chip & 2) != 0
    behind = jnp.where(south, fade(2.0 * (chip & 1).astype(F32)), none)
    keep, give = jnp.where(first, one, fade(1.0)), jnp.where(first, fade(1.0), one)
    return [
        jnp.where(first, one, none),
        jnp.where(first, none, one),
        jnp.where(first, fade(1.0), one),
        jnp.where(first, one, fade(1.0)),
        jnp.where(east, one, none),
        jnp.where(east, fade(2.0), one),
        jnp.where(east, one, fade(2.0)),
        keep,
        keep * behind,
        jnp.where(first, none, one),
        give,
        give * behind,
        jnp.where(first, one, none),
    ]


def head_kernel(place_ref, rate_ref, q_ref, local_ref, keep_ref, got_ref, out_ref):
    part, size = keep_ref.shape[0], keep_ref.shape[1]
    length = q_ref.shape[0]
    pos = lax.broadcasted_iota(jnp.int32, (length, size), 0).astype(F32)
    for state_ref, half in ((keep_ref, place_ref[1]), (got_ref, 1 - place_ref[1])):
        for j in range(part):
            head = half * part + j
            at = tile(head, size)
            high, low = halves(state_ref[j])
            q = q_ref[:, at]
            carried = dot(q, high, NN) + dot(q, low, NN)
            carried = carried * jnp.exp(rate_ref[head][:, :size] * pos)
            attended = local_ref[:, at] + carried
            scale = lax.rsqrt(jnp.mean(attended * attended, axis=-1, keepdims=True) + 1e-05)
            out_ref[:, at] = (attended * scale).astype(BF16)


def larger_kernel(a_ref, b_ref, out_ref):
    out_ref[...] = jnp.maximum(a_ref[...], b_ref[...])


def stack_kernel(which, place_ref, a_ref, b_ref, out_ref):
    rows = a_ref.shape[0]
    upper = (place_ref[which] >> (1 if which == 2 else 0)) & 1
    out_ref[tile(upper, rows), :] = a_ref[...]
    out_ref[tile(1 - upper, rows), :] = b_ref[...]


def picks_kernel(tokens, capacity, place_ref, own_ref, got_ref, out_ref):
    slots = out_ref.shape[0]
    before = lax.broadcasted_iota(jnp.int32, (LANES, LANES), 0)
    token = lax.broadcasted_iota(jnp.int32, (LANES, LANES), 1)
    earlier = ((before < token) & (before // tokens == token // tokens)).astype(BF16)
    lane = lax.broadcasted_iota(jnp.int32, (8, LANES), 1)
    slot = lax.broadcasted_iota(jnp.int32, (slots, LANES), 0)
    per = own_ref.shape[0] // 8
    for ref, half in ((own_ref, place_ref[1]), (got_ref, 1 - place_ref[1])):
        for n in range(per):
            first, second = ref[8 * n : 8 * n + 1, :], ref[8 * n + 1 : 8 * n + 2, :]
            named = (first == place_ref[2]) | (second == place_ref[2])
            named = jnp.broadcast_to(named.astype(F32), (8, LANES))
            rank = dot(named.astype(BF16), earlier, NN).astype(jnp.int32)
            run = half * per + n
            row = (run * (LANES // tokens) + lane // tokens) * capacity + rank
            row = jnp.where((named > 0.5) & (rank < capacity), row, -1)
            out_ref[:, tile(run, LANES)] = (slot == row[0:1, :]).astype(BF16)


def project_kernel(t, place_ref, own_ref, got_ref, rest_ref, rest_got_ref, *refs):
    weights, (sum_ref, sent_ref) = refs[:-2], refs[-2:]
    length, tokens, cols = own_ref.shape[0], rest_ref.shape[0], sum_ref.shape[1]
    first = place_ref[1] == 0
    weight = weights[0][...]
    if len(weights) > 1:
        weight = jnp.where(first, weight, weights[1][...])
    at = tile((place_ref[0] ^ t) * CORES + place_ref[1], cols)
    for head_ref, row_ref, half in (
        (own_ref, rest_ref, place_ref[1]),
        (got_ref, rest_got_ref, 1 - place_ref[1]),
    ):
        value = dot(head_ref[...], weight, NN)
        pieces = []
        for z in range(length // tokens):
            piece = value[z * tokens : (z + 1) * tokens, :]
            pieces.append(
                jnp.where(place_ref[2] == z, piece + row_ref[:, at].astype(F32), piece)
            )
        value = jnp.concatenate(pieces, axis=0)
        sum_ref[tile(half, length), :] = value
        sent_ref[tile(half, length), :] = value.astype(BF16)


def inward_kernel(part_ref, got_ref, sum_ref, sent_ref):
    total = part_ref[...] + got_ref[...].astype(F32)
    sum_ref[...] = total
    sent_ref[...] = total.astype(BF16)


def outer(place_ref):
    return (place_ref[2] == 0) | (place_ref[2] == 3)


def outward_kernel(place_ref, part_ref, got_ref, *refs):
    total = (part_ref[...] + got_ref[...].astype(F32)).astype(BF16)
    if len(refs) > 1:
        total = jnp.where(outer(place_ref), refs[0][...], total)
    refs[-1][...] = total


def dispatch_kernel(t, place_ref, got_ref, given_ref, gain_ref, picks_ref, *refs):
    earlier, (out_ref, mixed_ref), gives = refs[:-2], refs[-2:], []
    if t == GROUPS - 1:
        earlier, (out_ref, mixed_ref, give_ref) = refs[:-3], refs[-3:]
        gives = [give_ref]
    cols = mixed_ref.shape[1]
    mixed = jnp.where(outer(place_ref), got_ref[...], given_ref[...])
    mixed_ref[...] = mixed
    value = mixed.astype(F32)
    gain = gain_ref[:, tile((place_ref[0] ^ t) * CORES + place_ref[1], cols)]
    out_ref[:, :cols] = dot(picks_ref[...], (value * gain).astype(BF16), NN).astype(BF16)
    if not gives:
        return
    squares = jnp.sum(value * value, axis=1, keepdims=True)
    for ref in earlier:
        value = ref[...].astype(F32)
        squares = squares + jnp.sum(value * value, axis=1, keepdims=True)
    extra = dot(picks_ref[...], in_three(squares), NN)
    out_ref[:, cols:] = extra.astype(BF16)
    tokens = give_ref.shape[0]
    per = mixed_ref.shape[0] // CORES // tokens
    rows = tile((1 - place_ref[1]) * per + place_ref[2], tokens)
    for n, ref in enumerate(list(earlier) + [mixed_ref]):
        give_ref[:, n * cols : (n + 1) * cols] = ref[rows, :]


def in_three(column):
    lane = lax.broadcasted_iota(jnp.int32, (column.shape[0], LANES), 1)
    rest, out = column, jnp.zeros((column.shape[0], LANES), F32)
    for place in range(3):
        high = rest.astype(BF16).astype(F32)
        out = jnp.where(lane == place, high, out)
        rest = rest - high
    return out.astype(BF16)


def join_kernel(cols, place_ref, own_ref, got_ref, out_ref):
    out_ref[:, tile(place_ref[1], cols)] = own_ref[:, :cols]
    out_ref[:, tile(1 - place_ref[1], cols)] = got_ref[:, :cols]
    if own_ref.shape[1] > cols:
        extra = own_ref[:, cols:].astype(F32) + got_ref[:, cols:].astype(F32)
        total = jnp.sum(extra, axis=1, keepdims=True)
        out_ref[:, CORES * cols :] = in_three(total)


def half_kernel(place_ref, in_ref, out_ref):
    out_ref[...] = in_ref[tile(place_ref[1], out_ref.shape[0]), :]


def both_kernel(place_ref, own_ref, got_ref, out_ref):
    rows = own_ref.shape[0]
    out_ref[tile(place_ref[1], rows), :] = own_ref[...]
    out_ref[tile(1 - place_ref[1], rows), :] = got_ref[...]


def parts_kernel(place_ref, in_ref, keep_ref, give_ref):
    rows = keep_ref.shape[0]
    keep_ref[...] = in_ref[tile(place_ref[1], rows), :]
    give_ref[...] = in_ref[tile(1 - place_ref[1], rows), :]


def mixed_kernel(place_ref, got_ref, *refs):
    mixed, out_ref = refs[:-1], refs[-1]
    tokens, cols = out_ref.shape[0], mixed[0].shape[1]
    per = mixed[0].shape[0] // CORES // tokens
    own = tile(place_ref[1] * per + place_ref[2], tokens)
    for t, ref in enumerate(mixed):
        block = (place_ref[0] ^ t) * CORES
        out_ref[:, tile(block + place_ref[1], cols)] = ref[own, :]
        out_ref[:, tile(block + 1 - place_ref[1], cols)] = got_ref[:, t * cols : (t + 1) * cols]


ROLES = ("own", "mine", "other", "diagonal")


def expert_kernel(t, roles, mode, place_ref, gate_ref, up_ref, *refs):
    refs = list(refs)
    pieces = [[refs.pop(0) for _ in range(2 if r == "diagonal" else 1)] for r in roles]
    sums = [[refs.pop(0), refs.pop(0)] for _ in roles] if t > 0 else None
    if mode == "next":
        refs.pop(0)
    model = gate_ref.shape[1]
    width = model // GROUPS
    away = {"own": 0, "mine": 1 + place_ref[1], "other": 2 - place_ref[1], "diagonal": 3}
    if mode is None:
        outs = refs[: 2 * len(roles)]
        held = refs[2 * len(roles) :]
    else:
        outs, ready, sems = refs[0], refs[1], refs[2]
        held = refs[3:]
    copies = []
    for n, role in enumerate(roles):
        source = place_ref[0] ^ away[role]
        ref = pieces[n][0]
        if role == "diagonal":
            rows = ref.shape[0]
            held[0][tile(place_ref[1], rows), :] = ref[...]
            held[0][tile(1 - place_ref[1], rows), :] = pieces[n][1][...]
            ref = held[0]
        x = ref[:, :width]
        cols = tile(source ^ t, width)
        gated = dot(gate_ref[:, cols], x, NT)
        lifted = dot(up_ref[:, cols], x, NT)
        if sums is not None:
            gated = gated + sums[n][0][...]
            lifted = lifted + sums[n][1][...]
        if mode is None:
            outs[2 * n][...] = gated
            outs[2 * n + 1][...] = lifted
            continue
        lane = lax.broadcasted_iota(jnp.int32, (8, LANES), 1)
        squares = dot((lane < 3).astype(BF16), ref[:, width:], NT)[0:1, :]
        scale = lax.rsqrt(squares / model + 1e-05)
        gated, lifted = gated * scale, lifted * scale
        silu = (0.5 * gated) * (1.0 + jnp.tanh(0.5 * gated))
        ready[n] = (silu * lifted).astype(BF16)
        at = tile(source, ready.shape[2])
        copies.append(pltpu.make_async_copy(ready.at[n], outs.at[:, at], sems.at[n]))
        copies[-1].start()
    for copy in copies:
        copy.wait()


def expert_step(place, t, roles, pieces, gate, up, sums, hidden, deps):
    hid, model = gate.shape
    width = model // GROUPS
    slots = sum(x.shape[0] for x in pieces[0])
    operands = [place, gate, up] + [x for per in pieces for x in per]
    if t > 0:
        operands += [x for r in roles for x in sums[r]]
    specs = [SM] + [VM] * (len(operands) - 1)
    kwargs, mode, scratch = {}, None, []
    if t == GROUPS - 1:
        mode = "first" if hidden is None else "next"
        if hidden is not None:
            kwargs["input_output_aliases"] = {len(operands): 0}
            operands.append(hidden)
            specs.append(ANY)
        out_shape = like((hid, slots * GROUPS))
        kwargs["out_specs"] = ANY
        scratch += [
            pltpu.VMEM((len(roles), hid, slots), BF16),
            pltpu.SemaphoreType.DMA((len(roles),)),
        ]
    else:
        out_shape = [like((hid, slots), F32)] * (2 * len(roles))
    if "diagonal" in roles:
        wide = pieces[roles.index("diagonal")][0].shape[1]
        scratch.append(pltpu.VMEM((slots, wide), BF16))
    out = call(
        functools.partial(expert_kernel, t, roles, mode),
        out_shape,
        operands,
        4 * hid * slots * width * len(roles),
        hid * slots * len(roles) if mode else 0,
        deps,
        specs,
        20,
        scratch_shapes=scratch,
        **kwargs,
    )
    if mode:
        return out, None
    for n, r in enumerate(roles):
        sums[r] = out[2 * n : 2 * n + 2]
    return hidden, out[0]


def send(x, axis, pairs):
    return lax.ppermute(x, axis, pairs)


def swap(x):
    return send(x, "ctx", [(d, d ^ 1) for d in range(lax.axis_size("ctx"))])


def outbound(x):
    return send(x, "ctx", [(d, d ^ (4 if d % 2 else 2)) for d in range(lax.axis_size("ctx"))])


def onward(x):
    return send(x, "ctx", [(d, d ^ (2 if d % 2 else 4)) for d in range(lax.axis_size("ctx"))])


def on_square(
    queries,
    key_rows,
    value_rows,
    decay_rate,
    out_weight,
    residual,
    moe_gain,
    expert_ids,
    gate_weight,
    up_weight,
):
    ctx, exp = lax.axis_index("ctx"), lax.axis_index("exp")
    chip, core = ctx // CORES, lax.rem(ctx, CORES)
    place = jnp.stack([chip, core, exp]).astype(jnp.int32)
    length, here = queries.shape
    heads = decay_rate.shape[0]
    size = here // heads
    part = heads // CORES
    tokens, model = residual.shape
    cols = model // GROUPS // CORES
    capacity = max(2, 3 * tokens // lax.axis_size("exp"))
    every = CORES * length
    slots = every // tokens * capacity
    gate, up = gate_weight[0], up_weight[0]
    last = []

    def run(kernel, out_shape, operands, *more, deps=(), **kwargs):
        out = call(kernel, out_shape, operands, *more, deps=list(last) + list(deps), **kwargs)
        last[:] = [out[0] if isinstance(out, (list, tuple)) else out]
        return out

    rate = jnp.broadcast_to(-decay_rate[:, None, None], (heads, 1, length))
    rows = jnp.stack(scan_rows(chip, core, decay_rate, part, length))
    coef = jnp.broadcast_to(rows[:, :, None, None], rows.shape + (1, size))
    turned = jnp.tile(expert_ids.T, (1, LANES // tokens))
    lane = jnp.arange(LANES, dtype=jnp.int32)[None, :]
    ids = jnp.where(lane // tokens == exp % (LANES // tokens), turned, -1)
    ids = jnp.pad(ids, ((0, 6), (0, 0)), constant_values=-1)
    gain = moe_gain[None, :] * 1.0

    state_like = like((part, size, size), F32)
    mine, theirs, keys, values = run(
        fresh_kernel,
        [state_like] * 2 + [like((length, here))] * 2,
        [place, rate, key_rows, value_rows],
        4 * heads * length * size * size,
        heads * length * size,
        deps=[coef, ids],
        specs=[SM, VM, HBM, HBM],
        scratch_shapes=[pltpu.SemaphoreType.DMA((4,))],
    )

    def mix(recipe, operands, deps=()):
        return run(
            functools.partial(mix_kernel, recipe),
            [state_like] * len(recipe),
            [coef] + operands,
            deps=deps,
        )

    got = swap(theirs)
    first, total = mix([[(0, 0), (1, 1)], [(0, 2), (1, 3)]], [mine, got])
    got = send(total, "ctx", [(d, d ^ 2) for d in range(8)])
    ids_got = send(ids, "exp", [(d, d ^ 1) for d in range(4)])
    rest_got = swap(residual)
    weight_got = swap(out_weight)
    local, queries_here = run(
        local_kernel,
        [like((length, here), F32), like((length, here))],
        [rate, queries, keys, values],
        4 * heads * length * length * size,
        heads * length * length,
        specs=[VM, HBM, VM, VM],
        scratch_shapes=[pltpu.SemaphoreType.DMA(())],
    )
    ids = run(larger_kernel, like(ids.shape, ids.dtype), [ids, ids_got])
    state, total = mix(
        [[(0, 4)], [(0, 5), (1, 6)]], [got, total], [rest_got, weight_got]
    )
    got = send(total, "ctx", [(d, d + 4) for d in range(4)])
    ids_got = send(ids, "exp", [(d, d ^ 2) for d in range(4)])
    ids = run(
        functools.partial(stack_kernel, 2),
        like((16, LANES), ids.dtype),
        [place, ids, ids_got],
        specs=[SM, VM, VM],
    )
    keep, give = mix(
        [[(0, 7), (1, 8), (2, 9)], [(0, 10), (1, 11), (2, 12)]], [state, got, first]
    )
    got = swap(give)
    ids_got = swap(ids)
    whole_weight = run(
        both_kernel,
        like((CORES * here, cols)),
        [place, out_weight, weight_got],
        specs=[SM, VM, VM],
    )
    weight_in = outbound(whole_weight)
    head_out = run(
        head_kernel,
        like((length, here)),
        [place, rate, queries_here, local, keep, got],
        4 * heads * length * size * size,
        heads * length * size,
        specs=[SM] + [VM] * 5,
    )
    heads_got = swap(head_out)
    picks = run(
        functools.partial(picks_kernel, tokens, capacity),
        like((slots, every)),
        [place, ids, ids_got],
        specs=[SM, VM, VM],
    )

    chunk_f32, chunk_b16 = like((every, cols), F32), like((every, cols))
    wide = [cols + LANES * (t == GROUPS - 1) for t in range(GROUPS)]
    weights = {0: [out_weight]}
    part_of, sent, mixed, joined, near, far = {}, {}, {}, {}, {}, {}
    along, across, given = {}, {}, {}
    sums, hidden, mixed_out = {}, None, None

    def project(t):
        part_of[t], sent[t] = run(
            functools.partial(project_kernel, t),
            [chunk_f32, chunk_b16],
            [place, head_out, heads_got, residual, rest_got] + weights[t],
            2 * every * here * cols,
            specs=[SM] + [VM] * (4 + len(weights[t])),
        )

    def experts(t, roles, pieces):
        nonlocal hidden
        hidden, mark = expert_step(place, t, roles, pieces, gate, up, sums, hidden, last[:])
        if mark is not None:
            last[:] = [mark]

    project(0)
    for k in range(GROUPS + 7):
        if 1 <= k <= GROUPS:
            t = k - 1
            part_of[t], out = run(
                inward_kernel, [chunk_f32, chunk_b16], [part_of[t], along[t]], every * cols
            )
            across[t] = send(out, "exp", [(1, 2), (2, 1)])
        if k == 1:
            kept, other = run(
                parts_kernel, [like((here, cols))] * 2, [place, weight_in], specs=[SM, VM]
            )
            other = swap(other)
            weights[3] = [onward(kept)]
            weights[1], weights[2] = [kept, other], [other, kept]
            project(1)
        if k <= GROUPS + 1:
            pairs = [(0, 1), (3, 2)] if k < GROUPS else []
            out = sent.get(k)
            if k >= 2:
                t = k - 2
                pairs = pairs + [(1, 0), (2, 3)]
                operands = [place, part_of[t], across[t]] + ([out] if k < GROUPS else [])
                out = run(
                    outward_kernel,
                    chunk_b16,
                    operands,
                    every * cols,
                    specs=[SM] + [VM] * (len(operands) - 1),
                )
            given[k] = out
            along[k] = send(out, "exp", pairs)
        if k in (1, 2):
            project(k + 1)
        if 3 <= k <= GROUPS + 2:
            t = k - 3
            outs = [like((slots, wide[t])), chunk_b16]
            known = []
            if t == GROUPS - 1:
                outs.append(like((tokens, GROUPS * cols)))
                known = [mixed[n] for n in range(t)]
            x, mixed[t], *gives = run(
                functools.partial(dispatch_kernel, t),
                outs,
                [place, along[k - 1], given[k - 1], gain, picks] + known,
                2 * slots * every * wide[t],
                specs=[SM] + [VM] * (4 + len(known)),
            )
            x_got = swap(x)
            if gives:
                mixed_got = swap(gives[0])
        if 4 <= k <= GROUPS + 3:
            t = k - 4
            half = run(
                half_kernel,
                like((slots // 2, near[t].shape[1])),
                [place, near[t]],
                specs=[SM, VM],
            )
            far[t] = onward(half)
            near[t] = [near[t], swap(near[t])]
        if 3 <= k <= GROUPS + 2:
            t = k - 3
            joined[t] = run(
                functools.partial(join_kernel, cols),
                like((slots, wide[t] + cols)),
                [place, x, x_got],
                specs=[SM, VM, VM],
            )
            near[t] = outbound(joined[t])
        if 4 <= k <= GROUPS + 3:
            t = k - 4
            experts(t, ROLES[:3], [[joined[t]], [near[t][0]], [near[t][1]]])
        if 5 <= k <= GROUPS + 4:
            t = k - 5
            if t == GROUPS - 1:
                mixed_out = call(
                    mixed_kernel,
                    like((tokens, model)),
                    [place, mixed_got] + [mixed[n] for n in range(GROUPS)],
                    deps=last[:],
                    specs=[SM] + [VM] * (GROUPS + 1),
                )
            experts(t, ROLES[3:], [[far[t], swap(far[t])]])
    return (mixed_out, hidden[None])


def entering(value, axis, combine, identity):
    devices, position = (lax.axis_size(axis), lax.axis_index(axis))
    everything = jax.tree.map(lambda part: lax.all_gather(part, axis), value)
    start = jax.tree.map(
        lambda part, zero: jnp.broadcast_to(jnp.asarray(zero, part.dtype), part.shape),
        value,
        identity,
    )

    def hop(k, before):
        reached = k < position
        new = combine(before, jax.tree.map(lambda part: part[k], everything))
        return jax.tree.map(lambda a, b: jnp.where(reached, a, b), new, before)

    return lax.fori_loop(0, devices, hop, start)


def route_slots(id_rows):
    count = id_rows.shape[1]
    same = id_rows[:, :, None] == id_rows[:, None, :]
    before = lax.broadcasted_iota(jnp.int32, (count, count), 1) < lax.broadcasted_iota(
        jnp.int32, (count, count), 0
    )
    return jnp.sum((same & before[None]).astype(jnp.int32), axis=2)


def select_matrix(id_rows, slot_rows, owners, capacity):
    routes = id_rows.shape[1]
    places = jnp.arange(capacity, dtype=jnp.int32)
    hits = (id_rows[:, None, None, :] == owners[None, :, None, None]) & (
        slot_rows[:, None, None, :] == places[None, None, :, None]
    )
    to_token = (
        jnp.arange(routes, dtype=jnp.int32)[:, None] // 2
        == jnp.arange(routes // 2, dtype=jnp.int32)[None, :]
    ).astype(jnp.float32)
    return jnp.einsum("bepr,rt->bept", hits.astype(jnp.float32), to_token)


def on_any_mesh(
    queries,
    key_rows,
    value_rows,
    decay_rate,
    out_weight,
    residual,
    moe_gain,
    expert_ids,
    gate_weight,
    up_weight,
):
    highest = lax.Precision.HIGHEST
    block_len = queries.shape[0]
    heads_here = decay_rate.shape[0]
    width_here = queries.shape[1]
    head_size = width_here // heads_here
    exp_count = lax.axis_size("exp")
    tok_count = block_len // exp_count
    capacity = max(2, 3 * tok_count // exp_count)
    query_here = queries.reshape(block_len, heads_here, head_size)
    key_here = key_rows.reshape(block_len, heads_here, head_size)
    value_here = value_rows.reshape(block_len, heads_here, head_size)
    position = jnp.arange(block_len, dtype=jnp.float32)
    offset = position[:, None] - position[None, :]
    masked = jnp.where(
        (offset >= 0)[None],
        jnp.exp(-decay_rate[:, None, None] * jnp.maximum(offset, 0.0)[None]),
        0.0,
    )
    inner = jnp.exp(-decay_rate[None, :] * position[:, None])
    tail = jnp.exp(-decay_rate[None, :] * (block_len - position[:, None]))
    whole = jnp.exp(-decay_rate * block_len)
    scores = jnp.einsum("ihd,jhd->hij", query_here, key_here, preferred_element_type=jnp.float32)
    weighted = (scores * masked).astype(jnp.bfloat16)
    local_part = jnp.einsum(
        "hij,jhd->ihd", weighted, value_here, preferred_element_type=jnp.float32
    )
    fresh = jnp.einsum(
        "jhd,jhe->hde",
        key_here.astype(jnp.float32) * tail[:, :, None],
        value_here.astype(jnp.float32),
        precision=highest,
    )

    def combine(earlier, later):
        return (earlier[0] * later[0], later[0][:, None, None] * earlier[1] + later[1])

    unused, state_in = entering(
        (whole, fresh), "ctx", combine, (jnp.ones_like(whole), jnp.zeros_like(fresh))
    )
    carried = (
        jnp.einsum("ihd,hde->ihe", query_here.astype(jnp.float32), state_in, precision=highest)
        * inner[:, :, None]
    )
    attended = local_part + carried
    scale_rows = lax.rsqrt(jnp.mean(attended * attended, axis=-1, keepdims=True) + 1e-05)
    head_out = (attended * scale_rows).astype(jnp.bfloat16).reshape(block_len, width_here)
    partial_rows = jnp.dot(
        head_out,
        lax.all_gather(out_weight, "ctx", axis=1, tiled=True),
        preferred_element_type=jnp.float32,
    )
    attn = lax.psum_scatter(partial_rows, "exp", scatter_dimension=0, tiled=True)
    mixed = (residual.astype(jnp.float32) + attn).astype(jnp.bfloat16)
    mixed_f = mixed.astype(jnp.float32)
    normed = (
        mixed_f * lax.rsqrt(jnp.mean(mixed_f * mixed_f, axis=-1, keepdims=True) + 1e-05) * moe_gain
    ).astype(jnp.bfloat16)
    id_rows = expert_ids.reshape(1, 2 * tok_count)
    slot_rows = route_slots(id_rows)
    picks = select_matrix(id_rows, slot_rows, jnp.arange(exp_count, dtype=jnp.int32), capacity)[0]
    picks = picks.reshape(exp_count * capacity, tok_count).astype(jnp.bfloat16)
    buffer = jnp.dot(picks, normed, preferred_element_type=jnp.float32).astype(jnp.bfloat16)
    received = lax.all_to_all(buffer, "exp", split_axis=0, concat_axis=0, tiled=True)
    gate_here = gate_weight[0]
    up_here = up_weight[0]
    contract = (((1,), (1,)), ((), ()))
    piece = lax.all_gather(received, "ctx", axis=0, tiled=True)
    gated = lax.dot_general(gate_here, piece, contract, preferred_element_type=jnp.float32)
    lifted = lax.dot_general(up_here, piece, contract, preferred_element_type=jnp.float32)
    hidden = (jax.nn.silu(gated) * lifted).astype(jnp.bfloat16)
    return (mixed, hidden[None])


def solution(mesh):
    in_specs = (
        P("ctx", "exp"),
        P("ctx", "exp"),
        P("ctx", "exp"),
        P("exp"),
        P("exp", "ctx"),
        P(("ctx", "exp"), None),
        P(),
        P(("ctx", "exp"), None),
        P("exp", "ctx", None),
        P("exp", "ctx", None),
    )
    out_specs = (P(("ctx", "exp"), None), P("exp", "ctx", None))
    square, line = mesh.shape["ctx"] == GROUPS * CORES, mesh.shape["exp"] == 4

    def per_device(*args):
        tokens, model = args[5].shape
        fits = square and line and 2 * tokens == LANES and args[3].shape[0] % CORES == 0
        fits = fits and model % (GROUPS * CORES * LANES) == 0
        return (on_square if fits else on_any_mesh)(*args)

    return jax.shard_map(
        per_device, mesh=mesh, in_specs=in_specs, out_specs=out_specs, check_vma=False
    )
```

```python
import functools

import jax
import jax.numpy as jnp
from jax import lax
from jax.experimental import pallas as pl
from jax.experimental.pallas import tpu as pltpu
from jax.sharding import PartitionSpec as P

GROUPS = 4
CORES = 2
ORDER = (0, 2, 1, 3)
LANES = 128
BF16 = jnp.bfloat16
F32 = jnp.float32
NT = (((1,), (1,)), ((), ()))
TN = (((0,), (0,)), ((), ()))
NN = (((1,), (0,)), ((), ()))
VM = pl.BlockSpec(memory_space=pltpu.VMEM)
SM = pl.BlockSpec(memory_space=pltpu.SMEM)
HBM = pl.BlockSpec(memory_space=pltpu.HBM)
ANY = pl.BlockSpec(memory_space=pl.ANY)


def dot(a, b, dims):
    return lax.dot_general(a, b, dims, preferred_element_type=F32)


def halves(x):
    high = x.astype(BF16)
    return high, (x - high.astype(F32)).astype(BF16)


def like(shape, dtype=BF16):
    return jax.ShapeDtypeStruct(tuple(shape), dtype)


def call(kernel, out_shape, operands, flops=0, exps=0, deps=(), specs=None, limit=12, **kwargs):
    count, extra = len(operands), len(deps)

    def body(*refs):
        kernel(*refs[:count], *refs[count + extra :])

    shapes = out_shape if isinstance(out_shape, (list, tuple)) else [out_shape]
    nbytes = sum(x.size * x.dtype.itemsize for x in list(operands) + list(shapes))
    kwargs.setdefault("out_specs", jax.tree.map(lambda _: VM, out_shape))
    return pl.pallas_call(
        body,
        out_shape=out_shape,
        in_specs=list(specs or [VM] * count) + [ANY] * extra,
        compiler_params=pltpu.CompilerParams(vmem_limit_bytes=limit * 1024 * 1024),
        cost_estimate=pl.CostEstimate(
            flops=int(flops), bytes_accessed=int(nbytes), transcendentals=int(exps)
        ),
        **kwargs,
    )(*operands, *deps)


def tile(index, size):
    return pl.ds(pl.multiple_of(index * size, size), size)


def fresh_kernel(place_ref, rate_ref, k_in, v_in, mine_ref, theirs_ref, k_ref, v_ref, sems):
    part, size = mine_ref.shape[0], mine_ref.shape[1]
    length = k_ref.shape[0]
    left = length - lax.broadcasted_iota(jnp.int32, (length, size), 0).astype(F32)
    order = ((theirs_ref, 1 - place_ref[1]), (mine_ref, place_ref[1]))
    copies = []
    for n, (_, half) in enumerate(order):
        at = tile(half, part * size)
        for source, target in ((k_in, k_ref), (v_in, v_ref)):
            copies.append(
                pltpu.make_async_copy(source.at[:, at], target.at[:, at], sems.at[len(copies)])
            )
            copies[-1].start()
    for n, (out_ref, half) in enumerate(order):
        copies[2 * n].wait()
        copies[2 * n + 1].wait()
        for j in range(part):
            head = half * part + j
            cols = tile(head, size)
            tail = jnp.exp(rate_ref[head] * left)
            high, low = halves(k_ref[:, cols].astype(F32) * tail)
            v = v_ref[:, cols]
            out_ref[j] = dot(high, v, TN) + dot(low, v, TN)


def local_kernel(rate_ref, q_in, k_ref, v_ref, out_ref, q_ref, sem):
    length, size = k_ref.shape[0], rate_ref.shape[2]
    heads = k_ref.shape[1] // size
    copy = pltpu.make_async_copy(q_in, q_ref, sem)
    copy.start()
    rows = lax.broadcasted_iota(jnp.int32, (length, length), 0)
    cols = lax.broadcasted_iota(jnp.int32, (length, length), 1)
    offset = (rows - cols).astype(F32)
    keep = offset >= 0
    offset = jnp.maximum(offset, 0.0)
    copy.wait()
    for h in range(heads):
        at = slice(h * size, (h + 1) * size)
        rate = jnp.concatenate([rate_ref[h]] * (length // LANES), axis=1)
        masked = jnp.where(keep, jnp.exp(rate * offset), 0.0)
        weighted = (dot(q_ref[:, at], k_ref[:, at], NT) * masked).astype(BF16)
        out_ref[:, at] = dot(weighted, v_ref[:, at], NN)


def mix_kernel(recipe, coef_ref, *refs):
    count = 1 + max(i for terms in recipe for i, _ in terms)
    part = refs[0].shape[0]
    first = CORES * part
    for j in range(part):
        values = [refs[i][j] for i in range(count)]
        for out_ref, terms in zip(refs[count:], recipe):
            out_ref[j] = sum(values[i] * coef_ref[first + row * part + j] for i, row in terms)


def scan_rows(chip, core, rate, part, length):
    rates = lax.dynamic_slice(rate, (core * part,), (part,))

    def fade(blocks):
        return jnp.exp(-rates * (length * blocks))

    one, none = jnp.ones_like(rates), jnp.zeros_like(rates)
    first, east, south = core == 0, (chip & 1) != 0, (chip & 2) != 0
    behind = jnp.where(south, fade(2.0 * (chip & 1).astype(F32)), none)
    keep, give = jnp.where(first, one, fade(1.0)), jnp.where(first, fade(1.0), one)
    return [
        jnp.where(first, one, none),
        jnp.where(first, none, one),
        jnp.where(first, fade(1.0), one),
        jnp.where(first, one, fade(1.0)),
        jnp.where(east, one, none),
        jnp.where(east, fade(2.0), one),
        jnp.where(east, one, fade(2.0)),
        keep,
        keep * behind,
        jnp.where(first, none, one),
        give,
        give * behind,
        jnp.where(first, one, none),
    ]


def head_kernel(place_ref, rate_ref, q_ref, local_ref, keep_ref, got_ref, out_ref):
    part, size = keep_ref.shape[0], keep_ref.shape[1]
    length = q_ref.shape[0]
    pos = lax.broadcasted_iota(jnp.int32, (length, size), 0).astype(F32)
    for state_ref, half in ((keep_ref, place_ref[1]), (got_ref, 1 - place_ref[1])):
        for j in range(part):
            head = half * part + j
            at = tile(head, size)
            high, low = halves(state_ref[j])
            q = q_ref[:, at]
            carried = dot(q, high, NN) + dot(q, low, NN)
            carried = carried * jnp.exp(rate_ref[head] * pos)
            attended = local_ref[:, at] + carried
            scale = lax.rsqrt(jnp.mean(attended * attended, axis=-1, keepdims=True) + 1e-05)
            out_ref[:, at] = (attended * scale).astype(BF16)


def larger_kernel(a_ref, b_ref, out_ref):
    out_ref[...] = jnp.maximum(a_ref[...], b_ref[...])


def stack_kernel(which, place_ref, a_ref, b_ref, out_ref):
    rows = a_ref.shape[0]
    upper = (place_ref[which] >> (1 if which == 2 else 0)) & 1
    out_ref[tile(upper, rows), :] = a_ref[...]
    out_ref[tile(1 - upper, rows), :] = b_ref[...]


def picks_kernel(tokens, capacity, place_ref, own_ref, got_ref, out_ref):
    slots = out_ref.shape[0]
    before = lax.broadcasted_iota(jnp.int32, (LANES, LANES), 0)
    token = lax.broadcasted_iota(jnp.int32, (LANES, LANES), 1)
    earlier = ((before < token) & (before // tokens == token // tokens)).astype(BF16)
    lane = lax.broadcasted_iota(jnp.int32, (8, LANES), 1)
    slot = lax.broadcasted_iota(jnp.int32, (slots, LANES), 0)
    per = own_ref.shape[0] // 8
    for ref, half in ((own_ref, place_ref[1]), (got_ref, 1 - place_ref[1])):
        for n in range(per):
            first, second = ref[8 * n : 8 * n + 1, :], ref[8 * n + 1 : 8 * n + 2, :]
            named = (first == place_ref[2]) | (second == place_ref[2])
            named = jnp.broadcast_to(named.astype(F32), (8, LANES))
            rank = dot(named.astype(BF16), earlier, NN).astype(jnp.int32)
            run = half * per + n
            row = (run * (LANES // tokens) + lane // tokens) * capacity + rank
            row = jnp.where((named > 0.5) & (rank < capacity), row, -1)
            out_ref[:, tile(run, LANES)] = (slot == row[0:1, :]).astype(BF16)


def project_kernel(t, place_ref, own_ref, got_ref, rest_ref, rest_got_ref, *refs):
    weights, (sum_ref, sent_ref) = refs[:-2], refs[-2:]
    length, tokens, cols = own_ref.shape[0], rest_ref.shape[0], sum_ref.shape[1]
    depth = own_ref.shape[1] // len(weights)
    at = tile((place_ref[0] ^ t) * CORES + place_ref[1], cols)
    for head_ref, row_ref, half in (
        (own_ref, rest_ref, place_ref[1]),
        (got_ref, rest_got_ref, 1 - place_ref[1]),
    ):
        value = 0.0
        for n, weight in enumerate(weights):
            value = value + dot(head_ref[:, n * depth : (n + 1) * depth], weight[...], NN)
        pieces = []
        for z in range(length // tokens):
            piece = value[z * tokens : (z + 1) * tokens, :]
            pieces.append(
                jnp.where(place_ref[2] == z, piece + row_ref[:, at].astype(F32), piece)
            )
        value = jnp.concatenate(pieces, axis=0)
        sum_ref[tile(half, length), :] = value
        sent_ref[tile(half, length), :] = value.astype(BF16)


def inward_kernel(part_ref, got_ref, sum_ref, sent_ref):
    total = part_ref[...] + got_ref[...].astype(F32)
    sum_ref[...] = total
    sent_ref[...] = total.astype(BF16)


def outer(place_ref):
    return (place_ref[2] == 0) | (place_ref[2] == 3)


def total_kernel(part_ref, got_ref, out_ref):
    out_ref[...] = (part_ref[...] + got_ref[...].astype(F32)).astype(BF16)


def dispatch_kernel(t, final, place_ref, got_ref, given_ref, gain_ref, picks_ref, *refs):
    earlier, (out_ref, mixed_ref), gives = refs[:-2], refs[-2:], []
    if final:
        earlier, (out_ref, mixed_ref, give_ref) = refs[:-3], refs[-3:]
        gives = [give_ref]
    cols = mixed_ref.shape[1]
    mixed = jnp.where(outer(place_ref), got_ref[...], given_ref[...])
    mixed_ref[...] = mixed
    value = mixed.astype(F32)
    gain = gain_ref[:, tile((place_ref[0] ^ t) * CORES + place_ref[1], cols)]
    out_ref[:, :cols] = dot(picks_ref[...], (value * gain).astype(BF16), NN).astype(BF16)
    if not gives:
        return
    squares = jnp.sum(value * value, axis=1, keepdims=True)
    for ref in earlier:
        value = ref[...].astype(F32)
        squares = squares + jnp.sum(value * value, axis=1, keepdims=True)
    extra = dot(picks_ref[...], in_three(squares), NN)
    out_ref[:, cols:] = extra.astype(BF16)
    tokens = give_ref.shape[0]
    per = mixed_ref.shape[0] // CORES // tokens
    rows = tile((1 - place_ref[1]) * per + place_ref[2], tokens)
    for n, ref in enumerate(list(earlier) + [mixed_ref]):
        give_ref[:, n * cols : (n + 1) * cols] = ref[rows, :]


def in_three(column):
    lane = lax.broadcasted_iota(jnp.int32, (column.shape[0], LANES), 1)
    rest, out = column, jnp.zeros((column.shape[0], LANES), F32)
    for place in range(3):
        high = rest.astype(BF16).astype(F32)
        out = jnp.where(lane == place, high, out)
        rest = rest - high
    return out.astype(BF16)


def join_kernel(cols, place_ref, own_ref, got_ref, out_ref):
    out_ref[:, tile(place_ref[1], cols)] = own_ref[:, :cols]
    out_ref[:, tile(1 - place_ref[1], cols)] = got_ref[:, :cols]
    if own_ref.shape[1] > cols:
        extra = own_ref[:, cols:].astype(F32) + got_ref[:, cols:].astype(F32)
        total = jnp.sum(extra, axis=1, keepdims=True)
        out_ref[:, CORES * cols :] = in_three(total)


def half_kernel(place_ref, in_ref, out_ref, all_ref):
    out_ref[...] = in_ref[tile(place_ref[1], out_ref.shape[0]), :]
    all_ref[...] = in_ref[...]


def copy_kernel(in_ref, out_ref):
    out_ref[...] = in_ref[...]


def rows_kernel(start, in_ref, out_ref):
    out_ref[...] = in_ref[start : start + out_ref.shape[0], :]


def mixed_kernel(place_ref, got_ref, *refs):
    mixed, out_ref = refs[:-1], refs[-1]
    tokens, cols = out_ref.shape[0], mixed[0].shape[1]
    per = mixed[0].shape[0] // CORES // tokens
    own = tile(place_ref[1] * per + place_ref[2], tokens)
    for t, ref in zip(ORDER, mixed):
        block = (place_ref[0] ^ t) * CORES
        n = ORDER.index(t)
        out_ref[:, tile(block + place_ref[1], cols)] = ref[own, :]
        out_ref[:, tile(block + 1 - place_ref[1], cols)] = got_ref[:, n * cols : (n + 1) * cols]


ROLES = ("own", "mine", "other", "diagonal")


def expert_kernel(t, roles, mode, has_sums, place_ref, gate_ref, up_ref, *refs):
    refs = list(refs)
    pieces = [[refs.pop(0) for _ in range(2 if r == "diagonal" else 1)] for r in roles]
    sums = [[refs.pop(0), refs.pop(0)] for _ in roles] if has_sums else None
    if mode == "next":
        refs.pop(0)
    model = gate_ref.shape[1]
    width = model // GROUPS
    away = {"own": 0, "mine": 1 + place_ref[1], "other": 2 - place_ref[1], "diagonal": 3}
    if mode is None:
        outs = refs[: 2 * len(roles)]
        held = refs[2 * len(roles) :]
    else:
        outs, mark_ref, ready, sems = refs[:4]
        held = refs[4:]
        mark_ref[...] = jnp.zeros_like(mark_ref)
    copies = []
    for n, role in enumerate(roles):
        source = place_ref[0] ^ away[role]
        ref = pieces[n][0]
        if role == "diagonal":
            rows = ref.shape[0]
            held[0][tile(place_ref[1], rows), :] = ref[...]
            held[0][tile(1 - place_ref[1], rows), :] = pieces[n][1][...]
            ref = held[0]
        x = ref[:, :width]
        cols = tile(source ^ t, width)
        gated = dot(gate_ref[:, cols], x, NT)
        lifted = dot(up_ref[:, cols], x, NT)
        if sums is not None:
            gated = gated + sums[n][0][...]
            lifted = lifted + sums[n][1][...]
        if mode is None:
            outs[2 * n][...] = gated
            outs[2 * n + 1][...] = lifted
            continue
        lane = lax.broadcasted_iota(jnp.int32, (8, LANES), 1)
        squares = dot((lane < 3).astype(BF16), ref[:, width:], NT)[0:1, :]
        scale = lax.rsqrt(squares / model + 1e-05)
        gated, lifted = gated * scale, lifted * scale
        silu = (0.5 * gated) * (1.0 + jnp.tanh(0.5 * gated))
        ready[n] = (silu * lifted).astype(BF16)
        at = tile(source, ready.shape[2])
        rows = ready.shape[1] // 4
        for q in range(4):
            cut = slice(q * rows, (q + 1) * rows)
            copies.append(
                pltpu.make_async_copy(
                    ready.at[n, cut], outs.at[cut, at], sems.at[4 * n + q]
                )
            )
            copies[-1].start()
    for copy in copies:
        copy.wait()


def expert_step(place, t, final, roles, pieces, gate, up, sums, hidden, deps):
    hid, model = gate.shape
    width = model // GROUPS
    slots = sum(x.shape[0] for x in pieces[0])
    operands = [place, gate, up] + [x for per in pieces for x in per]
    has_sums = roles[0] in sums
    if has_sums:
        operands += [x for r in roles for x in sums[r]]
    specs = [SM] + [VM] * (len(operands) - 1)
    kwargs, mode, scratch = {}, None, []
    if final:
        mode = "first" if hidden is None else "next"
        if hidden is not None:
            kwargs["input_output_aliases"] = {len(operands): 0}
            operands.append(hidden)
            specs.append(ANY)
        out_shape = [like((hid, slots * GROUPS)), like((8, LANES), F32)]
        kwargs["out_specs"] = [ANY, VM]
        scratch += [
            pltpu.VMEM((len(roles), hid, slots), BF16),
            pltpu.SemaphoreType.DMA((4 * len(roles),)),
        ]
    else:
        out_shape = [like((hid, slots), F32)] * (2 * len(roles))
    if "diagonal" in roles:
        wide = pieces[roles.index("diagonal")][0].shape[1]
        scratch.append(pltpu.VMEM((slots, wide), BF16))
    out = call(
        functools.partial(expert_kernel, t, roles, mode, has_sums),
        out_shape,
        operands,
        4 * hid * slots * width * len(roles),
        hid * slots * len(roles) if mode else 0,
        deps,
        specs,
        20,
        scratch_shapes=scratch,
        **kwargs,
    )
    if mode:
        return out
    for n, r in enumerate(roles):
        sums[r] = out[2 * n : 2 * n + 2]
    return hidden, out[0]


def send(x, axis, pairs):
    return lax.ppermute(x, axis, pairs)


def swap(x):
    return send(x, "ctx", [(d, d ^ 1) for d in range(lax.axis_size("ctx"))])


def outbound(x):
    return send(x, "ctx", [(d, d ^ (4 if d % 2 else 2)) for d in range(lax.axis_size("ctx"))])


def onward(x):
    return send(x, "ctx", [(d, d ^ (2 if d % 2 else 4)) for d in range(lax.axis_size("ctx"))])


def on_square(
    queries,
    key_rows,
    value_rows,
    decay_rate,
    out_weight,
    residual,
    moe_gain,
    expert_ids,
    gate_weight,
    up_weight,
):
    ctx, exp = lax.axis_index("ctx"), lax.axis_index("exp")
    chip, core = ctx // CORES, lax.rem(ctx, CORES)
    place = jnp.stack([chip, core, exp]).astype(jnp.int32)
    length, here = queries.shape
    heads = decay_rate.shape[0]
    size = here // heads
    part = heads // CORES
    tokens, model = residual.shape
    cols = model // GROUPS // CORES
    capacity = max(2, 3 * tokens // lax.axis_size("exp"))
    every = CORES * length
    slots = every // tokens * capacity
    gate, up = gate_weight[0], up_weight[0]
    last = []

    def run(kernel, out_shape, operands, *more, deps=(), **kwargs):
        out = call(kernel, out_shape, operands, *more, deps=list(last) + list(deps), **kwargs)
        last[:] = [out[0] if isinstance(out, (list, tuple)) else out]
        return out

    rows = jnp.stack(scan_rows(chip, core, decay_rate, part, length)).reshape(-1)
    rows = jnp.concatenate([-decay_rate, rows])
    table = jnp.broadcast_to(rows[:, None, None], (rows.shape[0], 1, LANES))
    ids = jnp.concatenate([expert_ids.T, expert_ids.T], axis=1)
    lane = jnp.arange(LANES, dtype=jnp.int32)[None, :]
    ids = jnp.where(lane // tokens == exp % (LANES // tokens), ids, -1)
    ids = jnp.pad(ids, ((0, 6), (0, 0)), constant_values=-1)
    gain = moe_gain[None, :]
    weight_y = send(out_weight, "ctx", [(d, d ^ 4) for d in range(8)])

    state_like = like((part, size, size), F32)
    mine, theirs, keys, values = run(
        fresh_kernel,
        [state_like] * 2 + [like((length, here))] * 2,
        [place, table, key_rows, value_rows],
        4 * heads * length * size * size,
        heads * length * size,
        deps=[ids],
        specs=[SM, VM, HBM, HBM],
        scratch_shapes=[pltpu.SemaphoreType.DMA((4,))],
    )

    def mix(recipe, operands, deps=()):
        return run(
            functools.partial(mix_kernel, recipe),
            [state_like] * len(recipe),
            [table] + operands,
            deps=deps,
        )

    def copy(x):
        return run(copy_kernel, like(x.shape, x.dtype), [x])

    def cut(x, start):
        return run(
            functools.partial(rows_kernel, start), like((x.shape[0] // 2, x.shape[1])), [x]
        )

    got = swap(theirs)
    first, total = mix([[(0, 0), (1, 1)], [(0, 2), (1, 3)]], [mine, got])
    got = send(total, "ctx", [(d, d ^ 2) for d in range(8)])
    ids_got = send(ids, "exp", [(d, d ^ 1) for d in range(4)])
    rest_got = swap(residual)
    local, queries_here = run(
        local_kernel,
        [like((length, here), F32), like((length, here))],
        [table, queries, keys, values],
        4 * heads * length * length * size,
        heads * length * length,
        specs=[VM, HBM, VM, VM],
        scratch_shapes=[pltpu.SemaphoreType.DMA(())],
    )
    ids = run(larger_kernel, like(ids.shape, ids.dtype), [ids, ids_got])
    state, total = mix([[(0, 4)], [(0, 5), (1, 6)]], [got, total], [rest_got])
    got = send(total, "ctx", [(d, d + 4) for d in range(4)])
    weight_x = send(copy(out_weight), "ctx", [(d, d ^ 2) for d in range(8)])
    ids_got = send(ids, "exp", [(d, d ^ 2) for d in range(4)])
    ids = run(
        functools.partial(stack_kernel, 2),
        like((16, LANES), ids.dtype),
        [place, ids, ids_got],
        deps=[weight_y],
        specs=[SM, VM, VM],
    )
    keep, give = mix(
        [[(0, 7), (1, 8), (2, 9)], [(0, 10), (1, 11), (2, 12)]], [state, got, first]
    )
    got = swap(give)
    ids_got = swap(ids)
    head_out = run(
        head_kernel,
        like((length, here)),
        [place, table, queries_here, local, keep, got],
        4 * heads * length * size * size,
        heads * length * size,
        specs=[SM] + [VM] * 5,
    )
    heads_got = swap(head_out)
    picks = run(
        functools.partial(picks_kernel, tokens, capacity),
        like((slots, every)),
        [place, ids, ids_got],
        specs=[SM, VM, VM],
    )

    chunk_f32, chunk_b16 = like((every, cols), F32), like((every, cols))
    end = GROUPS - 1
    wide = [cols + LANES * (n == end) for n in range(GROUPS)]
    weights = [[out_weight], [weight_y], [weight_x], None]
    parts, totals, mixed, joined = [None] * 4, [None] * 4, [None] * 4, [None] * 4
    moved = {}
    sums, hidden = {}, None

    def project(n):
        parts[n], sent = run(
            functools.partial(project_kernel, ORDER[n]),
            [chunk_f32, chunk_b16],
            [place, head_out, heads_got, residual, rest_got] + weights[n],
            2 * every * here * cols,
            specs=[SM] + [VM] * (4 + len(weights[n])),
        )
        moved["in", n] = send(sent, "exp", [(0, 1), (3, 2)])

    def inward(n):
        parts[n], sent = run(
            inward_kernel, [chunk_f32, chunk_b16], [parts[n], moved["in", n]], every * cols
        )
        moved["across", n] = send(sent, "exp", [(1, 2), (2, 1)])

    def outward(n):
        totals[n] = run(total_kernel, chunk_b16, [parts[n], moved["across", n]], every * cols)
        moved["out", n] = send(totals[n], "exp", [(1, 0), (2, 3)])

    def dispatch(n):
        outs = [like((slots, wide[n])), chunk_b16]
        known = []
        if n == end:
            outs.append(like((tokens, GROUPS * cols)))
            known = mixed[:n]
        x, mixed[n], *gives = run(
            functools.partial(dispatch_kernel, ORDER[n], n == end),
            outs,
            [place, moved["out", n], totals[n], gain, picks] + known,
            2 * slots * every * wide[n],
            specs=[SM] + [VM] * (4 + len(known)),
        )
        moved["x", n] = (x, swap(x))
        if gives:
            moved["mixed"] = swap(gives[0])

    def join(n):
        joined[n] = run(
            functools.partial(join_kernel, cols),
            like((slots, wide[n] + cols)),
            [place, *moved["x", n]],
            specs=[SM, VM, VM],
        )
        moved["near", n] = outbound(joined[n])

    def half(n):
        near = moved["near", n]
        out, copied = run(
            half_kernel,
            [like((slots // 2, near.shape[1])), like(near.shape)],
            [place, near],
            specs=[SM, VM],
        )
        moved["far", n] = onward(out)
        moved["other", n] = swap(copied)

    def diagonal(n):
        moved["far", n] = copy(moved["far", n])
        moved["rest", n] = swap(moved["far", n])

    def experts(n, roles, pieces):
        nonlocal hidden
        hidden, mark = expert_step(
            place, ORDER[n], n == end, roles, pieces, gate, up, sums, hidden, last[:]
        )
        last[:] = [mark]

    def nearer(n):
        experts(n, ROLES[:3], [[joined[n]], [moved["near", n]], [moved["other", n]]])

    def farther(n):
        experts(n, ROLES[3:], [[moved["far", n], moved["rest", n]]])

    project(0)
    project(1)
    project(2)
    weight_top = send(cut(weight_x, 0), "ctx", [(d, d ^ 4) for d in range(8)])
    weight_bottom = send(cut(weight_y, here // 2), "ctx", [(d, d ^ 2) for d in range(8)])
    weights[3] = [weight_top, weight_bottom]
    for work, n in (
        (inward, 0), (inward, 1), (project, 3), (outward, 0), (inward, 2), (outward, 1),
        (dispatch, 0), (inward, 3), (join, 0), (outward, 2), (dispatch, 1), (join, 1),
        (outward, 3), (half, 0), (dispatch, 2), (nearer, 0), (join, 2), (half, 1),
        (diagonal, 0), (farther, 0), (dispatch, 3), (nearer, 1), (join, 3), (half, 2),
        (diagonal, 1), (farther, 1), (nearer, 2), (half, 3), (diagonal, 2), (farther, 2),
        (nearer, 3),
    ):
        work(n)
    mixed_out = call(
        mixed_kernel,
        like((tokens, model)),
        [place, moved["mixed"]] + mixed,
        deps=last[:],
        specs=[SM] + [VM] * (GROUPS + 1),
    )
    diagonal(3)
    farther(3)
    return (mixed_out, hidden[None])


def entering(value, axis, combine, identity):
    devices, position = (lax.axis_size(axis), lax.axis_index(axis))
    everything = jax.tree.map(lambda part: lax.all_gather(part, axis), value)
    start = jax.tree.map(
        lambda part, zero: jnp.broadcast_to(jnp.asarray(zero, part.dtype), part.shape),
        value,
        identity,
    )

    def hop(k, before):
        reached = k < position
        new = combine(before, jax.tree.map(lambda part: part[k], everything))
        return jax.tree.map(lambda a, b: jnp.where(reached, a, b), new, before)

    return lax.fori_loop(0, devices, hop, start)


def route_slots(id_rows):
    count = id_rows.shape[1]
    same = id_rows[:, :, None] == id_rows[:, None, :]
    before = lax.broadcasted_iota(jnp.int32, (count, count), 1) < lax.broadcasted_iota(
        jnp.int32, (count, count), 0
    )
    return jnp.sum((same & before[None]).astype(jnp.int32), axis=2)


def select_matrix(id_rows, slot_rows, owners, capacity):
    routes = id_rows.shape[1]
    places = jnp.arange(capacity, dtype=jnp.int32)
    hits = (id_rows[:, None, None, :] == owners[None, :, None, None]) & (
        slot_rows[:, None, None, :] == places[None, None, :, None]
    )
    to_token = (
        jnp.arange(routes, dtype=jnp.int32)[:, None] // 2
        == jnp.arange(routes // 2, dtype=jnp.int32)[None, :]
    ).astype(jnp.float32)
    return jnp.einsum("bepr,rt->bept", hits.astype(jnp.float32), to_token)


def on_any_mesh(
    queries,
    key_rows,
    value_rows,
    decay_rate,
    out_weight,
    residual,
    moe_gain,
    expert_ids,
    gate_weight,
    up_weight,
):
    highest = lax.Precision.HIGHEST
    block_len = queries.shape[0]
    heads_here = decay_rate.shape[0]
    width_here = queries.shape[1]
    head_size = width_here // heads_here
    exp_count = lax.axis_size("exp")
    tok_count = block_len // exp_count
    capacity = max(2, 3 * tok_count // exp_count)
    query_here = queries.reshape(block_len, heads_here, head_size)
    key_here = key_rows.reshape(block_len, heads_here, head_size)
    value_here = value_rows.reshape(block_len, heads_here, head_size)
    position = jnp.arange(block_len, dtype=jnp.float32)
    offset = position[:, None] - position[None, :]
    masked = jnp.where(
        (offset >= 0)[None],
        jnp.exp(-decay_rate[:, None, None] * jnp.maximum(offset, 0.0)[None]),
        0.0,
    )
    inner = jnp.exp(-decay_rate[None, :] * position[:, None])
    tail = jnp.exp(-decay_rate[None, :] * (block_len - position[:, None]))
    whole = jnp.exp(-decay_rate * block_len)
    scores = jnp.einsum("ihd,jhd->hij", query_here, key_here, preferred_element_type=jnp.float32)
    weighted = (scores * masked).astype(jnp.bfloat16)
    local_part = jnp.einsum(
        "hij,jhd->ihd", weighted, value_here, preferred_element_type=jnp.float32
    )
    fresh = jnp.einsum(
        "jhd,jhe->hde",
        key_here.astype(jnp.float32) * tail[:, :, None],
        value_here.astype(jnp.float32),
        precision=highest,
    )

    def combine(earlier, later):
        return (earlier[0] * later[0], later[0][:, None, None] * earlier[1] + later[1])

    unused, state_in = entering(
        (whole, fresh), "ctx", combine, (jnp.ones_like(whole), jnp.zeros_like(fresh))
    )
    carried = (
        jnp.einsum("ihd,hde->ihe", query_here.astype(jnp.float32), state_in, precision=highest)
        * inner[:, :, None]
    )
    attended = local_part + carried
    scale_rows = lax.rsqrt(jnp.mean(attended * attended, axis=-1, keepdims=True) + 1e-05)
    head_out = (attended * scale_rows).astype(jnp.bfloat16).reshape(block_len, width_here)
    partial_rows = jnp.dot(
        head_out,
        lax.all_gather(out_weight, "ctx", axis=1, tiled=True),
        preferred_element_type=jnp.float32,
    )
    attn = lax.psum_scatter(partial_rows, "exp", scatter_dimension=0, tiled=True)
    mixed = (residual.astype(jnp.float32) + attn).astype(jnp.bfloat16)
    mixed_f = mixed.astype(jnp.float32)
    normed = (
        mixed_f * lax.rsqrt(jnp.mean(mixed_f * mixed_f, axis=-1, keepdims=True) + 1e-05) * moe_gain
    ).astype(jnp.bfloat16)
    id_rows = expert_ids.reshape(1, 2 * tok_count)
    slot_rows = route_slots(id_rows)
    picks = select_matrix(id_rows, slot_rows, jnp.arange(exp_count, dtype=jnp.int32), capacity)[0]
    picks = picks.reshape(exp_count * capacity, tok_count).astype(jnp.bfloat16)
    buffer = jnp.dot(picks, normed, preferred_element_type=jnp.float32).astype(jnp.bfloat16)
    received = lax.all_to_all(buffer, "exp", split_axis=0, concat_axis=0, tiled=True)
    gate_here = gate_weight[0]
    up_here = up_weight[0]
    contract = (((1,), (1,)), ((), ()))
    piece = lax.all_gather(received, "ctx", axis=0, tiled=True)
    gated = lax.dot_general(gate_here, piece, contract, preferred_element_type=jnp.float32)
    lifted = lax.dot_general(up_here, piece, contract, preferred_element_type=jnp.float32)
    hidden = (jax.nn.silu(gated) * lifted).astype(jnp.bfloat16)
    return (mixed, hidden[None])


def solution(mesh):
    in_specs = (
        P("ctx", "exp"),
        P("ctx", "exp"),
        P("ctx", "exp"),
        P("exp"),
        P("exp", "ctx"),
        P(("ctx", "exp"), None),
        P(),
        P(("ctx", "exp"), None),
        P("exp", "ctx", None),
        P("exp", "ctx", None),
    )
    out_specs = (P(("ctx", "exp"), None), P("exp", "ctx", None))
    square, line = mesh.shape["ctx"] == GROUPS * CORES, mesh.shape["exp"] == 4

    def per_device(*args):
        tokens, model = args[5].shape
        fits = square and line and 2 * tokens == LANES and args[3].shape[0] % CORES == 0
        fits = fits and model % (GROUPS * CORES * LANES) == 0
        return (on_square if fits else on_any_mesh)(*args)

    return jax.shard_map(
        per_device, mesh=mesh, in_specs=in_specs, out_specs=out_specs, check_vma=False
    )
```

```python
import functools

import jax
import jax.numpy as jnp
from jax import lax
from jax.experimental import pallas as pl
from jax.experimental.pallas import tpu as pltpu
from jax.sharding import PartitionSpec as P

GROUPS = 4
CORES = 2
ORDER = (0, 2, 1, 3)
LANES = 128
BF16 = jnp.bfloat16
F32 = jnp.float32
NT = (((1,), (1,)), ((), ()))
TN = (((0,), (0,)), ((), ()))
NN = (((1,), (0,)), ((), ()))
VM = pl.BlockSpec(memory_space=pltpu.VMEM)
SM = pl.BlockSpec(memory_space=pltpu.SMEM)
HBM = pl.BlockSpec(memory_space=pltpu.HBM)
ANY = pl.BlockSpec(memory_space=pl.ANY)


def dot(a, b, dims):
    return lax.dot_general(a, b, dims, preferred_element_type=F32)


def halves(x):
    high = x.astype(BF16)
    return high, (x - high.astype(F32)).astype(BF16)


def like(shape, dtype=BF16):
    return jax.ShapeDtypeStruct(tuple(shape), dtype)


def call(kernel, out_shape, operands, flops=0, exps=0, deps=(), specs=None, limit=12, **kwargs):
    count, extra = len(operands), len(deps)

    def body(*refs):
        kernel(*refs[:count], *refs[count + extra :])

    kwargs.setdefault("out_specs", jax.tree.map(lambda _: VM, out_shape))
    return pl.pallas_call(
        body,
        out_shape=out_shape,
        in_specs=list(specs or [VM] * count) + [ANY] * extra,
        compiler_params=pltpu.CompilerParams(vmem_limit_bytes=limit * 1024 * 1024),
        cost_estimate=pl.CostEstimate(flops=1, bytes_accessed=1, transcendentals=0),
        **kwargs,
    )(*operands, *deps)


def tile(index, size):
    return pl.ds(pl.multiple_of(index * size, size), size)


def fresh_kernel(place_ref, rate_ref, k_in, v_in, mine_ref, theirs_ref, k_ref, v_ref, sems):
    part, size = mine_ref.shape[0], mine_ref.shape[1]
    length = k_ref.shape[0]
    left = length - lax.broadcasted_iota(jnp.int32, (length, size), 0).astype(F32)
    order = ((theirs_ref, 1 - place_ref[1]), (mine_ref, place_ref[1]))
    copies = []
    for n, (_, half) in enumerate(order):
        at = tile(half, part * size)
        for source, target in ((k_in, k_ref), (v_in, v_ref)):
            copies.append(
                pltpu.make_async_copy(source.at[:, at], target.at[:, at], sems.at[len(copies)])
            )
            copies[-1].start()
    for n, (out_ref, half) in enumerate(order):
        copies[2 * n].wait()
        copies[2 * n + 1].wait()
        for j in range(part):
            head = half * part + j
            cols = tile(head, size)
            tail = jnp.exp(rate_ref[head] * left)
            high, low = halves(k_ref[:, cols].astype(F32) * tail)
            v = v_ref[:, cols]
            out_ref[j] = dot(high, v, TN) + dot(low, v, TN)


def local_kernel(rate_ref, q_in, k_ref, v_ref, out_ref, q_ref, sem):
    length, size = k_ref.shape[0], rate_ref.shape[2]
    heads = k_ref.shape[1] // size
    copy = pltpu.make_async_copy(q_in, q_ref, sem)
    copy.start()
    rows = lax.broadcasted_iota(jnp.int32, (length, length), 0)
    cols = lax.broadcasted_iota(jnp.int32, (length, length), 1)
    offset = (rows - cols).astype(F32)
    keep = offset >= 0
    offset = jnp.maximum(offset, 0.0)
    copy.wait()
    for h in range(heads):
        at = slice(h * size, (h + 1) * size)
        rate = jnp.concatenate([rate_ref[h]] * (length // LANES), axis=1)
        masked = jnp.where(keep, jnp.exp(rate * offset), 0.0)
        weighted = (dot(q_ref[:, at], k_ref[:, at], NT) * masked).astype(BF16)
        out_ref[:, at] = dot(weighted, v_ref[:, at], NN)


def mix_kernel(recipe, coef_ref, *refs):
    count = 1 + max(i for terms in recipe for i, _ in terms)
    part = refs[0].shape[0]
    first = CORES * part
    for j in range(part):
        values = [refs[i][j] for i in range(count)]
        for out_ref, terms in zip(refs[count:], recipe):
            out_ref[j] = sum(values[i] * coef_ref[first + row * part + j] for i, row in terms)


def scan_rows(chip, core, rate, part, length):
    rates = lax.dynamic_slice(rate, (core * part,), (part,))

    def fade(blocks):
        return jnp.exp(-rates * (length * blocks))

    one, none = jnp.ones_like(rates), jnp.zeros_like(rates)
    first, east, south = core == 0, (chip & 1) != 0, (chip & 2) != 0
    behind = jnp.where(south, fade(2.0 * (chip & 1).astype(F32)), none)
    keep, give = jnp.where(first, one, fade(1.0)), jnp.where(first, fade(1.0), one)
    return [
        jnp.where(first, one, none),
        jnp.where(first, none, one),
        jnp.where(first, fade(1.0), one),
        jnp.where(first, one, fade(1.0)),
        jnp.where(east, one, none),
        jnp.where(east, fade(2.0), one),
        jnp.where(east, one, fade(2.0)),
        keep,
        keep * behind,
        jnp.where(first, none, one),
        give,
        give * behind,
        jnp.where(first, one, none),
    ]


def head_kernel(place_ref, rate_ref, q_ref, local_ref, keep_ref, got_ref, out_ref):
    part, size = keep_ref.shape[0], keep_ref.shape[1]
    length = q_ref.shape[0]
    pos = lax.broadcasted_iota(jnp.int32, (length, size), 0).astype(F32)
    for state_ref, half in ((keep_ref, place_ref[1]), (got_ref, 1 - place_ref[1])):
        for j in range(part):
            head = half * part + j
            at = tile(head, size)
            high, low = halves(state_ref[j])
            q = q_ref[:, at]
            carried = dot(q, high, NN) + dot(q, low, NN)
            carried = carried * jnp.exp(rate_ref[head] * pos)
            attended = local_ref[:, at] + carried
            scale = lax.rsqrt(jnp.mean(attended * attended, axis=-1, keepdims=True) + 1e-05)
            out_ref[:, at] = (attended * scale).astype(BF16)


def larger_kernel(a_ref, b_ref, out_ref):
    out_ref[...] = jnp.maximum(a_ref[...], b_ref[...])


def stack_kernel(which, place_ref, a_ref, b_ref, out_ref):
    rows = a_ref.shape[0]
    upper = (place_ref[which] >> (1 if which == 2 else 0)) & 1
    out_ref[tile(upper, rows), :] = a_ref[...]
    out_ref[tile(1 - upper, rows), :] = b_ref[...]


def picks_kernel(tokens, capacity, place_ref, own_ref, got_ref, out_ref):
    slots = out_ref.shape[0]
    before = lax.broadcasted_iota(jnp.int32, (LANES, LANES), 0)
    token = lax.broadcasted_iota(jnp.int32, (LANES, LANES), 1)
    earlier = ((before < token) & (before // tokens == token // tokens)).astype(BF16)
    lane = lax.broadcasted_iota(jnp.int32, (8, LANES), 1)
    slot = lax.broadcasted_iota(jnp.int32, (slots, LANES), 0)
    per = own_ref.shape[0] // 8
    for ref, half in ((own_ref, place_ref[1]), (got_ref, 1 - place_ref[1])):
        for n in range(per):
            first, second = ref[8 * n : 8 * n + 1, :], ref[8 * n + 1 : 8 * n + 2, :]
            named = (first == place_ref[2]) | (second == place_ref[2])
            named = jnp.broadcast_to(named.astype(F32), (8, LANES))
            rank = dot(named.astype(BF16), earlier, NN).astype(jnp.int32)
            run = half * per + n
            row = (run * (LANES // tokens) + lane // tokens) * capacity + rank
            row = jnp.where((named > 0.5) & (rank < capacity), row, -1)
            out_ref[:, tile(run, LANES)] = (slot == row[0:1, :]).astype(BF16)


def project_kernel(t, place_ref, own_ref, got_ref, rest_ref, rest_got_ref, *refs):
    weights, (sum_ref, sent_ref) = refs[:-2], refs[-2:]
    length, tokens, cols = own_ref.shape[0], rest_ref.shape[0], sum_ref.shape[1]
    depth = own_ref.shape[1] // len(weights)
    at = tile((place_ref[0] ^ t) * CORES + place_ref[1], cols)
    for head_ref, row_ref, half in (
        (own_ref, rest_ref, place_ref[1]),
        (got_ref, rest_got_ref, 1 - place_ref[1]),
    ):
        value = 0.0
        for n, weight in enumerate(weights):
            value = value + dot(head_ref[:, n * depth : (n + 1) * depth], weight[...], NN)
        pieces = []
        for z in range(length // tokens):
            piece = value[z * tokens : (z + 1) * tokens, :]
            pieces.append(
                jnp.where(place_ref[2] == z, piece + row_ref[:, at].astype(F32), piece)
            )
        value = jnp.concatenate(pieces, axis=0)
        sum_ref[tile(half, length), :] = value
        sent_ref[tile(half, length), :] = value.astype(BF16)


def inward_kernel(part_ref, got_ref, sum_ref, sent_ref):
    total = part_ref[...] + got_ref[...].astype(F32)
    sum_ref[...] = total
    sent_ref[...] = total.astype(BF16)


def outer(place_ref):
    return (place_ref[2] == 0) | (place_ref[2] == 3)


def total_kernel(part_ref, got_ref, out_ref):
    out_ref[...] = (part_ref[...] + got_ref[...].astype(F32)).astype(BF16)


def dispatch_kernel(t, final, place_ref, got_ref, given_ref, gain_ref, picks_ref, *refs):
    earlier, (out_ref, mixed_ref), gives = refs[:-2], refs[-2:], []
    if final:
        earlier, (out_ref, mixed_ref, give_ref) = refs[:-3], refs[-3:]
        gives = [give_ref]
    cols = mixed_ref.shape[1]
    mixed = jnp.where(outer(place_ref), got_ref[...], given_ref[...])
    mixed_ref[...] = mixed
    value = mixed.astype(F32)
    gain = gain_ref[:, tile((place_ref[0] ^ t) * CORES + place_ref[1], cols)]
    out_ref[:, :cols] = dot(picks_ref[...], (value * gain).astype(BF16), NN).astype(BF16)
    if not gives:
        return
    squares = jnp.sum(value * value, axis=1, keepdims=True)
    for ref in earlier:
        value = ref[...].astype(F32)
        squares = squares + jnp.sum(value * value, axis=1, keepdims=True)
    extra = dot(picks_ref[...], in_three(squares), NN)
    out_ref[:, cols:] = extra.astype(BF16)
    tokens = give_ref.shape[0]
    per = mixed_ref.shape[0] // CORES // tokens
    rows = tile((1 - place_ref[1]) * per + place_ref[2], tokens)
    for n, ref in enumerate(list(earlier) + [mixed_ref]):
        give_ref[:, n * cols : (n + 1) * cols] = ref[rows, :]


def in_three(column):
    lane = lax.broadcasted_iota(jnp.int32, (column.shape[0], LANES), 1)
    rest, out = column, jnp.zeros((column.shape[0], LANES), F32)
    for place in range(3):
        high = rest.astype(BF16).astype(F32)
        out = jnp.where(lane == place, high, out)
        rest = rest - high
    return out.astype(BF16)


def join_kernel(cols, place_ref, own_ref, got_ref, out_ref):
    out_ref[:, tile(place_ref[1], cols)] = own_ref[:, :cols]
    out_ref[:, tile(1 - place_ref[1], cols)] = got_ref[:, :cols]
    if own_ref.shape[1] > cols:
        extra = own_ref[:, cols:].astype(F32) + got_ref[:, cols:].astype(F32)
        total = jnp.sum(extra, axis=1, keepdims=True)
        out_ref[:, CORES * cols :] = in_three(total)


def half_kernel(place_ref, in_ref, out_ref, all_ref):
    out_ref[...] = in_ref[tile(place_ref[1], out_ref.shape[0]), :]
    all_ref[...] = in_ref[...]


def copy_kernel(in_ref, out_ref):
    out_ref[...] = in_ref[...]


def rows_kernel(start, in_ref, out_ref):
    out_ref[...] = in_ref[start : start + out_ref.shape[0], :]


def mixed_kernel(place_ref, got_ref, *refs):
    mixed, out_ref = refs[:-1], refs[-1]
    tokens, cols = out_ref.shape[0], mixed[0].shape[1]
    per = mixed[0].shape[0] // CORES // tokens
    own = tile(place_ref[1] * per + place_ref[2], tokens)
    for t, ref in zip(ORDER, mixed):
        block = (place_ref[0] ^ t) * CORES
        n = ORDER.index(t)
        out_ref[:, tile(block + place_ref[1], cols)] = ref[own, :]
        out_ref[:, tile(block + 1 - place_ref[1], cols)] = got_ref[:, n * cols : (n + 1) * cols]


ROLES = ("own", "mine", "other", "diagonal")


def expert_kernel(t, roles, mode, has_sums, place_ref, gate_ref, up_ref, *refs):
    refs = list(refs)
    pieces = [[refs.pop(0) for _ in range(2 if r == "diagonal" else 1)] for r in roles]
    sums = [[refs.pop(0), refs.pop(0)] for _ in roles] if has_sums else None
    if mode == "next":
        refs.pop(0)
    model = gate_ref.shape[1]
    width = model // GROUPS
    away = {"own": 0, "mine": 1 + place_ref[1], "other": 2 - place_ref[1], "diagonal": 3}
    if mode is None:
        outs = refs[: 2 * len(roles)]
        held = refs[2 * len(roles) :]
    else:
        outs, mark_ref, ready, sems = refs[:4]
        held = refs[4:]
        mark_ref[...] = jnp.zeros_like(mark_ref)
    copies = []
    for n, role in enumerate(roles):
        source = place_ref[0] ^ away[role]
        ref = pieces[n][0]
        if role == "diagonal":
            rows = ref.shape[0]
            held[0][tile(place_ref[1], rows), :] = ref[...]
            held[0][tile(1 - place_ref[1], rows), :] = pieces[n][1][...]
            ref = held[0]
        x = ref[:, :width]
        cols = tile(source ^ t, width)
        gated = dot(gate_ref[:, cols], x, NT)
        lifted = dot(up_ref[:, cols], x, NT)
        if sums is not None:
            gated = gated + sums[n][0][...]
            lifted = lifted + sums[n][1][...]
        if mode is None:
            outs[2 * n][...] = gated
            outs[2 * n + 1][...] = lifted
            continue
        lane = lax.broadcasted_iota(jnp.int32, (8, LANES), 1)
        squares = dot((lane < 3).astype(BF16), ref[:, width:], NT)[0:1, :]
        scale = lax.rsqrt(squares / model + 1e-05)
        gated, lifted = gated * scale, lifted * scale
        silu = (0.5 * gated) * (1.0 + jnp.tanh(0.5 * gated))
        ready[n] = (silu * lifted).astype(BF16)
        at = tile(source, ready.shape[2])
        rows = ready.shape[1] // 4
        for q in range(4):
            cut = slice(q * rows, (q + 1) * rows)
            copies.append(
                pltpu.make_async_copy(
                    ready.at[n, cut], outs.at[cut, at], sems.at[4 * n + q]
                )
            )
            copies[-1].start()
    for copy in copies:
        copy.wait()


def expert_step(place, t, final, roles, pieces, gate, up, sums, hidden, deps):
    hid, model = gate.shape
    width = model // GROUPS
    slots = sum(x.shape[0] for x in pieces[0])
    operands = [place, gate, up] + [x for per in pieces for x in per]
    has_sums = roles[0] in sums
    if has_sums:
        operands += [x for r in roles for x in sums[r]]
    specs = [SM] + [VM] * (len(operands) - 1)
    kwargs, mode, scratch = {}, None, []
    if final:
        mode = "first" if hidden is None else "next"
        if hidden is not None:
            kwargs["input_output_aliases"] = {len(operands): 0}
            operands.append(hidden)
            specs.append(ANY)
        out_shape = [like((hid, slots * GROUPS)), like((8, LANES), F32)]
        kwargs["out_specs"] = [ANY, VM]
        scratch += [
            pltpu.VMEM((len(roles), hid, slots), BF16),
            pltpu.SemaphoreType.DMA((4 * len(roles),)),
        ]
    else:
        out_shape = [like((hid, slots), F32)] * (2 * len(roles))
    if "diagonal" in roles:
        wide = pieces[roles.index("diagonal")][0].shape[1]
        scratch.append(pltpu.VMEM((slots, wide), BF16))
    out = call(
        functools.partial(expert_kernel, t, roles, mode, has_sums),
        out_shape,
        operands,
        4 * hid * slots * width * len(roles),
        hid * slots * len(roles) if mode else 0,
        deps,
        specs,
        20,
        scratch_shapes=scratch,
        **kwargs,
    )
    if mode:
        return out
    for n, r in enumerate(roles):
        sums[r] = out[2 * n : 2 * n + 2]
    return hidden, out[0]


def send(x, axis, pairs):
    return lax.ppermute(x, axis, pairs)


def swap(x):
    return send(x, "ctx", [(d, d ^ 1) for d in range(lax.axis_size("ctx"))])


def outbound(x):
    return send(x, "ctx", [(d, d ^ (4 if d % 2 else 2)) for d in range(lax.axis_size("ctx"))])


def onward(x):
    return send(x, "ctx", [(d, d ^ (2 if d % 2 else 4)) for d in range(lax.axis_size("ctx"))])


def on_square(
    queries,
    key_rows,
    value_rows,
    decay_rate,
    out_weight,
    residual,
    moe_gain,
    expert_ids,
    gate_weight,
    up_weight,
):
    ctx, exp = lax.axis_index("ctx"), lax.axis_index("exp")
    chip, core = ctx // CORES, lax.rem(ctx, CORES)
    place = jnp.stack([chip, core, exp]).astype(jnp.int32)
    length, here = queries.shape
    heads = decay_rate.shape[0]
    size = here // heads
    part = heads // CORES
    tokens, model = residual.shape
    cols = model // GROUPS // CORES
    capacity = max(2, 3 * tokens // lax.axis_size("exp"))
    every = CORES * length
    slots = every // tokens * capacity
    gate, up = gate_weight[0], up_weight[0]
    last = []

    def run(kernel, out_shape, operands, *more, deps=(), **kwargs):
        out = call(kernel, out_shape, operands, *more, deps=list(last) + list(deps), **kwargs)
        last[:] = [out[0] if isinstance(out, (list, tuple)) else out]
        return out

    rows = jnp.stack(scan_rows(chip, core, decay_rate, part, length)).reshape(-1)
    rows = jnp.concatenate([-decay_rate, rows])
    table = jnp.broadcast_to(rows[:, None, None], (rows.shape[0], 1, LANES))
    ids = jnp.concatenate([expert_ids.T, expert_ids.T], axis=1)
    lane = jnp.arange(LANES, dtype=jnp.int32)[None, :]
    ids = jnp.where(lane // tokens == exp % (LANES // tokens), ids, -1)
    ids = jnp.pad(ids, ((0, 6), (0, 0)), constant_values=-1)
    gain = moe_gain[None, :]
    weight_y = send(out_weight, "ctx", [(d, d ^ 4) for d in range(8)])

    state_like = like((part, size, size), F32)
    mine, theirs, keys, values = run(
        fresh_kernel,
        [state_like] * 2 + [like((length, here))] * 2,
        [place, table, key_rows, value_rows],
        4 * heads * length * size * size,
        heads * length * size,
        deps=[ids],
        specs=[SM, VM, HBM, HBM],
        scratch_shapes=[pltpu.SemaphoreType.DMA((4,))],
    )

    def mix(recipe, operands, deps=()):
        return run(
            functools.partial(mix_kernel, recipe),
            [state_like] * len(recipe),
            [table] + operands,
            deps=deps,
        )

    def copy(x):
        return run(copy_kernel, like(x.shape, x.dtype), [x])

    def cut(x, start):
        return run(
            functools.partial(rows_kernel, start), like((x.shape[0] // 2, x.shape[1])), [x]
        )

    got = swap(theirs)
    first, total = mix([[(0, 0), (1, 1)], [(0, 2), (1, 3)]], [mine, got])
    got = send(total, "ctx", [(d, d ^ 2) for d in range(8)])
    ids_got = send(ids, "exp", [(d, d ^ 1) for d in range(4)])
    rest_got = swap(residual)
    local, queries_here = run(
        local_kernel,
        [like((length, here), F32), like((length, here))],
        [table, queries, keys, values],
        4 * heads * length * length * size,
        heads * length * length,
        specs=[VM, HBM, VM, VM],
        scratch_shapes=[pltpu.SemaphoreType.DMA(())],
    )
    ids = run(larger_kernel, like(ids.shape, ids.dtype), [ids, ids_got])
    state, total = mix([[(0, 4)], [(0, 5), (1, 6)]], [got, total], [rest_got, weight_y])
    got = send(total, "ctx", [(d, d + 4) for d in range(4)])
    weight_x = send(copy(out_weight), "ctx", [(d, d ^ 2) for d in range(8)])
    ids_got = send(ids, "exp", [(d, d ^ 2) for d in range(4)])
    ids = run(
        functools.partial(stack_kernel, 2),
        like((16, LANES), ids.dtype),
        [place, ids, ids_got],
        specs=[SM, VM, VM],
    )
    keep, give = mix(
        [[(0, 7), (1, 8), (2, 9)], [(0, 10), (1, 11), (2, 12)]], [state, got, first]
    )
    got = swap(give)
    ids_got = swap(ids)
    head_out = run(
        head_kernel,
        like((length, here)),
        [place, table, queries_here, local, keep, got],
        4 * heads * length * size * size,
        heads * length * size,
        specs=[SM] + [VM] * 5,
    )
    heads_got = swap(head_out)
    picks = run(
        functools.partial(picks_kernel, tokens, capacity),
        like((slots, every)),
        [place, ids, ids_got],
        specs=[SM, VM, VM],
    )

    chunk_f32, chunk_b16 = like((every, cols), F32), like((every, cols))
    end = GROUPS - 1
    wide = [cols + LANES * (n == end) for n in range(GROUPS)]
    weights = [[out_weight], [weight_y], [weight_x], None]
    parts, totals, mixed, joined = [None] * 4, [None] * 4, [None] * 4, [None] * 4
    moved = {}
    sums, hidden = {}, None

    def project(n):
        parts[n], sent = run(
            functools.partial(project_kernel, ORDER[n]),
            [chunk_f32, chunk_b16],
            [place, head_out, heads_got, residual, rest_got] + weights[n],
            2 * every * here * cols,
            specs=[SM] + [VM] * (4 + len(weights[n])),
        )
        moved["in", n] = send(sent, "exp", [(0, 1), (3, 2)])

    def inward(n):
        parts[n], sent = run(
            inward_kernel, [chunk_f32, chunk_b16], [parts[n], moved["in", n]], every * cols
        )
        moved["across", n] = send(sent, "exp", [(1, 2), (2, 1)])

    def outward(n):
        totals[n] = run(total_kernel, chunk_b16, [parts[n], moved["across", n]], every * cols)
        moved["out", n] = send(totals[n], "exp", [(1, 0), (2, 3)])

    def dispatch(n):
        outs = [like((slots, wide[n])), chunk_b16]
        known = []
        if n == end:
            outs.append(like((tokens, GROUPS * cols)))
            known = mixed[:n]
        x, mixed[n], *gives = run(
            functools.partial(dispatch_kernel, ORDER[n], n == end),
            outs,
            [place, moved["out", n], totals[n], gain, picks] + known,
            2 * slots * every * wide[n],
            specs=[SM] + [VM] * (4 + len(known)),
        )
        moved["x", n] = (x, swap(x))
        if gives:
            moved["mixed"] = swap(gives[0])

    def join(n):
        joined[n] = run(
            functools.partial(join_kernel, cols),
            like((slots, wide[n] + cols)),
            [place, *moved["x", n]],
            specs=[SM, VM, VM],
        )
        moved["near", n] = outbound(joined[n])

    def half(n):
        near = moved["near", n]
        out, copied = run(
            half_kernel,
            [like((slots // 2, near.shape[1])), like(near.shape)],
            [place, near],
            specs=[SM, VM],
        )
        moved["far", n] = onward(out)
        moved["other", n] = swap(copied)

    def diagonal(n):
        moved["far", n] = copy(moved["far", n])
        moved["rest", n] = swap(moved["far", n])

    def experts(n, roles, pieces):
        nonlocal hidden
        hidden, mark = expert_step(
            place, ORDER[n], n == end, roles, pieces, gate, up, sums, hidden, last[:]
        )
        last[:] = [mark]

    def nearer(n):
        experts(n, ROLES[:3], [[joined[n]], [moved["near", n]], [moved["other", n]]])

    def farther(n):
        experts(n, ROLES[3:], [[moved["far", n], moved["rest", n]]])

    def fetch(n):
        top = send(cut(weight_x, 0), "ctx", [(d, d ^ 4) for d in range(8)])
        bottom = send(cut(weight_y, here // 2), "ctx", [(d, d ^ 2) for d in range(8)])
        weights[n] = [top, bottom]

    for work, n in (
        (project, 0), (project, 1), (inward, 0), (project, 2), (fetch, 3), (inward, 1),
        (outward, 0), (project, 3), (inward, 2), (outward, 1), (dispatch, 0), (inward, 3),
        (join, 0), (outward, 2), (dispatch, 1), (join, 1), (outward, 3), (half, 0),
        (dispatch, 2), (join, 2), (nearer, 0), (half, 1), (diagonal, 0), (farther, 0),
        (dispatch, 3), (join, 3), (nearer, 1), (half, 2), (diagonal, 1), (farther, 1),
        (nearer, 2), (half, 3), (diagonal, 2), (farther, 2), (nearer, 3),
    ):
        work(n)
    mixed_out = call(
        mixed_kernel,
        like((tokens, model)),
        [place, moved["mixed"]] + mixed,
        deps=last[:],
        specs=[SM] + [VM] * (GROUPS + 1),
    )
    diagonal(3)
    farther(3)
    return (mixed_out, hidden[None])


def entering(value, axis, combine, identity):
    devices, position = (lax.axis_size(axis), lax.axis_index(axis))
    everything = jax.tree.map(lambda part: lax.all_gather(part, axis), value)
    start = jax.tree.map(
        lambda part, zero: jnp.broadcast_to(jnp.asarray(zero, part.dtype), part.shape),
        value,
        identity,
    )

    def hop(k, before):
        reached = k < position
        new = combine(before, jax.tree.map(lambda part: part[k], everything))
        return jax.tree.map(lambda a, b: jnp.where(reached, a, b), new, before)

    return lax.fori_loop(0, devices, hop, start)


def route_slots(id_rows):
    count = id_rows.shape[1]
    same = id_rows[:, :, None] == id_rows[:, None, :]
    before = lax.broadcasted_iota(jnp.int32, (count, count), 1) < lax.broadcasted_iota(
        jnp.int32, (count, count), 0
    )
    return jnp.sum((same & before[None]).astype(jnp.int32), axis=2)


def select_matrix(id_rows, slot_rows, owners, capacity):
    routes = id_rows.shape[1]
    places = jnp.arange(capacity, dtype=jnp.int32)
    hits = (id_rows[:, None, None, :] == owners[None, :, None, None]) & (
        slot_rows[:, None, None, :] == places[None, None, :, None]
    )
    to_token = (
        jnp.arange(routes, dtype=jnp.int32)[:, None] // 2
        == jnp.arange(routes // 2, dtype=jnp.int32)[None, :]
    ).astype(jnp.float32)
    return jnp.einsum("bepr,rt->bept", hits.astype(jnp.float32), to_token)


def on_any_mesh(
    queries,
    key_rows,
    value_rows,
    decay_rate,
    out_weight,
    residual,
    moe_gain,
    expert_ids,
    gate_weight,
    up_weight,
):
    highest = lax.Precision.HIGHEST
    block_len = queries.shape[0]
    heads_here = decay_rate.shape[0]
    width_here = queries.shape[1]
    head_size = width_here // heads_here
    exp_count = lax.axis_size("exp")
    tok_count = block_len // exp_count
    capacity = max(2, 3 * tok_count // exp_count)
    query_here = queries.reshape(block_len, heads_here, head_size)
    key_here = key_rows.reshape(block_len, heads_here, head_size)
    value_here = value_rows.reshape(block_len, heads_here, head_size)
    position = jnp.arange(block_len, dtype=jnp.float32)
    offset = position[:, None] - position[None, :]
    masked = jnp.where(
        (offset >= 0)[None],
        jnp.exp(-decay_rate[:, None, None] * jnp.maximum(offset, 0.0)[None]),
        0.0,
    )
    inner = jnp.exp(-decay_rate[None, :] * position[:, None])
    tail = jnp.exp(-decay_rate[None, :] * (block_len - position[:, None]))
    whole = jnp.exp(-decay_rate * block_len)
    scores = jnp.einsum("ihd,jhd->hij", query_here, key_here, preferred_element_type=jnp.float32)
    weighted = (scores * masked).astype(jnp.bfloat16)
    local_part = jnp.einsum(
        "hij,jhd->ihd", weighted, value_here, preferred_element_type=jnp.float32
    )
    fresh = jnp.einsum(
        "jhd,jhe->hde",
        key_here.astype(jnp.float32) * tail[:, :, None],
        value_here.astype(jnp.float32),
        precision=highest,
    )

    def combine(earlier, later):
        return (earlier[0] * later[0], later[0][:, None, None] * earlier[1] + later[1])

    unused, state_in = entering(
        (whole, fresh), "ctx", combine, (jnp.ones_like(whole), jnp.zeros_like(fresh))
    )
    carried = (
        jnp.einsum("ihd,hde->ihe", query_here.astype(jnp.float32), state_in, precision=highest)
        * inner[:, :, None]
    )
    attended = local_part + carried
    scale_rows = lax.rsqrt(jnp.mean(attended * attended, axis=-1, keepdims=True) + 1e-05)
    head_out = (attended * scale_rows).astype(jnp.bfloat16).reshape(block_len, width_here)
    partial_rows = jnp.dot(
        head_out,
        lax.all_gather(out_weight, "ctx", axis=1, tiled=True),
        preferred_element_type=jnp.float32,
    )
    attn = lax.psum_scatter(partial_rows, "exp", scatter_dimension=0, tiled=True)
    mixed = (residual.astype(jnp.float32) + attn).astype(jnp.bfloat16)
    mixed_f = mixed.astype(jnp.float32)
    normed = (
        mixed_f * lax.rsqrt(jnp.mean(mixed_f * mixed_f, axis=-1, keepdims=True) + 1e-05) * moe_gain
    ).astype(jnp.bfloat16)
    id_rows = expert_ids.reshape(1, 2 * tok_count)
    slot_rows = route_slots(id_rows)
    picks = select_matrix(id_rows, slot_rows, jnp.arange(exp_count, dtype=jnp.int32), capacity)[0]
    picks = picks.reshape(exp_count * capacity, tok_count).astype(jnp.bfloat16)
    buffer = jnp.dot(picks, normed, preferred_element_type=jnp.float32).astype(jnp.bfloat16)
    received = lax.all_to_all(buffer, "exp", split_axis=0, concat_axis=0, tiled=True)
    gate_here = gate_weight[0]
    up_here = up_weight[0]
    contract = (((1,), (1,)), ((), ()))
    piece = lax.all_gather(received, "ctx", axis=0, tiled=True)
    gated = lax.dot_general(gate_here, piece, contract, preferred_element_type=jnp.float32)
    lifted = lax.dot_general(up_here, piece, contract, preferred_element_type=jnp.float32)
    hidden = (jax.nn.silu(gated) * lifted).astype(jnp.bfloat16)
    return (mixed, hidden[None])


def solution(mesh):
    in_specs = (
        P("ctx", "exp"),
        P("ctx", "exp"),
        P("ctx", "exp"),
        P("exp"),
        P("exp", "ctx"),
        P(("ctx", "exp"), None),
        P(),
        P(("ctx", "exp"), None),
        P("exp", "ctx", None),
        P("exp", "ctx", None),
    )
    out_specs = (P(("ctx", "exp"), None), P("exp", "ctx", None))
    square, line = mesh.shape["ctx"] == GROUPS * CORES, mesh.shape["exp"] == 4

    def per_device(*args):
        tokens, model = args[5].shape
        fits = square and line and 2 * tokens == LANES and args[3].shape[0] % CORES == 0
        fits = fits and model % (GROUPS * CORES * LANES) == 0
        return (on_square if fits else on_any_mesh)(*args)

    return jax.shard_map(
        per_device, mesh=mesh, in_specs=in_specs, out_specs=out_specs, check_vma=False
    )
```

```python
import functools

import jax
import jax.numpy as jnp
from jax import lax
from jax.experimental import pallas as pl
from jax.experimental.pallas import tpu as pltpu
from jax.sharding import PartitionSpec as P

GROUPS = 4
CORES = 2
ORDER = (0, 2, 1, 3)
LANES = 128
BF16 = jnp.bfloat16
F32 = jnp.float32
NT = (((1,), (1,)), ((), ()))
TN = (((0,), (0,)), ((), ()))
NN = (((1,), (0,)), ((), ()))
VM = pl.BlockSpec(memory_space=pltpu.VMEM)
SM = pl.BlockSpec(memory_space=pltpu.SMEM)
HBM = pl.BlockSpec(memory_space=pltpu.HBM)
ANY = pl.BlockSpec(memory_space=pl.ANY)


def dot(a, b, dims):
    return lax.dot_general(a, b, dims, preferred_element_type=F32)


def halves(x):
    high = x.astype(BF16)
    return high, (x - high.astype(F32)).astype(BF16)


def like(shape, dtype=BF16):
    return jax.ShapeDtypeStruct(tuple(shape), dtype)


def call(kernel, out_shape, operands, deps=(), specs=None, limit=12, **kwargs):
    count, extra = len(operands), len(deps)

    def body(*refs):
        kernel(*refs[:count], *refs[count + extra :])

    kwargs.setdefault("out_specs", jax.tree.map(lambda _: VM, out_shape))
    return pl.pallas_call(
        body,
        out_shape=out_shape,
        in_specs=list(specs or [VM] * count) + [ANY] * extra,
        compiler_params=pltpu.CompilerParams(vmem_limit_bytes=limit * 1024 * 1024),
        cost_estimate=pl.CostEstimate(flops=1, bytes_accessed=1, transcendentals=0),
        **kwargs,
    )(*operands, *deps)


def tile(index, size):
    return pl.ds(pl.multiple_of(index * size, size), size)


def fresh_kernel(place_ref, rate_ref, k_in, v_in, mine_ref, theirs_ref, k_ref, v_ref, sems):
    part, size = mine_ref.shape[0], mine_ref.shape[1]
    length = k_ref.shape[0]
    left = length - lax.broadcasted_iota(jnp.int32, (length, size), 0).astype(F32)
    order = ((theirs_ref, 1 - place_ref[1]), (mine_ref, place_ref[1]))
    copies = []
    for n, (_, half) in enumerate(order):
        at = tile(half, part * size)
        for source, target in ((k_in, k_ref), (v_in, v_ref)):
            copies.append(
                pltpu.make_async_copy(source.at[:, at], target.at[:, at], sems.at[len(copies)])
            )
            copies[-1].start()
    for n, (out_ref, half) in enumerate(order):
        copies[2 * n].wait()
        copies[2 * n + 1].wait()
        for j in range(part):
            head = half * part + j
            cols = tile(head, size)
            tail = jnp.exp(rate_ref[head] * left)
            high, low = halves(k_ref[:, cols].astype(F32) * tail)
            v = v_ref[:, cols]
            out_ref[j] = dot(high, v, TN) + dot(low, v, TN)


def local_kernel(rate_ref, q_in, k_ref, v_ref, out_ref, q_ref, sem):
    length, size = k_ref.shape[0], rate_ref.shape[2]
    heads = k_ref.shape[1] // size
    copy = pltpu.make_async_copy(q_in, q_ref, sem)
    copy.start()
    rows = lax.broadcasted_iota(jnp.int32, (length, length), 0)
    cols = lax.broadcasted_iota(jnp.int32, (length, length), 1)
    offset = (rows - cols).astype(F32)
    keep = offset >= 0
    offset = jnp.maximum(offset, 0.0)
    copy.wait()
    for h in range(heads):
        at = slice(h * size, (h + 1) * size)
        rate = jnp.concatenate([rate_ref[h]] * (length // LANES), axis=1)
        masked = jnp.where(keep, jnp.exp(rate * offset), 0.0)
        weighted = (dot(q_ref[:, at], k_ref[:, at], NT) * masked).astype(BF16)
        out_ref[:, at] = dot(weighted, v_ref[:, at], NN)


def mix_kernel(recipe, coef_ref, *refs):
    count = 1 + max(i for terms in recipe for i, _ in terms)
    part = refs[0].shape[0]
    first = CORES * part
    for j in range(part):
        values = [refs[i][j] for i in range(count)]
        for out_ref, terms in zip(refs[count:], recipe):
            out_ref[j] = sum(values[i] * coef_ref[first + row * part + j] for i, row in terms)


def scan_rows(chip, core, rate, part, length):
    rates = lax.dynamic_slice(rate, (core * part,), (part,))

    def fade(blocks):
        return jnp.exp(-rates * (length * blocks))

    one, none = jnp.ones_like(rates), jnp.zeros_like(rates)
    first, east, south = core == 0, (chip & 1) != 0, (chip & 2) != 0
    behind = jnp.where(south, fade(2.0 * (chip & 1).astype(F32)), none)
    keep, give = jnp.where(first, one, fade(1.0)), jnp.where(first, fade(1.0), one)
    return [
        jnp.where(first, one, none),
        jnp.where(first, none, one),
        jnp.where(first, fade(1.0), one),
        jnp.where(first, one, fade(1.0)),
        jnp.where(east, one, none),
        jnp.where(east, fade(2.0), one),
        jnp.where(east, one, fade(2.0)),
        keep,
        keep * behind,
        jnp.where(first, none, one),
        give,
        give * behind,
        jnp.where(first, one, none),
    ]


def head_kernel(place_ref, rate_ref, q_ref, local_ref, keep_ref, got_ref, out_ref):
    part, size = keep_ref.shape[0], keep_ref.shape[1]
    length = q_ref.shape[0]
    pos = lax.broadcasted_iota(jnp.int32, (length, size), 0).astype(F32)
    for state_ref, half in ((keep_ref, place_ref[1]), (got_ref, 1 - place_ref[1])):
        for j in range(part):
            head = half * part + j
            at = tile(head, size)
            high, low = halves(state_ref[j])
            q = q_ref[:, at]
            carried = dot(q, high, NN) + dot(q, low, NN)
            carried = carried * jnp.exp(rate_ref[head] * pos)
            attended = local_ref[:, at] + carried
            scale = lax.rsqrt(jnp.mean(attended * attended, axis=-1, keepdims=True) + 1e-05)
            out_ref[:, at] = (attended * scale).astype(BF16)


def larger_kernel(a_ref, b_ref, out_ref):
    out_ref[...] = jnp.maximum(a_ref[...], b_ref[...])


def stack_kernel(which, place_ref, a_ref, b_ref, out_ref):
    rows = a_ref.shape[0]
    upper = (place_ref[which] >> (1 if which == 2 else 0)) & 1
    out_ref[tile(upper, rows), :] = a_ref[...]
    out_ref[tile(1 - upper, rows), :] = b_ref[...]


def picks_kernel(tokens, capacity, place_ref, own_ref, got_ref, out_ref):
    slots = out_ref.shape[0]
    before = lax.broadcasted_iota(jnp.int32, (LANES, LANES), 0)
    token = lax.broadcasted_iota(jnp.int32, (LANES, LANES), 1)
    earlier = ((before < token) & (before // tokens == token // tokens)).astype(BF16)
    lane = lax.broadcasted_iota(jnp.int32, (8, LANES), 1)
    slot = lax.broadcasted_iota(jnp.int32, (slots, LANES), 0)
    per = own_ref.shape[0] // 8
    for ref, half in ((own_ref, place_ref[1]), (got_ref, 1 - place_ref[1])):
        for n in range(per):
            first, second = ref[8 * n : 8 * n + 1, :], ref[8 * n + 1 : 8 * n + 2, :]
            named = (first == place_ref[2]) | (second == place_ref[2])
            named = jnp.broadcast_to(named.astype(F32), (8, LANES))
            rank = dot(named.astype(BF16), earlier, NN).astype(jnp.int32)
            run = half * per + n
            row = (run * (LANES // tokens) + lane // tokens) * capacity + rank
            row = jnp.where((named > 0.5) & (rank < capacity), row, -1)
            out_ref[:, tile(run, LANES)] = (slot == row[0:1, :]).astype(BF16)


def project_kernel(t, place_ref, own_ref, got_ref, rest_ref, rest_got_ref, *refs):
    weights, (sum_ref, sent_ref) = refs[:-2], refs[-2:]
    length, tokens, cols = own_ref.shape[0], rest_ref.shape[0], sum_ref.shape[1]
    depth = own_ref.shape[1] // len(weights)
    at = tile((place_ref[0] ^ t) * CORES + place_ref[1], cols)
    for head_ref, row_ref, half in (
        (own_ref, rest_ref, place_ref[1]),
        (got_ref, rest_got_ref, 1 - place_ref[1]),
    ):
        value = 0.0
        for n, weight in enumerate(weights):
            value = value + dot(head_ref[:, n * depth : (n + 1) * depth], weight[...], NN)
        pieces = []
        for z in range(length // tokens):
            piece = value[z * tokens : (z + 1) * tokens, :]
            pieces.append(
                jnp.where(place_ref[2] == z, piece + row_ref[:, at].astype(F32), piece)
            )
        value = jnp.concatenate(pieces, axis=0)
        sum_ref[tile(half, length), :] = value
        sent_ref[tile(half, length), :] = value.astype(BF16)


def inward_kernel(part_ref, got_ref, sum_ref, sent_ref):
    total = part_ref[...] + got_ref[...].astype(F32)
    sum_ref[...] = total
    sent_ref[...] = total.astype(BF16)


def outer(place_ref):
    return (place_ref[2] == 0) | (place_ref[2] == 3)


def total_kernel(part_ref, got_ref, out_ref):
    out_ref[...] = (part_ref[...] + got_ref[...].astype(F32)).astype(BF16)


def dispatch_kernel(t, final, place_ref, got_ref, given_ref, gain_ref, picks_ref, *refs):
    earlier, (out_ref, mixed_ref), gives = refs[:-2], refs[-2:], []
    if final:
        earlier, (out_ref, mixed_ref, give_ref) = refs[:-3], refs[-3:]
        gives = [give_ref]
    cols = mixed_ref.shape[1]
    mixed = jnp.where(outer(place_ref), got_ref[...], given_ref[...])
    mixed_ref[...] = mixed
    value = mixed.astype(F32)
    gain = gain_ref[:, tile((place_ref[0] ^ t) * CORES + place_ref[1], cols)]
    out_ref[:, :cols] = dot(picks_ref[...], (value * gain).astype(BF16), NN).astype(BF16)
    if not gives:
        return
    squares = jnp.sum(value * value, axis=1, keepdims=True)
    for ref in earlier:
        value = ref[...].astype(F32)
        squares = squares + jnp.sum(value * value, axis=1, keepdims=True)
    extra = dot(picks_ref[...], in_three(squares), NN)
    out_ref[:, cols:] = extra.astype(BF16)
    tokens = give_ref.shape[0]
    per = mixed_ref.shape[0] // CORES // tokens
    rows = tile((1 - place_ref[1]) * per + place_ref[2], tokens)
    for n, ref in enumerate(list(earlier) + [mixed_ref]):
        give_ref[:, n * cols : (n + 1) * cols] = ref[rows, :]


def in_three(column):
    lane = lax.broadcasted_iota(jnp.int32, (column.shape[0], LANES), 1)
    rest, out = column, jnp.zeros((column.shape[0], LANES), F32)
    for place in range(3):
        high = rest.astype(BF16).astype(F32)
        out = jnp.where(lane == place, high, out)
        rest = rest - high
    return out.astype(BF16)


def pack_kernel(place_ref, own_ref, near_ref, far_ref, onward_ref, pack_ref):
    wide = own_ref.shape[1]
    onward_ref[...] = jnp.where(place_ref[1] == 0, near_ref[...], far_ref[...])
    for n, ref in enumerate((own_ref, near_ref, far_ref)):
        pack_ref[:, n * wide : (n + 1) * wide] = ref[...]


def copy_kernel(in_ref, out_ref):
    out_ref[...] = in_ref[...]


def rows_kernel(start, in_ref, out_ref):
    out_ref[...] = in_ref[start : start + out_ref.shape[0], :]


def mixed_kernel(place_ref, got_ref, *refs):
    mixed, out_ref = refs[:-1], refs[-1]
    tokens, cols = out_ref.shape[0], mixed[0].shape[1]
    per = mixed[0].shape[0] // CORES // tokens
    own = tile(place_ref[1] * per + place_ref[2], tokens)
    for t, ref in zip(ORDER, mixed):
        block = (place_ref[0] ^ t) * CORES
        n = ORDER.index(t)
        out_ref[:, tile(block + place_ref[1], cols)] = ref[own, :]
        out_ref[:, tile(block + 1 - place_ref[1], cols)] = got_ref[:, n * cols : (n + 1) * cols]


def expert_kernel(t, away, mode, has_sums, place_ref, gate_ref, up_ref, *refs):
    refs = list(refs)
    pieces, others = refs[: len(away)], refs[len(away)]
    refs = refs[len(away) + 1 :]
    sums = [[refs.pop(0), refs.pop(0)] for _ in away] if has_sums else None
    if mode == "next":
        refs.pop(0)
    model = gate_ref.shape[1]
    width = model // GROUPS
    cols, wide = width // CORES, pieces[0].shape[1]
    if mode is None:
        outs = refs[: 2 * len(away)]
        held = refs[2 * len(away)]
    else:
        outs, mark_ref, held, ready, sems = refs
        mark_ref[...] = jnp.zeros_like(mark_ref)
    copies = []
    for n, s in enumerate(away):
        source = place_ref[0] ^ s
        held[n, :, tile(place_ref[1], cols)] = pieces[n][:, :cols]
        held[n, :, tile(1 - place_ref[1], cols)] = others[:, n * wide : n * wide + cols]
        x = held[n]
        at = tile(source ^ t, width)
        gated = dot(gate_ref[:, at], x, NT)
        lifted = dot(up_ref[:, at], x, NT)
        if sums is not None:
            gated = gated + sums[n][0][...]
            lifted = lifted + sums[n][1][...]
        if mode is None:
            outs[2 * n][...] = gated
            outs[2 * n + 1][...] = lifted
            continue
        lane = lax.broadcasted_iota(jnp.int32, (8, LANES), 1)
        pick = (lane < 3).astype(BF16)
        squares = dot(pick, pieces[n][:, cols:], NT)
        squares = squares + dot(pick, others[:, n * wide + cols : (n + 1) * wide], NT)
        scale = lax.rsqrt(squares[0:1, :] / model + 1e-05)
        gated, lifted = gated * scale, lifted * scale
        silu = (0.5 * gated) * (1.0 + jnp.tanh(0.5 * gated))
        ready[n] = (silu * lifted).astype(BF16)
        at = tile(source, ready.shape[2])
        rows = ready.shape[1] // 4
        for q in range(4):
            part = slice(q * rows, (q + 1) * rows)
            copies.append(
                pltpu.make_async_copy(ready.at[n, part], outs.at[part, at], sems.at[4 * n + q])
            )
            copies[-1].start()
    for copy in copies:
        copy.wait()


def expert_step(place, t, final, away, pieces, others, gate, up, sums, hidden, deps):
    hid, model = gate.shape
    width = model // GROUPS
    slots = pieces[0].shape[0]
    operands = [place, gate, up] + pieces + [others]
    has_sums = away[0] in sums
    if has_sums:
        operands += [x for s in away for x in sums[s]]
    specs = [SM] + [VM] * (len(operands) - 1)
    kwargs, mode = {}, None
    scratch = [pltpu.VMEM((len(away), slots, width), BF16)]
    if final:
        mode = "first" if hidden is None else "next"
        if hidden is not None:
            kwargs["input_output_aliases"] = {len(operands): 0}
            operands.append(hidden)
            specs.append(ANY)
        out_shape = [like((hid, slots * GROUPS)), like((8, LANES), F32)]
        kwargs["out_specs"] = [ANY, VM]
        scratch += [
            pltpu.VMEM((len(away), hid, slots), BF16),
            pltpu.SemaphoreType.DMA((4 * len(away),)),
        ]
    else:
        out_shape = [like((hid, slots), F32)] * (2 * len(away))
    out = call(
        functools.partial(expert_kernel, t, away, mode, has_sums),
        out_shape,
        operands,
        deps=deps,
        specs=specs,
        limit=20,
        scratch_shapes=scratch,
        **kwargs,
    )
    if mode:
        return out
    for n, s in enumerate(away):
        sums[s] = out[2 * n : 2 * n + 2]
    return hidden, out[0]


def send(x, axis, pairs):
    return lax.ppermute(x, axis, pairs)


def swap(x):
    return send(x, "ctx", [(d, d ^ 1) for d in range(lax.axis_size("ctx"))])


def onward(x):
    return send(x, "ctx", [(d, d ^ (2 if d % 2 else 4)) for d in range(lax.axis_size("ctx"))])


def on_square(
    queries,
    key_rows,
    value_rows,
    decay_rate,
    out_weight,
    residual,
    moe_gain,
    expert_ids,
    gate_weight,
    up_weight,
):
    ctx, exp = lax.axis_index("ctx"), lax.axis_index("exp")
    chip, core = ctx // CORES, lax.rem(ctx, CORES)
    place = jnp.stack([chip, core, exp]).astype(jnp.int32)
    length, here = queries.shape
    heads = decay_rate.shape[0]
    size = here // heads
    part = heads // CORES
    tokens, model = residual.shape
    cols = model // GROUPS // CORES
    capacity = max(2, 3 * tokens // lax.axis_size("exp"))
    every = CORES * length
    slots = every // tokens * capacity
    gate, up = gate_weight[0], up_weight[0]
    last = []

    def run(kernel, out_shape, operands, deps=(), **kwargs):
        out = call(kernel, out_shape, operands, list(last) + list(deps), **kwargs)
        last[:] = [out[0] if isinstance(out, (list, tuple)) else out]
        return out

    rows = jnp.stack(scan_rows(chip, core, decay_rate, part, length)).reshape(-1)
    rows = jnp.concatenate([-decay_rate, rows])
    table = jnp.broadcast_to(rows[:, None, None], (rows.shape[0], 1, LANES))
    ids = jnp.concatenate([expert_ids.T, expert_ids.T], axis=1)
    lane = jnp.arange(LANES, dtype=jnp.int32)[None, :]
    ids = jnp.where(lane // tokens == exp % (LANES // tokens), ids, -1)
    ids = jnp.pad(ids, ((0, 6), (0, 0)), constant_values=-1)
    gain = moe_gain[None, :]
    weight_y = send(out_weight, "ctx", [(d, d ^ 4) for d in range(8)])

    state_like = like((part, size, size), F32)
    mine, theirs, keys, values = run(
        fresh_kernel,
        [state_like] * 2 + [like((length, here))] * 2,
        [place, table, key_rows, value_rows],
        deps=[ids],
        specs=[SM, VM, HBM, HBM],
        scratch_shapes=[pltpu.SemaphoreType.DMA((4,))],
    )

    def mix(recipe, operands, deps=()):
        return run(
            functools.partial(mix_kernel, recipe),
            [state_like] * len(recipe),
            [table] + operands,
            deps=deps,
        )

    def copy(x):
        return run(copy_kernel, like(x.shape, x.dtype), [x])

    def cut(x, start):
        return run(
            functools.partial(rows_kernel, start), like((x.shape[0] // 2, x.shape[1])), [x]
        )

    got = swap(theirs)
    first, total = mix([[(0, 0), (1, 1)], [(0, 2), (1, 3)]], [mine, got])
    got = send(total, "ctx", [(d, d ^ 2) for d in range(8)])
    ids_got = send(ids, "exp", [(d, d ^ 1) for d in range(4)])
    rest_got = swap(residual)
    local, queries_here = run(
        local_kernel,
        [like((length, here), F32), like((length, here))],
        [table, queries, keys, values],
        specs=[VM, HBM, VM, VM],
        scratch_shapes=[pltpu.SemaphoreType.DMA(())],
    )
    ids = run(larger_kernel, like(ids.shape, ids.dtype), [ids, ids_got])
    state, total = mix([[(0, 4)], [(0, 5), (1, 6)]], [got, total], [rest_got, weight_y])
    got = send(total, "ctx", [(d, d + 4) for d in range(4)])
    weight_x = send(copy(out_weight), "ctx", [(d, d ^ 2) for d in range(8)])
    ids_got = send(ids, "exp", [(d, d ^ 2) for d in range(4)])
    ids = run(
        functools.partial(stack_kernel, 2),
        like((16, LANES), ids.dtype),
        [place, ids, ids_got],
        specs=[SM, VM, VM],
    )
    keep, give = mix(
        [[(0, 7), (1, 8), (2, 9)], [(0, 10), (1, 11), (2, 12)]], [state, got, first]
    )
    got = swap(give)
    ids_got = swap(ids)
    head_out = run(
        head_kernel,
        like((length, here)),
        [place, table, queries_here, local, keep, got],
        specs=[SM] + [VM] * 5,
    )
    heads_got = swap(head_out)

    chunk_f32, chunk_b16 = like((every, cols), F32), like((every, cols))
    end = GROUPS - 1
    wide = [cols + LANES * (n == end) for n in range(GROUPS)]
    weights = [[out_weight], [weight_y], [weight_x], None]
    parts, totals, mixed = [None] * 4, [None] * 4, [None] * 4
    moved = {}
    sums, hidden = {}, None

    def routes(n):
        moved["picks", n] = run(
            functools.partial(picks_kernel, tokens, capacity),
            like((slots, every)),
            [place, ids, ids_got],
            specs=[SM, VM, VM],
        )

    def project(n):
        parts[n], sent = run(
            functools.partial(project_kernel, ORDER[n]),
            [chunk_f32, chunk_b16],
            [place, head_out, heads_got, residual, rest_got] + weights[n],
            specs=[SM] + [VM] * (4 + len(weights[n])),
        )
        moved["in", n] = send(sent, "exp", [(0, 1), (3, 2)])

    def inward(n):
        parts[n], sent = run(
            inward_kernel, [chunk_f32, chunk_b16], [parts[n], moved["in", n]]
        )
        moved["across", n] = send(sent, "exp", [(1, 2), (2, 1)])

    def outward(n):
        totals[n] = run(total_kernel, chunk_b16, [parts[n], moved["across", n]])
        moved["out", n] = send(totals[n], "exp", [(1, 0), (2, 3)])

    def dispatch(n):
        outs = [like((slots, wide[n])), chunk_b16]
        known = []
        if n == end:
            outs.append(like((tokens, GROUPS * cols)))
            known = mixed[:n]
        x, mixed[n], *gives = run(
            functools.partial(dispatch_kernel, ORDER[n], n == end),
            outs,
            [place, moved["out", n], totals[n], gain, moved["picks", 0]] + known,
            specs=[SM] + [VM] * (4 + len(known)),
        )
        moved["own", n] = x
        moved["near", n] = send(x, "ctx", [(d, d ^ 2) for d in range(8)])
        moved["far", n] = send(x, "ctx", [(d, d ^ 4) for d in range(8)])
        if gives:
            moved["mixed"] = swap(gives[0])

    def forward(n):
        x = moved["own", n]
        out, pack = run(
            pack_kernel,
            [like(x.shape), like((slots, 3 * wide[n]))],
            [place, x, moved["near", n], moved["far", n]],
            specs=[SM] + [VM] * 3,
        )
        moved["diagonal", n] = onward(out)
        moved["others", n] = swap(pack)

    def diagonal(n):
        moved["diagonal", n] = copy(moved["diagonal", n])
        moved["rest", n] = swap(moved["diagonal", n])

    def experts(n, away, pieces, others):
        nonlocal hidden
        hidden, mark = expert_step(
            place, ORDER[n], n == end, away, pieces, others, gate, up, sums, hidden, last[:]
        )
        last[:] = [mark]

    def nearer(n):
        pieces = [moved["own", n], moved["near", n], moved["far", n]]
        experts(n, (0, 1, 2), pieces, moved["others", n])

    def farther(n):
        experts(n, (3,), [moved["diagonal", n]], moved["rest", n])

    def fetch(n):
        top = send(cut(weight_x, 0), "ctx", [(d, d ^ 4) for d in range(8)])
        bottom = send(cut(weight_y, here // 2), "ctx", [(d, d ^ 2) for d in range(8)])
        weights[n] = [top, bottom]

    for work, n in (
        (project, 0), (project, 1), (routes, 0), (inward, 0), (fetch, 3), (project, 2),
        (inward, 1), (outward, 0), (project, 3), (inward, 2), (outward, 1), (dispatch, 0),
        (inward, 3), (outward, 2), (dispatch, 1), (forward, 0), (outward, 3), (dispatch, 2),
        (forward, 1), (dispatch, 3), (forward, 2), (nearer, 0), (diagonal, 0), (nearer, 1),
        (farther, 0), (diagonal, 1), (forward, 3), (farther, 1), (nearer, 2), (diagonal, 2),
        (farther, 2), (nearer, 3),
    ):
        work(n)
    mixed_out = call(
        mixed_kernel,
        like((tokens, model)),
        [place, moved["mixed"]] + mixed,
        deps=last[:],
        specs=[SM] + [VM] * (GROUPS + 1),
    )
    diagonal(3)
    farther(3)
    return (mixed_out, hidden[None])


def entering(value, axis, combine, identity):
    devices, position = (lax.axis_size(axis), lax.axis_index(axis))
    everything = jax.tree.map(lambda part: lax.all_gather(part, axis), value)
    start = jax.tree.map(
        lambda part, zero: jnp.broadcast_to(jnp.asarray(zero, part.dtype), part.shape),
        value,
        identity,
    )

    def hop(k, before):
        reached = k < position
        new = combine(before, jax.tree.map(lambda part: part[k], everything))
        return jax.tree.map(lambda a, b: jnp.where(reached, a, b), new, before)

    return lax.fori_loop(0, devices, hop, start)


def route_slots(id_rows):
    count = id_rows.shape[1]
    same = id_rows[:, :, None] == id_rows[:, None, :]
    before = lax.broadcasted_iota(jnp.int32, (count, count), 1) < lax.broadcasted_iota(
        jnp.int32, (count, count), 0
    )
    return jnp.sum((same & before[None]).astype(jnp.int32), axis=2)


def select_matrix(id_rows, slot_rows, owners, capacity):
    routes = id_rows.shape[1]
    places = jnp.arange(capacity, dtype=jnp.int32)
    hits = (id_rows[:, None, None, :] == owners[None, :, None, None]) & (
        slot_rows[:, None, None, :] == places[None, None, :, None]
    )
    to_token = (
        jnp.arange(routes, dtype=jnp.int32)[:, None] // 2
        == jnp.arange(routes // 2, dtype=jnp.int32)[None, :]
    ).astype(jnp.float32)
    return jnp.einsum("bepr,rt->bept", hits.astype(jnp.float32), to_token)


def on_any_mesh(
    queries,
    key_rows,
    value_rows,
    decay_rate,
    out_weight,
    residual,
    moe_gain,
    expert_ids,
    gate_weight,
    up_weight,
):
    highest = lax.Precision.HIGHEST
    block_len = queries.shape[0]
    heads_here = decay_rate.shape[0]
    width_here = queries.shape[1]
    head_size = width_here // heads_here
    exp_count = lax.axis_size("exp")
    tok_count = block_len // exp_count
    capacity = max(2, 3 * tok_count // exp_count)
    query_here = queries.reshape(block_len, heads_here, head_size)
    key_here = key_rows.reshape(block_len, heads_here, head_size)
    value_here = value_rows.reshape(block_len, heads_here, head_size)
    position = jnp.arange(block_len, dtype=jnp.float32)
    offset = position[:, None] - position[None, :]
    masked = jnp.where(
        (offset >= 0)[None],
        jnp.exp(-decay_rate[:, None, None] * jnp.maximum(offset, 0.0)[None]),
        0.0,
    )
    inner = jnp.exp(-decay_rate[None, :] * position[:, None])
    tail = jnp.exp(-decay_rate[None, :] * (block_len - position[:, None]))
    whole = jnp.exp(-decay_rate * block_len)
    scores = jnp.einsum("ihd,jhd->hij", query_here, key_here, preferred_element_type=jnp.float32)
    weighted = (scores * masked).astype(jnp.bfloat16)
    local_part = jnp.einsum(
        "hij,jhd->ihd", weighted, value_here, preferred_element_type=jnp.float32
    )
    fresh = jnp.einsum(
        "jhd,jhe->hde",
        key_here.astype(jnp.float32) * tail[:, :, None],
        value_here.astype(jnp.float32),
        precision=highest,
    )

    def combine(earlier, later):
        return (earlier[0] * later[0], later[0][:, None, None] * earlier[1] + later[1])

    unused, state_in = entering(
        (whole, fresh), "ctx", combine, (jnp.ones_like(whole), jnp.zeros_like(fresh))
    )
    carried = (
        jnp.einsum("ihd,hde->ihe", query_here.astype(jnp.float32), state_in, precision=highest)
        * inner[:, :, None]
    )
    attended = local_part + carried
    scale_rows = lax.rsqrt(jnp.mean(attended * attended, axis=-1, keepdims=True) + 1e-05)
    head_out = (attended * scale_rows).astype(jnp.bfloat16).reshape(block_len, width_here)
    partial_rows = jnp.dot(
        head_out,
        lax.all_gather(out_weight, "ctx", axis=1, tiled=True),
        preferred_element_type=jnp.float32,
    )
    attn = lax.psum_scatter(partial_rows, "exp", scatter_dimension=0, tiled=True)
    mixed = (residual.astype(jnp.float32) + attn).astype(jnp.bfloat16)
    mixed_f = mixed.astype(jnp.float32)
    normed = (
        mixed_f * lax.rsqrt(jnp.mean(mixed_f * mixed_f, axis=-1, keepdims=True) + 1e-05) * moe_gain
    ).astype(jnp.bfloat16)
    id_rows = expert_ids.reshape(1, 2 * tok_count)
    slot_rows = route_slots(id_rows)
    picks = select_matrix(id_rows, slot_rows, jnp.arange(exp_count, dtype=jnp.int32), capacity)[0]
    picks = picks.reshape(exp_count * capacity, tok_count).astype(jnp.bfloat16)
    buffer = jnp.dot(picks, normed, preferred_element_type=jnp.float32).astype(jnp.bfloat16)
    received = lax.all_to_all(buffer, "exp", split_axis=0, concat_axis=0, tiled=True)
    gate_here = gate_weight[0]
    up_here = up_weight[0]
    contract = (((1,), (1,)), ((), ()))
    piece = lax.all_gather(received, "ctx", axis=0, tiled=True)
    gated = lax.dot_general(gate_here, piece, contract, preferred_element_type=jnp.float32)
    lifted = lax.dot_general(up_here, piece, contract, preferred_element_type=jnp.float32)
    hidden = (jax.nn.silu(gated) * lifted).astype(jnp.bfloat16)
    return (mixed, hidden[None])


def solution(mesh):
    in_specs = (
        P("ctx", "exp"),
        P("ctx", "exp"),
        P("ctx", "exp"),
        P("exp"),
        P("exp", "ctx"),
        P(("ctx", "exp"), None),
        P(),
        P(("ctx", "exp"), None),
        P("exp", "ctx", None),
        P("exp", "ctx", None),
    )
    out_specs = (P(("ctx", "exp"), None), P("exp", "ctx", None))
    square, line = mesh.shape["ctx"] == GROUPS * CORES, mesh.shape["exp"] == 4

    def per_device(*args):
        tokens, model = args[5].shape
        fits = square and line and 2 * tokens == LANES and args[3].shape[0] % CORES == 0
        fits = fits and model % (GROUPS * CORES * LANES) == 0
        return (on_square if fits else on_any_mesh)(*args)

    return jax.shard_map(
        per_device, mesh=mesh, in_specs=in_specs, out_specs=out_specs, check_vma=False
    )
```

```python
import functools

import jax
import jax.numpy as jnp
from jax import lax
from jax.experimental import pallas as pl
from jax.experimental.pallas import tpu as pltpu
from jax.sharding import PartitionSpec as P

GROUPS = 4
CORES = 2
ORDER = (0, 2, 1, 3)
LANES = 128
BF16 = jnp.bfloat16
F32 = jnp.float32
NT = (((1,), (1,)), ((), ()))
TN = (((0,), (0,)), ((), ()))
NN = (((1,), (0,)), ((), ()))
VM = pl.BlockSpec(memory_space=pltpu.VMEM)
SM = pl.BlockSpec(memory_space=pltpu.SMEM)
HBM = pl.BlockSpec(memory_space=pltpu.HBM)
ANY = pl.BlockSpec(memory_space=pl.ANY)


def dot(a, b, dims):
    return lax.dot_general(a, b, dims, preferred_element_type=F32)


def halves(x):
    high = x.astype(BF16)
    return high, (x - high.astype(F32)).astype(BF16)


def like(shape, dtype=BF16):
    return jax.ShapeDtypeStruct(tuple(shape), dtype)


def call(kernel, out_shape, operands, deps=(), specs=None, limit=12, **kwargs):
    count, extra = len(operands), len(deps)

    def body(*refs):
        kernel(*refs[:count], *refs[count + extra :])

    kwargs.setdefault("out_specs", jax.tree.map(lambda _: VM, out_shape))
    return pl.pallas_call(
        body,
        out_shape=out_shape,
        in_specs=list(specs or [VM] * count) + [ANY] * extra,
        compiler_params=pltpu.CompilerParams(vmem_limit_bytes=limit * 1024 * 1024),
        cost_estimate=pl.CostEstimate(flops=1, bytes_accessed=1, transcendentals=0),
        **kwargs,
    )(*operands, *deps)


def tile(index, size):
    return pl.ds(pl.multiple_of(index * size, size), size)


def fresh_kernel(place_ref, rate_ref, k_in, v_in, mine_ref, theirs_ref, k_ref, v_ref, sems):
    part, size = mine_ref.shape[0], mine_ref.shape[1]
    length = k_ref.shape[0]
    left = length - lax.broadcasted_iota(jnp.int32, (length, size), 0).astype(F32)
    order = ((theirs_ref, 1 - place_ref[1]), (mine_ref, place_ref[1]))
    copies = []
    for n, (_, half) in enumerate(order):
        at = tile(half, part * size)
        for source, target in ((k_in, k_ref), (v_in, v_ref)):
            copies.append(
                pltpu.make_async_copy(source.at[:, at], target.at[:, at], sems.at[len(copies)])
            )
            copies[-1].start()
    for n, (out_ref, half) in enumerate(order):
        copies[2 * n].wait()
        copies[2 * n + 1].wait()
        for j in range(part):
            head = half * part + j
            cols = tile(head, size)
            tail = jnp.exp(rate_ref[head] * left)
            high, low = halves(k_ref[:, cols].astype(F32) * tail)
            v = v_ref[:, cols]
            out_ref[j] = dot(high, v, TN) + dot(low, v, TN)


def local_kernel(rate_ref, q_in, k_ref, v_ref, out_ref, q_ref, sem):
    length, size = k_ref.shape[0], rate_ref.shape[2]
    heads = k_ref.shape[1] // size
    copy = pltpu.make_async_copy(q_in, q_ref, sem)
    copy.start()
    rows = lax.broadcasted_iota(jnp.int32, (length, length), 0)
    cols = lax.broadcasted_iota(jnp.int32, (length, length), 1)
    offset = (rows - cols).astype(F32)
    keep = offset >= 0
    offset = jnp.maximum(offset, 0.0)
    copy.wait()
    for h in range(heads):
        at = slice(h * size, (h + 1) * size)
        rate = jnp.concatenate([rate_ref[h]] * (length // LANES), axis=1)
        masked = jnp.where(keep, jnp.exp(rate * offset), 0.0)
        weighted = (dot(q_ref[:, at], k_ref[:, at], NT) * masked).astype(BF16)
        out_ref[:, at] = dot(weighted, v_ref[:, at], NN)


def mix_kernel(recipe, coef_ref, *refs):
    count = 1 + max(i for terms in recipe for i, _ in terms)
    part = refs[0].shape[0]
    first = CORES * part
    for j in range(part):
        values = [refs[i][j] for i in range(count)]
        for out_ref, terms in zip(refs[count:], recipe):
            out_ref[j] = sum(values[i] * coef_ref[first + row * part + j] for i, row in terms)


def scan_rows(chip, core, rate, part, length):
    rates = lax.dynamic_slice(rate, (core * part,), (part,))

    def fade(blocks):
        return jnp.exp(-rates * (length * blocks))

    one, none = jnp.ones_like(rates), jnp.zeros_like(rates)
    first, east, south = core == 0, (chip & 1) != 0, (chip & 2) != 0
    behind = jnp.where(south, fade(2.0 * (chip & 1).astype(F32)), none)
    keep, give = jnp.where(first, one, fade(1.0)), jnp.where(first, fade(1.0), one)
    return [
        jnp.where(first, one, none),
        jnp.where(first, none, one),
        jnp.where(first, fade(1.0), one),
        jnp.where(first, one, fade(1.0)),
        jnp.where(east, one, none),
        jnp.where(east, fade(2.0), one),
        jnp.where(east, one, fade(2.0)),
        keep,
        keep * behind,
        jnp.where(first, none, one),
        give,
        give * behind,
        jnp.where(first, one, none),
    ]


def head_kernel(place_ref, rate_ref, q_ref, local_ref, keep_ref, got_ref, out_ref):
    part, size = keep_ref.shape[0], keep_ref.shape[1]
    length = q_ref.shape[0]
    pos = lax.broadcasted_iota(jnp.int32, (length, size), 0).astype(F32)
    for state_ref, half in ((keep_ref, place_ref[1]), (got_ref, 1 - place_ref[1])):
        for j in range(part):
            head = half * part + j
            at = tile(head, size)
            high, low = halves(state_ref[j])
            q = q_ref[:, at]
            carried = dot(q, high, NN) + dot(q, low, NN)
            carried = carried * jnp.exp(rate_ref[head] * pos)
            attended = local_ref[:, at] + carried
            scale = lax.rsqrt(jnp.mean(attended * attended, axis=-1, keepdims=True) + 1e-05)
            out_ref[:, at] = (attended * scale).astype(BF16)


def larger_kernel(a_ref, b_ref, out_ref):
    out_ref[...] = jnp.maximum(a_ref[...], b_ref[...])


def stack_kernel(which, place_ref, a_ref, b_ref, out_ref):
    rows = a_ref.shape[0]
    upper = (place_ref[which] >> (1 if which == 2 else 0)) & 1
    out_ref[tile(upper, rows), :] = a_ref[...]
    out_ref[tile(1 - upper, rows), :] = b_ref[...]


def picks_kernel(tokens, capacity, place_ref, own_ref, got_ref, out_ref):
    slots = out_ref.shape[0]
    before = lax.broadcasted_iota(jnp.int32, (LANES, LANES), 0)
    token = lax.broadcasted_iota(jnp.int32, (LANES, LANES), 1)
    earlier = ((before < token) & (before // tokens == token // tokens)).astype(BF16)
    lane = lax.broadcasted_iota(jnp.int32, (8, LANES), 1)
    slot = lax.broadcasted_iota(jnp.int32, (slots, LANES), 0)
    per = own_ref.shape[0] // 8
    for ref, half in ((own_ref, place_ref[1]), (got_ref, 1 - place_ref[1])):
        for n in range(per):
            first, second = ref[8 * n : 8 * n + 1, :], ref[8 * n + 1 : 8 * n + 2, :]
            named = (first == place_ref[2]) | (second == place_ref[2])
            named = jnp.broadcast_to(named.astype(F32), (8, LANES))
            rank = dot(named.astype(BF16), earlier, NN).astype(jnp.int32)
            run = half * per + n
            row = (run * (LANES // tokens) + lane // tokens) * capacity + rank
            row = jnp.where((named > 0.5) & (rank < capacity), row, -1)
            out_ref[:, tile(run, LANES)] = (slot == row[0:1, :]).astype(BF16)


def project_kernel(t, place_ref, own_ref, got_ref, rest_ref, rest_got_ref, *refs):
    weights, (sum_ref, sent_ref) = refs[:-2], refs[-2:]
    length, tokens, cols = own_ref.shape[0], rest_ref.shape[0], sum_ref.shape[1]
    depth = own_ref.shape[1] // len(weights)
    at = tile((place_ref[0] ^ t) * CORES + place_ref[1], cols)
    for head_ref, row_ref, half in (
        (own_ref, rest_ref, place_ref[1]),
        (got_ref, rest_got_ref, 1 - place_ref[1]),
    ):
        value = 0.0
        for n, weight in enumerate(weights):
            value = value + dot(head_ref[:, n * depth : (n + 1) * depth], weight[...], NN)
        pieces = []
        for z in range(length // tokens):
            piece = value[z * tokens : (z + 1) * tokens, :]
            pieces.append(
                jnp.where(place_ref[2] == z, piece + row_ref[:, at].astype(F32), piece)
            )
        value = jnp.concatenate(pieces, axis=0)
        sum_ref[tile(half, length), :] = value
        sent_ref[tile(half, length), :] = value.astype(BF16)


def inward_kernel(part_ref, got_ref, sum_ref, sent_ref):
    total = part_ref[...] + got_ref[...].astype(F32)
    sum_ref[...] = total
    sent_ref[...] = total.astype(BF16)


def outer(place_ref):
    return (place_ref[2] == 0) | (place_ref[2] == 3)


def total_kernel(part_ref, got_ref, out_ref):
    out_ref[...] = (part_ref[...] + got_ref[...].astype(F32)).astype(BF16)


def dispatch_kernel(t, final, place_ref, got_ref, given_ref, gain_ref, picks_ref, *refs):
    earlier, (out_ref, mixed_ref), gives = refs[:-2], refs[-2:], []
    if final:
        earlier, (out_ref, mixed_ref, give_ref) = refs[:-3], refs[-3:]
        gives = [give_ref]
    cols = mixed_ref.shape[1]
    mixed = jnp.where(outer(place_ref), got_ref[...], given_ref[...])
    mixed_ref[...] = mixed
    value = mixed.astype(F32)
    gain = gain_ref[:, tile((place_ref[0] ^ t) * CORES + place_ref[1], cols)]
    out_ref[:, :cols] = dot(picks_ref[...], (value * gain).astype(BF16), NN).astype(BF16)
    if not gives:
        return
    squares = jnp.sum(value * value, axis=1, keepdims=True)
    for ref in earlier:
        value = ref[...].astype(F32)
        squares = squares + jnp.sum(value * value, axis=1, keepdims=True)
    extra = dot(picks_ref[...], in_three(squares), NN)
    out_ref[:, cols:] = extra.astype(BF16)
    tokens = give_ref.shape[0]
    per = mixed_ref.shape[0] // CORES // tokens
    rows = tile((1 - place_ref[1]) * per + place_ref[2], tokens)
    for n, ref in enumerate(list(earlier) + [mixed_ref]):
        give_ref[:, n * cols : (n + 1) * cols] = ref[rows, :]


def in_three(column):
    lane = lax.broadcasted_iota(jnp.int32, (column.shape[0], LANES), 1)
    rest, out = column, jnp.zeros((column.shape[0], LANES), F32)
    for place in range(3):
        high = rest.astype(BF16).astype(F32)
        out = jnp.where(lane == place, high, out)
        rest = rest - high
    return out.astype(BF16)


def pack_kernel(place_ref, own_ref, near_ref, far_ref, onward_ref, pack_ref):
    wide = own_ref.shape[1]
    onward_ref[...] = jnp.where(place_ref[1] == 0, near_ref[...], far_ref[...])
    for n, ref in enumerate((own_ref, near_ref, far_ref)):
        pack_ref[:, n * wide : (n + 1) * wide] = ref[...]


def copy_kernel(in_ref, out_ref):
    out_ref[...] = in_ref[...]


def rows_kernel(start, in_ref, out_ref):
    out_ref[...] = in_ref[start : start + out_ref.shape[0], :]


def mixed_kernel(place_ref, got_ref, *refs):
    mixed, (mark_ref, out_ref) = refs[:-2], refs[-2:]
    mark_ref[...] = jnp.zeros_like(mark_ref)
    tokens, cols = out_ref.shape[0], mixed[0].shape[1]
    per = mixed[0].shape[0] // CORES // tokens
    own = tile(place_ref[1] * per + place_ref[2], tokens)
    for t, ref in zip(ORDER, mixed):
        block = (place_ref[0] ^ t) * CORES
        n = ORDER.index(t)
        out_ref[:, tile(block + place_ref[1], cols)] = ref[own, :]
        out_ref[:, tile(block + 1 - place_ref[1], cols)] = got_ref[:, n * cols : (n + 1) * cols]


def expert_kernel(jobs, mode, held_sums, place_ref, gate_ref, up_ref, *refs):
    count = 1 + max(max(own, other) for _, terms in jobs for _, own, other, _ in terms)
    inputs, refs = refs[:count], list(refs[count:])
    sums = {s: (refs.pop(0), refs.pop(0)) for s, _ in jobs if s in held_sums}
    if mode == "next":
        refs.pop(0)
    model = gate_ref.shape[1]
    width = model // GROUPS
    cols = width // CORES
    if mode is None:
        outs, held = refs[:-1], refs[-1]
    else:
        outs, mark_ref, ready, sems, held = refs
        mark_ref[...] = jnp.zeros_like(mark_ref)
    copies, slot = [], 0
    for n, (s, terms) in enumerate(jobs):
        source = place_ref[0] ^ s
        gated, lifted = 0.0, 0.0
        if s in sums:
            gated, lifted = sums[s][0][...], sums[s][1][...]
        for t, own, other, part in terms:
            own_ref, other_ref = inputs[own], inputs[other]
            wide = own_ref.shape[1]
            held[slot, :, tile(place_ref[1], cols)] = own_ref[:, :cols]
            held[slot, :, tile(1 - place_ref[1], cols)] = other_ref[
                :, part * wide : part * wide + cols
            ]
            x = held[slot]
            slot += 1
            at = tile(source ^ t, width)
            gated = gated + dot(gate_ref[:, at], x, NT)
            lifted = lifted + dot(up_ref[:, at], x, NT)
        if mode is None:
            outs[2 * n][...] = gated
            outs[2 * n + 1][...] = lifted
            continue
        lane = lax.broadcasted_iota(jnp.int32, (8, LANES), 1)
        pick = (lane < 3).astype(BF16)
        squares = dot(pick, own_ref[:, cols:], NT)
        squares = squares + dot(pick, other_ref[:, part * wide + cols : (part + 1) * wide], NT)
        scale = lax.rsqrt(squares[0:1, :] / model + 1e-05)
        gated, lifted = gated * scale, lifted * scale
        silu = (0.5 * gated) * (1.0 + jnp.tanh(0.5 * gated))
        ready[n] = (silu * lifted).astype(BF16)
        at = tile(source, ready.shape[2])
        rows = ready.shape[1] // 4
        for q in range(4):
            piece = slice(q * rows, (q + 1) * rows)
            copies.append(
                pltpu.make_async_copy(ready.at[n, piece], outs.at[piece, at], sems.at[4 * n + q])
            )
            copies[-1].start()
    for copy in copies:
        copy.wait()


def expert_step(place, final, work, gate, up, sums, hidden, deps):
    hid, model = gate.shape
    width = model // GROUPS
    arrays = []

    def index(x):
        if not any(x is y for y in arrays):
            arrays.append(x)
        return [x is y for y in arrays].index(True)

    jobs = [(s, [(t, index(a), index(b), n) for t, a, b, n in terms]) for s, terms in work]
    slots = arrays[0].shape[0]
    operands = [place, gate, up] + arrays
    held_sums = [s for s, _ in jobs if s in sums]
    operands += [x for s in held_sums for x in sums[s]]
    specs = [SM] + [VM] * (len(operands) - 1)
    kwargs, mode, scratch = {}, None, []
    if final:
        mode = "first" if hidden is None else "next"
        if hidden is not None:
            kwargs["input_output_aliases"] = {len(operands): 0}
            operands.append(hidden)
            specs.append(ANY)
        out_shape = [like((hid, slots * GROUPS)), like((8, LANES), F32)]
        kwargs["out_specs"] = [ANY, VM]
        scratch += [
            pltpu.VMEM((len(jobs), hid, slots), BF16),
            pltpu.SemaphoreType.DMA((4 * len(jobs),)),
        ]
    else:
        out_shape = [like((hid, slots), F32)] * (2 * len(jobs))
    scratch.append(pltpu.VMEM((sum(len(terms) for _, terms in jobs), slots, width), BF16))
    out = call(
        functools.partial(expert_kernel, jobs, mode, held_sums),
        out_shape,
        operands,
        deps=deps,
        specs=specs,
        limit=24,
        scratch_shapes=scratch,
        **kwargs,
    )
    if mode:
        return out
    for n, (s, _) in enumerate(jobs):
        sums[s] = out[2 * n : 2 * n + 2]
    return hidden, out[0]


def send(x, axis, pairs):
    return lax.ppermute(x, axis, pairs)


def swap(x):
    return send(x, "ctx", [(d, d ^ 1) for d in range(lax.axis_size("ctx"))])


def onward(x):
    return send(x, "ctx", [(d, d ^ (2 if d % 2 else 4)) for d in range(lax.axis_size("ctx"))])


def on_square(
    queries,
    key_rows,
    value_rows,
    decay_rate,
    out_weight,
    residual,
    moe_gain,
    expert_ids,
    gate_weight,
    up_weight,
):
    ctx, exp = lax.axis_index("ctx"), lax.axis_index("exp")
    chip, core = ctx // CORES, lax.rem(ctx, CORES)
    place = jnp.stack([chip, core, exp]).astype(jnp.int32)
    length, here = queries.shape
    heads = decay_rate.shape[0]
    size = here // heads
    part = heads // CORES
    tokens, model = residual.shape
    cols = model // GROUPS // CORES
    capacity = max(2, 3 * tokens // lax.axis_size("exp"))
    every = CORES * length
    slots = every // tokens * capacity
    gate, up = gate_weight[0], up_weight[0]
    last = []

    def run(kernel, out_shape, operands, deps=(), **kwargs):
        out = call(kernel, out_shape, operands, list(last) + list(deps), **kwargs)
        last[:] = [out[0] if isinstance(out, (list, tuple)) else out]
        return out

    rows = jnp.stack(scan_rows(chip, core, decay_rate, part, length)).reshape(-1)
    rows = jnp.concatenate([-decay_rate, rows])
    table = jnp.broadcast_to(rows[:, None, None], (rows.shape[0], 1, LANES))
    ids = jnp.concatenate([expert_ids.T, expert_ids.T], axis=1)
    lane = jnp.arange(LANES, dtype=jnp.int32)[None, :]
    ids = jnp.where(lane // tokens == exp % (LANES // tokens), ids, -1)
    ids = jnp.pad(ids, ((0, 6), (0, 0)), constant_values=-1)
    gain = moe_gain[None, :]
    weight_y = send(out_weight, "ctx", [(d, d ^ 4) for d in range(8)])

    state_like = like((part, size, size), F32)
    mine, theirs, keys, values = run(
        fresh_kernel,
        [state_like] * 2 + [like((length, here))] * 2,
        [place, table, key_rows, value_rows],
        deps=[ids],
        specs=[SM, VM, HBM, HBM],
        scratch_shapes=[pltpu.SemaphoreType.DMA((4,))],
    )

    def mix(recipe, operands, deps=()):
        return run(
            functools.partial(mix_kernel, recipe),
            [state_like] * len(recipe),
            [table] + operands,
            deps=deps,
        )

    def copy(x):
        return run(copy_kernel, like(x.shape, x.dtype), [x])

    def cut(x, start):
        return run(
            functools.partial(rows_kernel, start), like((x.shape[0] // 2, x.shape[1])), [x]
        )

    got = swap(theirs)
    first, total = mix([[(0, 0), (1, 1)], [(0, 2), (1, 3)]], [mine, got])
    got = send(total, "ctx", [(d, d ^ 2) for d in range(8)])
    ids_got = send(ids, "exp", [(d, d ^ 1) for d in range(4)])
    rest_got = swap(residual)
    local, queries_here = run(
        local_kernel,
        [like((length, here), F32), like((length, here))],
        [table, queries, keys, values],
        specs=[VM, HBM, VM, VM],
        scratch_shapes=[pltpu.SemaphoreType.DMA(())],
    )
    ids = run(larger_kernel, like(ids.shape, ids.dtype), [ids, ids_got])
    state, total = mix([[(0, 4)], [(0, 5), (1, 6)]], [got, total], [rest_got, weight_y])
    got = send(total, "ctx", [(d, d + 4) for d in range(4)])
    weight_x = send(copy(out_weight), "ctx", [(d, d ^ 2) for d in range(8)])
    ids_got = send(ids, "exp", [(d, d ^ 2) for d in range(4)])
    ids = run(
        functools.partial(stack_kernel, 2),
        like((16, LANES), ids.dtype),
        [place, ids, ids_got],
        specs=[SM, VM, VM],
    )
    keep, give = mix(
        [[(0, 7), (1, 8), (2, 9)], [(0, 10), (1, 11), (2, 12)]], [state, got, first]
    )
    got = swap(give)
    ids_got = swap(ids)
    head_out = run(
        head_kernel,
        like((length, here)),
        [place, table, queries_here, local, keep, got],
        specs=[SM] + [VM] * 5,
    )
    heads_got = swap(head_out)

    chunk_f32, chunk_b16 = like((every, cols), F32), like((every, cols))
    end = GROUPS - 1
    wide = [cols + LANES * (n == end) for n in range(GROUPS)]
    weights = [[out_weight], [weight_y], [weight_x], None]
    parts, totals, mixed = [None] * 4, [None] * 4, [None] * 4
    moved = {}
    sums, hidden = {}, None

    def routes(n):
        moved["picks", n] = run(
            functools.partial(picks_kernel, tokens, capacity),
            like((slots, every)),
            [place, ids, ids_got],
            specs=[SM, VM, VM],
        )

    def project(n):
        parts[n], sent = run(
            functools.partial(project_kernel, ORDER[n]),
            [chunk_f32, chunk_b16],
            [place, head_out, heads_got, residual, rest_got] + weights[n],
            specs=[SM] + [VM] * (4 + len(weights[n])),
        )
        moved["in", n] = send(sent, "exp", [(0, 1), (3, 2)])

    def inward(n):
        parts[n], sent = run(
            inward_kernel, [chunk_f32, chunk_b16], [parts[n], moved["in", n]]
        )
        moved["across", n] = send(sent, "exp", [(1, 2), (2, 1)])

    def outward(n):
        totals[n] = run(total_kernel, chunk_b16, [parts[n], moved["across", n]])
        moved["out", n] = send(totals[n], "exp", [(1, 0), (2, 3)])

    def dispatch(n):
        outs = [like((slots, wide[n])), chunk_b16]
        known = []
        if n == end:
            outs.append(like((tokens, GROUPS * cols)))
            known = mixed[:n]
        x, mixed[n], *gives = run(
            functools.partial(dispatch_kernel, ORDER[n], n == end),
            outs,
            [place, moved["out", n], totals[n], gain, moved["picks", 0]] + known,
            specs=[SM] + [VM] * (4 + len(known)),
        )
        moved["own", n] = x
        moved["near", n] = send(x, "ctx", [(d, d ^ 2) for d in range(8)])
        moved["far", n] = send(x, "ctx", [(d, d ^ 4) for d in range(8)])
        if gives:
            moved["mixed"] = swap(gives[0])

    def forward(n):
        x = moved["own", n]
        out, pack = run(
            pack_kernel,
            [like(x.shape), like((slots, 3 * wide[n]))],
            [place, x, moved["near", n], moved["far", n]],
            specs=[SM] + [VM] * 3,
        )
        moved["diagonal", n] = onward(out)
        moved["others", n] = swap(pack)

    def diagonal(n):
        moved["diagonal", n] = copy(moved["diagonal", n])
        moved["rest", n] = swap(moved["diagonal", n])

    def near_terms(n):
        held = ("own", "near", "far")
        return [
            (s, [(ORDER[n], moved[name, n], moved["others", n], s)])
            for s, name in enumerate(held)
        ]

    def far_terms(*ns):
        return [(3, [(ORDER[n], moved["diagonal", n], moved["rest", n], 0) for n in ns])]

    def experts(n):
        nonlocal hidden
        work = near_terms(n) + (far_terms(n - 1) if 0 < n < end else [])
        hidden, mark = expert_step(place, n == end, work, gate, up, sums, hidden, last[:])
        last[:] = [mark]

    def finish(n):
        nonlocal hidden
        work = far_terms(n - 1, n)
        hidden, _ = expert_step(place, True, work, gate, up, sums, hidden, last[:])

    def finish_rows(n):
        mark, moved["rows"] = run(
            mixed_kernel,
            [like((8, LANES), F32), like((tokens, model))],
            [place, moved["mixed"]] + mixed,
            specs=[SM] + [VM] * (GROUPS + 1),
        )

    def fetch(n):
        top = send(cut(weight_x, 0), "ctx", [(d, d ^ 4) for d in range(8)])
        bottom = send(cut(weight_y, here // 2), "ctx", [(d, d ^ 2) for d in range(8)])
        weights[n] = [top, bottom]

    for work, n in (
        (project, 0), (project, 1), (routes, 0), (inward, 0), (fetch, 3), (project, 2),
        (inward, 1), (outward, 0), (project, 3), (inward, 2), (outward, 1), (dispatch, 0),
        (inward, 3), (outward, 2), (dispatch, 1), (forward, 0), (outward, 3), (dispatch, 2),
        (forward, 1), (dispatch, 3), (forward, 2), (experts, 0), (diagonal, 0), (experts, 1),
        (diagonal, 1), (forward, 3), (experts, 2), (diagonal, 2), (experts, 3), (diagonal, 3),
        (finish_rows, 0), (finish, 3),
    ):
        work(n)
    return (moved["rows"], hidden[None])


def entering(value, axis, combine, identity):
    devices, position = (lax.axis_size(axis), lax.axis_index(axis))
    everything = jax.tree.map(lambda part: lax.all_gather(part, axis), value)
    start = jax.tree.map(
        lambda part, zero: jnp.broadcast_to(jnp.asarray(zero, part.dtype), part.shape),
        value,
        identity,
    )

    def hop(k, before):
        reached = k < position
        new = combine(before, jax.tree.map(lambda part: part[k], everything))
        return jax.tree.map(lambda a, b: jnp.where(reached, a, b), new, before)

    return lax.fori_loop(0, devices, hop, start)


def route_slots(id_rows):
    count = id_rows.shape[1]
    same = id_rows[:, :, None] == id_rows[:, None, :]
    before = lax.broadcasted_iota(jnp.int32, (count, count), 1) < lax.broadcasted_iota(
        jnp.int32, (count, count), 0
    )
    return jnp.sum((same & before[None]).astype(jnp.int32), axis=2)


def select_matrix(id_rows, slot_rows, owners, capacity):
    routes = id_rows.shape[1]
    places = jnp.arange(capacity, dtype=jnp.int32)
    hits = (id_rows[:, None, None, :] == owners[None, :, None, None]) & (
        slot_rows[:, None, None, :] == places[None, None, :, None]
    )
    to_token = (
        jnp.arange(routes, dtype=jnp.int32)[:, None] // 2
        == jnp.arange(routes // 2, dtype=jnp.int32)[None, :]
    ).astype(jnp.float32)
    return jnp.einsum("bepr,rt->bept", hits.astype(jnp.float32), to_token)


def on_any_mesh(
    queries,
    key_rows,
    value_rows,
    decay_rate,
    out_weight,
    residual,
    moe_gain,
    expert_ids,
    gate_weight,
    up_weight,
):
    highest = lax.Precision.HIGHEST
    block_len = queries.shape[0]
    heads_here = decay_rate.shape[0]
    width_here = queries.shape[1]
    head_size = width_here // heads_here
    exp_count = lax.axis_size("exp")
    tok_count = block_len // exp_count
    capacity = max(2, 3 * tok_count // exp_count)
    query_here = queries.reshape(block_len, heads_here, head_size)
    key_here = key_rows.reshape(block_len, heads_here, head_size)
    value_here = value_rows.reshape(block_len, heads_here, head_size)
    position = jnp.arange(block_len, dtype=jnp.float32)
    offset = position[:, None] - position[None, :]
    masked = jnp.where(
        (offset >= 0)[None],
        jnp.exp(-decay_rate[:, None, None] * jnp.maximum(offset, 0.0)[None]),
        0.0,
    )
    inner = jnp.exp(-decay_rate[None, :] * position[:, None])
    tail = jnp.exp(-decay_rate[None, :] * (block_len - position[:, None]))
    whole = jnp.exp(-decay_rate * block_len)
    scores = jnp.einsum("ihd,jhd->hij", query_here, key_here, preferred_element_type=jnp.float32)
    weighted = (scores * masked).astype(jnp.bfloat16)
    local_part = jnp.einsum(
        "hij,jhd->ihd", weighted, value_here, preferred_element_type=jnp.float32
    )
    fresh = jnp.einsum(
        "jhd,jhe->hde",
        key_here.astype(jnp.float32) * tail[:, :, None],
        value_here.astype(jnp.float32),
        precision=highest,
    )

    def combine(earlier, later):
        return (earlier[0] * later[0], later[0][:, None, None] * earlier[1] + later[1])

    unused, state_in = entering(
        (whole, fresh), "ctx", combine, (jnp.ones_like(whole), jnp.zeros_like(fresh))
    )
    carried = (
        jnp.einsum("ihd,hde->ihe", query_here.astype(jnp.float32), state_in, precision=highest)
        * inner[:, :, None]
    )
    attended = local_part + carried
    scale_rows = lax.rsqrt(jnp.mean(attended * attended, axis=-1, keepdims=True) + 1e-05)
    head_out = (attended * scale_rows).astype(jnp.bfloat16).reshape(block_len, width_here)
    partial_rows = jnp.dot(
        head_out,
        lax.all_gather(out_weight, "ctx", axis=1, tiled=True),
        preferred_element_type=jnp.float32,
    )
    attn = lax.psum_scatter(partial_rows, "exp", scatter_dimension=0, tiled=True)
    mixed = (residual.astype(jnp.float32) + attn).astype(jnp.bfloat16)
    mixed_f = mixed.astype(jnp.float32)
    normed = (
        mixed_f * lax.rsqrt(jnp.mean(mixed_f * mixed_f, axis=-1, keepdims=True) + 1e-05) * moe_gain
    ).astype(jnp.bfloat16)
    id_rows = expert_ids.reshape(1, 2 * tok_count)
    slot_rows = route_slots(id_rows)
    picks = select_matrix(id_rows, slot_rows, jnp.arange(exp_count, dtype=jnp.int32), capacity)[0]
    picks = picks.reshape(exp_count * capacity, tok_count).astype(jnp.bfloat16)
    buffer = jnp.dot(picks, normed, preferred_element_type=jnp.float32).astype(jnp.bfloat16)
    received = lax.all_to_all(buffer, "exp", split_axis=0, concat_axis=0, tiled=True)
    gate_here = gate_weight[0]
    up_here = up_weight[0]
    contract = (((1,), (1,)), ((), ()))
    piece = lax.all_gather(received, "ctx", axis=0, tiled=True)
    gated = lax.dot_general(gate_here, piece, contract, preferred_element_type=jnp.float32)
    lifted = lax.dot_general(up_here, piece, contract, preferred_element_type=jnp.float32)
    hidden = (jax.nn.silu(gated) * lifted).astype(jnp.bfloat16)
    return (mixed, hidden[None])


def solution(mesh):
    in_specs = (
        P("ctx", "exp"),
        P("ctx", "exp"),
        P("ctx", "exp"),
        P("exp"),
        P("exp", "ctx"),
        P(("ctx", "exp"), None),
        P(),
        P(("ctx", "exp"), None),
        P("exp", "ctx", None),
        P("exp", "ctx", None),
    )
    out_specs = (P(("ctx", "exp"), None), P("exp", "ctx", None))
    square, line = mesh.shape["ctx"] == GROUPS * CORES, mesh.shape["exp"] == 4

    def per_device(*args):
        tokens, model = args[5].shape
        fits = square and line and 2 * tokens == LANES and args[3].shape[0] % CORES == 0
        fits = fits and model % (GROUPS * CORES * LANES) == 0
        return (on_square if fits else on_any_mesh)(*args)

    return jax.shard_map(
        per_device, mesh=mesh, in_specs=in_specs, out_specs=out_specs, check_vma=False
    )
```

```python
import functools

import jax
import jax.numpy as jnp
from jax import lax
from jax.experimental import pallas as pl
from jax.experimental.pallas import tpu as pltpu
from jax.sharding import PartitionSpec as P

GROUPS = 4
CORES = 2
ORDER = (0, 2, 1, 3)
LANES = 128
BF16 = jnp.bfloat16
F32 = jnp.float32
NT = (((1,), (1,)), ((), ()))
TN = (((0,), (0,)), ((), ()))
NN = (((1,), (0,)), ((), ()))
VM = pl.BlockSpec(memory_space=pltpu.VMEM)
SM = pl.BlockSpec(memory_space=pltpu.SMEM)
HBM = pl.BlockSpec(memory_space=pltpu.HBM)
ANY = pl.BlockSpec(memory_space=pl.ANY)


def dot(a, b, dims):
    return lax.dot_general(a, b, dims, preferred_element_type=F32)


def halves(x):
    high = x.astype(BF16)
    return high, (x - high.astype(F32)).astype(BF16)


def like(shape, dtype=BF16):
    return jax.ShapeDtypeStruct(tuple(shape), dtype)


def call(kernel, out_shape, operands, deps=(), specs=None, limit=12, **kwargs):
    count, extra = len(operands), len(deps)

    def body(*refs):
        kernel(*refs[:count], *refs[count + extra :])

    kwargs.setdefault("out_specs", jax.tree.map(lambda _: VM, out_shape))
    return pl.pallas_call(
        body,
        out_shape=out_shape,
        in_specs=list(specs or [VM] * count) + [ANY] * extra,
        compiler_params=pltpu.CompilerParams(vmem_limit_bytes=limit * 1024 * 1024),
        cost_estimate=pl.CostEstimate(flops=1, bytes_accessed=1, transcendentals=0),
        **kwargs,
    )(*operands, *deps)


def tile(index, size):
    return pl.ds(pl.multiple_of(index * size, size), size)


def fresh_kernel(place_ref, rate_ref, k_in, v_in, mine_ref, theirs_ref, k_ref, v_ref, sems):
    part, size = mine_ref.shape[0], mine_ref.shape[1]
    length = k_ref.shape[0]
    left = length - lax.broadcasted_iota(jnp.int32, (length, size), 0).astype(F32)
    order = ((theirs_ref, 1 - place_ref[1]), (mine_ref, place_ref[1]))
    copies = []
    for n, (_, half) in enumerate(order):
        at = tile(half, part * size)
        for source, target in ((k_in, k_ref), (v_in, v_ref)):
            copies.append(
                pltpu.make_async_copy(source.at[:, at], target.at[:, at], sems.at[len(copies)])
            )
            copies[-1].start()
    for n, (out_ref, half) in enumerate(order):
        copies[2 * n].wait()
        copies[2 * n + 1].wait()
        for j in range(part):
            head = half * part + j
            cols = tile(head, size)
            tail = jnp.exp(rate_ref[head] * left)
            high, low = halves(k_ref[:, cols].astype(F32) * tail)
            v = v_ref[:, cols]
            out_ref[j] = dot(high, v, TN) + dot(low, v, TN)


def local_kernel(rate_ref, q_in, k_ref, v_ref, out_ref, q_ref, sem):
    length, size = k_ref.shape[0], rate_ref.shape[2]
    heads = k_ref.shape[1] // size
    copy = pltpu.make_async_copy(q_in, q_ref, sem)
    copy.start()
    rows = lax.broadcasted_iota(jnp.int32, (length, length), 0)
    cols = lax.broadcasted_iota(jnp.int32, (length, length), 1)
    offset = (rows - cols).astype(F32)
    keep = offset >= 0
    offset = jnp.maximum(offset, 0.0)
    copy.wait()
    for h in range(heads):
        at = slice(h * size, (h + 1) * size)
        rate = jnp.concatenate([rate_ref[h]] * (length // LANES), axis=1)
        masked = jnp.where(keep, jnp.exp(rate * offset), 0.0)
        weighted = (dot(q_ref[:, at], k_ref[:, at], NT) * masked).astype(BF16)
        out_ref[:, at] = dot(weighted, v_ref[:, at], NN)


def mix_kernel(recipe, coef_ref, *refs):
    count = 1 + max(i for terms in recipe for i, _ in terms)
    part = refs[0].shape[0]
    first = CORES * part
    for j in range(part):
        values = [refs[i][j] for i in range(count)]
        for out_ref, terms in zip(refs[count:], recipe):
            out_ref[j] = sum(values[i] * coef_ref[first + row * part + j] for i, row in terms)


def scan_rows(chip, core, rate, part, length):
    rates = lax.dynamic_slice(rate, (core * part,), (part,))

    def fade(blocks):
        return jnp.exp(-rates * (length * blocks))

    one, none = jnp.ones_like(rates), jnp.zeros_like(rates)
    first, east, south = core == 0, (chip & 1) != 0, (chip & 2) != 0
    behind = jnp.where(south, fade(2.0 * (chip & 1).astype(F32)), none)
    keep, give = jnp.where(first, one, fade(1.0)), jnp.where(first, fade(1.0), one)
    return [
        jnp.where(first, one, none),
        jnp.where(first, none, one),
        jnp.where(first, fade(1.0), one),
        jnp.where(first, one, fade(1.0)),
        jnp.where(east, one, none),
        jnp.where(east, fade(2.0), one),
        jnp.where(east, one, fade(2.0)),
        keep,
        keep * behind,
        jnp.where(first, none, one),
        give,
        give * behind,
        jnp.where(first, one, none),
    ]


def head_kernel(place_ref, rate_ref, q_ref, local_ref, keep_ref, got_ref, out_ref):
    part, size = keep_ref.shape[0], keep_ref.shape[1]
    length = q_ref.shape[0]
    pos = lax.broadcasted_iota(jnp.int32, (length, size), 0).astype(F32)
    for state_ref, half in ((keep_ref, place_ref[1]), (got_ref, 1 - place_ref[1])):
        for j in range(part):
            head = half * part + j
            at = tile(head, size)
            high, low = halves(state_ref[j])
            q = q_ref[:, at]
            carried = dot(q, high, NN) + dot(q, low, NN)
            carried = carried * jnp.exp(rate_ref[head] * pos)
            attended = local_ref[:, at] + carried
            scale = lax.rsqrt(jnp.mean(attended * attended, axis=-1, keepdims=True) + 1e-05)
            out_ref[:, at] = (attended * scale).astype(BF16)


def larger_kernel(a_ref, b_ref, out_ref):
    out_ref[...] = jnp.maximum(a_ref[...], b_ref[...])


def stack_kernel(which, place_ref, a_ref, b_ref, out_ref):
    rows = a_ref.shape[0]
    upper = (place_ref[which] >> (1 if which == 2 else 0)) & 1
    out_ref[tile(upper, rows), :] = a_ref[...]
    out_ref[tile(1 - upper, rows), :] = b_ref[...]


def picks_kernel(tokens, capacity, place_ref, own_ref, got_ref, out_ref):
    slots = out_ref.shape[0]
    before = lax.broadcasted_iota(jnp.int32, (LANES, LANES), 0)
    token = lax.broadcasted_iota(jnp.int32, (LANES, LANES), 1)
    earlier = ((before < token) & (before // tokens == token // tokens)).astype(BF16)
    lane = lax.broadcasted_iota(jnp.int32, (8, LANES), 1)
    slot = lax.broadcasted_iota(jnp.int32, (slots, LANES), 0)
    per = own_ref.shape[0] // 8
    for ref, half in ((own_ref, place_ref[1]), (got_ref, 1 - place_ref[1])):
        for n in range(per):
            first, second = ref[8 * n : 8 * n + 1, :], ref[8 * n + 1 : 8 * n + 2, :]
            named = (first == place_ref[2]) | (second == place_ref[2])
            named = jnp.broadcast_to(named.astype(F32), (8, LANES))
            rank = dot(named.astype(BF16), earlier, NN).astype(jnp.int32)
            run = half * per + n
            row = (run * (LANES // tokens) + lane // tokens) * capacity + rank
            row = jnp.where((named > 0.5) & (rank < capacity), row, -1)
            out_ref[:, tile(run, LANES)] = (slot == row[0:1, :]).astype(BF16)


def project_kernel(t, place_ref, own_ref, got_ref, rest_ref, rest_got_ref, *refs):
    weights, (sum_ref, sent_ref) = refs[:-2], refs[-2:]
    length, tokens, cols = own_ref.shape[0], rest_ref.shape[0], sum_ref.shape[1]
    depth = own_ref.shape[1] // len(weights)
    at = tile((place_ref[0] ^ t) * CORES + place_ref[1], cols)
    for head_ref, row_ref, half in (
        (own_ref, rest_ref, place_ref[1]),
        (got_ref, rest_got_ref, 1 - place_ref[1]),
    ):
        value = 0.0
        for n, weight in enumerate(weights):
            value = value + dot(head_ref[:, n * depth : (n + 1) * depth], weight[...], NN)
        pieces = []
        for z in range(length // tokens):
            piece = value[z * tokens : (z + 1) * tokens, :]
            pieces.append(
                jnp.where(place_ref[2] == z, piece + row_ref[:, at].astype(F32), piece)
            )
        value = jnp.concatenate(pieces, axis=0)
        sum_ref[tile(half, length), :] = value
        sent_ref[tile(half, length), :] = value.astype(BF16)


def inward_kernel(part_ref, got_ref, sum_ref, sent_ref):
    total = part_ref[...] + got_ref[...].astype(F32)
    sum_ref[...] = total
    sent_ref[...] = total.astype(BF16)


def outer(place_ref):
    return (place_ref[2] == 0) | (place_ref[2] == 3)


def total_kernel(part_ref, got_ref, out_ref):
    out_ref[...] = (part_ref[...] + got_ref[...].astype(F32)).astype(BF16)


def dispatch_kernel(t, final, place_ref, got_ref, given_ref, gain_ref, picks_ref, *refs):
    earlier, (out_ref, mixed_ref), gives = refs[:-2], refs[-2:], []
    if final:
        earlier, (out_ref, mixed_ref, give_ref) = refs[:-3], refs[-3:]
        gives = [give_ref]
    cols = mixed_ref.shape[1]
    mixed = jnp.where(outer(place_ref), got_ref[...], given_ref[...])
    mixed_ref[...] = mixed
    value = mixed.astype(F32)
    gain = gain_ref[:, tile((place_ref[0] ^ t) * CORES + place_ref[1], cols)]
    out_ref[:, :cols] = dot(picks_ref[...], (value * gain).astype(BF16), NN).astype(BF16)
    if not gives:
        return
    squares = jnp.sum(value * value, axis=1, keepdims=True)
    for ref in earlier:
        value = ref[...].astype(F32)
        squares = squares + jnp.sum(value * value, axis=1, keepdims=True)
    extra = dot(picks_ref[...], in_three(squares), NN)
    out_ref[:, cols:] = extra.astype(BF16)
    tokens = give_ref.shape[0]
    per = mixed_ref.shape[0] // CORES // tokens
    rows = tile((1 - place_ref[1]) * per + place_ref[2], tokens)
    for n, ref in enumerate(list(earlier) + [mixed_ref]):
        give_ref[:, n * cols : (n + 1) * cols] = ref[rows, :]


def in_three(column):
    lane = lax.broadcasted_iota(jnp.int32, (column.shape[0], LANES), 1)
    rest, out = column, jnp.zeros((column.shape[0], LANES), F32)
    for place in range(3):
        high = rest.astype(BF16).astype(F32)
        out = jnp.where(lane == place, high, out)
        rest = rest - high
    return out.astype(BF16)


def pack_kernel(place_ref, own_ref, near_ref, far_ref, *refs):
    rows, (onward_ref, pack_ref) = refs[:-2], refs[-2:]
    slots, wide = own_ref.shape
    for ref in rows:
        pack_ref[slots:, : ref.shape[1]] = ref[...]
    onward_ref[...] = jnp.where(place_ref[1] == 0, near_ref[...], far_ref[...])
    for n, ref in enumerate((own_ref, near_ref, far_ref)):
        pack_ref[:slots, n * wide : (n + 1) * wide] = ref[...]


def copy_kernel(in_ref, out_ref):
    out_ref[...] = in_ref[...]


def rows_kernel(start, in_ref, out_ref):
    out_ref[...] = in_ref[start : start + out_ref.shape[0], :]


def mixed_kernel(place_ref, got_ref, *refs):
    mixed, (mark_ref, out_ref) = refs[:-2], refs[-2:]
    mark_ref[...] = jnp.zeros_like(mark_ref)
    tokens, cols = out_ref.shape[0], mixed[0].shape[1]
    per, first = mixed[0].shape[0] // CORES // tokens, got_ref.shape[0] - tokens
    own = tile(place_ref[1] * per + place_ref[2], tokens)
    for t, ref in zip(ORDER, mixed):
        block = (place_ref[0] ^ t) * CORES
        n = ORDER.index(t)
        out_ref[:, tile(block + place_ref[1], cols)] = ref[own, :]
        out_ref[:, tile(block + 1 - place_ref[1], cols)] = got_ref[first:, n * cols : (n + 1) * cols]


def expert_kernel(t, away, mode, has_sums, place_ref, gate_ref, up_ref, *refs):
    refs = list(refs)
    pieces, others = refs[: len(away)], refs[len(away)]
    refs = refs[len(away) + 1 :]
    sums = [[refs.pop(0), refs.pop(0)] for _ in away] if has_sums else None
    if mode == "next":
        refs.pop(0)
    model = gate_ref.shape[1]
    width = model // GROUPS
    cols, wide = width // CORES, pieces[0].shape[1]
    if mode is None:
        outs = refs[: 2 * len(away)]
        held = refs[2 * len(away)]
    else:
        outs, mark_ref, held, ready, sems = refs
        mark_ref[...] = jnp.zeros_like(mark_ref)
    copies = []
    for n, s in enumerate(away):
        source = place_ref[0] ^ s
        held[n, :, tile(place_ref[1], cols)] = pieces[n][:, :cols]
        slots = held.shape[1]
        held[n, :, tile(1 - place_ref[1], cols)] = others[:slots, n * wide : n * wide + cols]
        x = held[n]
        at = tile(source ^ t, width)
        gated = dot(gate_ref[:, at], x, NT)
        lifted = dot(up_ref[:, at], x, NT)
        if sums is not None:
            gated = gated + sums[n][0][...]
            lifted = lifted + sums[n][1][...]
        if mode is None:
            outs[2 * n][...] = gated
            outs[2 * n + 1][...] = lifted
            continue
        lane = lax.broadcasted_iota(jnp.int32, (8, LANES), 1)
        pick = (lane < 3).astype(BF16)
        squares = dot(pick, pieces[n][:, cols:], NT)
        extra = others[:slots, n * wide + cols : (n + 1) * wide]
        squares = squares + dot(pick, extra, NT)
        scale = lax.rsqrt(squares[0:1, :] / model + 1e-05)
        gated, lifted = gated * scale, lifted * scale
        silu = (0.5 * gated) * (1.0 + jnp.tanh(0.5 * gated))
        ready[n] = (silu * lifted).astype(BF16)
        at = tile(source, ready.shape[2])
        rows = ready.shape[1] // 4
        for q in range(4):
            part = slice(q * rows, (q + 1) * rows)
            copies.append(
                pltpu.make_async_copy(ready.at[n, part], outs.at[part, at], sems.at[4 * n + q])
            )
            copies[-1].start()
    for copy in copies:
        copy.wait()


def expert_step(place, t, final, away, pieces, others, gate, up, sums, hidden, deps):
    hid, model = gate.shape
    width = model // GROUPS
    slots = pieces[0].shape[0]
    operands = [place, gate, up] + pieces + [others]
    has_sums = away[0] in sums
    if has_sums:
        operands += [x for s in away for x in sums[s]]
    specs = [SM] + [VM] * (len(operands) - 1)
    kwargs, mode = {}, None
    scratch = [pltpu.VMEM((len(away), slots, width), BF16)]
    if final:
        mode = "first" if hidden is None else "next"
        if hidden is not None:
            kwargs["input_output_aliases"] = {len(operands): 0}
            operands.append(hidden)
            specs.append(ANY)
        out_shape = [like((hid, slots * GROUPS)), like((8, LANES), F32)]
        kwargs["out_specs"] = [ANY, VM]
        scratch += [
            pltpu.VMEM((len(away), hid, slots), BF16),
            pltpu.SemaphoreType.DMA((4 * len(away),)),
        ]
    else:
        out_shape = [like((hid, slots), F32)] * (2 * len(away))
    out = call(
        functools.partial(expert_kernel, t, away, mode, has_sums),
        out_shape,
        operands,
        deps=deps,
        specs=specs,
        limit=20,
        scratch_shapes=scratch,
        **kwargs,
    )
    if mode:
        return out
    for n, s in enumerate(away):
        sums[s] = out[2 * n : 2 * n + 2]
    return hidden, out[0]


def send(x, axis, pairs):
    return lax.ppermute(x, axis, pairs)


def swap(x):
    return send(x, "ctx", [(d, d ^ 1) for d in range(lax.axis_size("ctx"))])


def onward(x):
    return send(x, "ctx", [(d, d ^ (2 if d % 2 else 4)) for d in range(lax.axis_size("ctx"))])


def on_square(
    queries,
    key_rows,
    value_rows,
    decay_rate,
    out_weight,
    residual,
    moe_gain,
    expert_ids,
    gate_weight,
    up_weight,
):
    ctx, exp = lax.axis_index("ctx"), lax.axis_index("exp")
    chip, core = ctx // CORES, lax.rem(ctx, CORES)
    place = jnp.stack([chip, core, exp]).astype(jnp.int32)
    length, here = queries.shape
    heads = decay_rate.shape[0]
    size = here // heads
    part = heads // CORES
    tokens, model = residual.shape
    cols = model // GROUPS // CORES
    capacity = max(2, 3 * tokens // lax.axis_size("exp"))
    every = CORES * length
    slots = every // tokens * capacity
    gate, up = gate_weight[0], up_weight[0]
    last = []

    def run(kernel, out_shape, operands, deps=(), **kwargs):
        out = call(kernel, out_shape, operands, list(last) + list(deps), **kwargs)
        last[:] = [out[0] if isinstance(out, (list, tuple)) else out]
        return out

    rows = jnp.stack(scan_rows(chip, core, decay_rate, part, length)).reshape(-1)
    rows = jnp.concatenate([-decay_rate, rows])
    table = jnp.broadcast_to(rows[:, None, None], (rows.shape[0], 1, LANES))
    ids = jnp.concatenate([expert_ids.T, expert_ids.T], axis=1)
    lane = jnp.arange(LANES, dtype=jnp.int32)[None, :]
    ids = jnp.where(lane // tokens == exp % (LANES // tokens), ids, -1)
    ids = jnp.pad(ids, ((0, 6), (0, 0)), constant_values=-1)
    gain = moe_gain[None, :]
    weight_y = send(out_weight, "ctx", [(d, d ^ 4) for d in range(8)])

    state_like = like((part, size, size), F32)
    mine, theirs, keys, values = run(
        fresh_kernel,
        [state_like] * 2 + [like((length, here))] * 2,
        [place, table, key_rows, value_rows],
        deps=[ids],
        specs=[SM, VM, HBM, HBM],
        scratch_shapes=[pltpu.SemaphoreType.DMA((4,))],
    )

    def mix(recipe, operands, deps=()):
        return run(
            functools.partial(mix_kernel, recipe),
            [state_like] * len(recipe),
            [table] + operands,
            deps=deps,
        )

    def copy(x):
        return run(copy_kernel, like(x.shape, x.dtype), [x])

    def cut(x, start):
        return run(
            functools.partial(rows_kernel, start), like((x.shape[0] // 2, x.shape[1])), [x]
        )

    got = swap(theirs)
    first, total = mix([[(0, 0), (1, 1)], [(0, 2), (1, 3)]], [mine, got])
    got = send(total, "ctx", [(d, d ^ 2) for d in range(8)])
    ids_got = send(ids, "exp", [(d, d ^ 1) for d in range(4)])
    rest_got = swap(residual)
    local, queries_here = run(
        local_kernel,
        [like((length, here), F32), like((length, here))],
        [table, queries, keys, values],
        specs=[VM, HBM, VM, VM],
        scratch_shapes=[pltpu.SemaphoreType.DMA(())],
    )
    ids = run(larger_kernel, like(ids.shape, ids.dtype), [ids, ids_got])
    state, total = mix([[(0, 4)], [(0, 5), (1, 6)]], [got, total], [rest_got, weight_y])
    got = send(total, "ctx", [(d, d + 4) for d in range(4)])
    weight_x = send(copy(out_weight), "ctx", [(d, d ^ 2) for d in range(8)])
    ids_got = send(ids, "exp", [(d, d ^ 2) for d in range(4)])
    ids = run(
        functools.partial(stack_kernel, 2),
        like((16, LANES), ids.dtype),
        [place, ids, ids_got],
        specs=[SM, VM, VM],
    )
    keep, give = mix(
        [[(0, 7), (1, 8), (2, 9)], [(0, 10), (1, 11), (2, 12)]], [state, got, first]
    )
    got = swap(give)
    ids_got = swap(ids)
    head_out = run(
        head_kernel,
        like((length, here)),
        [place, table, queries_here, local, keep, got],
        specs=[SM] + [VM] * 5,
    )
    heads_got = swap(head_out)

    chunk_f32, chunk_b16 = like((every, cols), F32), like((every, cols))
    end = GROUPS - 1
    wide = [cols + LANES * (n == end) for n in range(GROUPS)]
    weights = [[out_weight], [weight_y], [weight_x], None]
    parts, totals, mixed = [None] * 4, [None] * 4, [None] * 4
    moved = {}
    sums, hidden = {}, None

    def routes(n):
        moved["picks", n] = run(
            functools.partial(picks_kernel, tokens, capacity),
            like((slots, every)),
            [place, ids, ids_got],
            specs=[SM, VM, VM],
        )

    def project(n):
        parts[n], sent = run(
            functools.partial(project_kernel, ORDER[n]),
            [chunk_f32, chunk_b16],
            [place, head_out, heads_got, residual, rest_got] + weights[n],
            specs=[SM] + [VM] * (4 + len(weights[n])),
        )
        moved["in", n] = send(sent, "exp", [(0, 1), (3, 2)])

    def inward(n):
        parts[n], sent = run(
            inward_kernel, [chunk_f32, chunk_b16], [parts[n], moved["in", n]]
        )
        moved["across", n] = send(sent, "exp", [(1, 2), (2, 1)])

    def outward(n):
        totals[n] = run(total_kernel, chunk_b16, [parts[n], moved["across", n]])
        moved["out", n] = send(totals[n], "exp", [(1, 0), (2, 3)])

    def dispatch(n):
        outs = [like((slots, wide[n])), chunk_b16]
        known = []
        if n == end:
            outs.append(like((tokens, GROUPS * cols)))
            known = mixed[:n]
        x, mixed[n], *gives = run(
            functools.partial(dispatch_kernel, ORDER[n], n == end),
            outs,
            [place, moved["out", n], totals[n], gain, moved["picks", 0]] + known,
            specs=[SM] + [VM] * (4 + len(known)),
        )
        moved["own", n] = x
        moved["near", n] = send(x, "ctx", [(d, d ^ 2) for d in range(8)])
        moved["far", n] = send(x, "ctx", [(d, d ^ 4) for d in range(8)])
        if gives:
            moved["rows"] = gives[0]

    def forward(n):
        x = moved["own", n]
        rows = [moved["rows"]] if n == end else []
        out, pack = run(
            pack_kernel,
            [like(x.shape), like((slots + tokens * len(rows), 3 * wide[n]))],
            [place, x, moved["near", n], moved["far", n]] + rows,
            specs=[SM] + [VM] * (3 + len(rows)),
        )
        moved["diagonal", n] = onward(out)
        moved["others", n] = swap(pack)

    def diagonal(n):
        moved["diagonal", n] = copy(moved["diagonal", n])
        moved["rest", n] = swap(moved["diagonal", n])

    def experts(n, away, pieces, others):
        nonlocal hidden
        hidden, mark = expert_step(
            place, ORDER[n], n == end, away, pieces, others, gate, up, sums, hidden, last[:]
        )
        last[:] = [mark]

    def nearer(n):
        pieces = [moved["own", n], moved["near", n], moved["far", n]]
        experts(n, (0, 1, 2), pieces, moved["others", n])

    def farther(n):
        experts(n, (3,), [moved["diagonal", n]], moved["rest", n])

    def finish_rows(n):
        mark, moved["out"] = run(
            mixed_kernel,
            [like((8, LANES), F32), like((tokens, model))],
            [place, moved["others", end]] + mixed,
            specs=[SM] + [VM] * (GROUPS + 1),
        )

    def fetch(n):
        top = send(cut(weight_x, 0), "ctx", [(d, d ^ 4) for d in range(8)])
        bottom = send(cut(weight_y, here // 2), "ctx", [(d, d ^ 2) for d in range(8)])
        weights[n] = [top, bottom]

    for work, n in (
        (project, 0), (project, 1), (routes, 0), (inward, 0), (fetch, 3), (project, 2),
        (inward, 1), (outward, 0), (project, 3), (inward, 2), (outward, 1), (dispatch, 0),
        (inward, 3), (outward, 2), (dispatch, 1), (forward, 0), (outward, 3), (dispatch, 2),
        (forward, 1), (dispatch, 3), (forward, 2), (nearer, 0), (diagonal, 0), (nearer, 1),
        (farther, 0), (diagonal, 1), (forward, 3), (farther, 1), (nearer, 2), (diagonal, 2),
        (farther, 2), (nearer, 3),
        (diagonal, 3), (finish_rows, 0), (farther, 3),
    ):
        work(n)
    return (moved["out"], hidden[None])


def entering(value, axis, combine, identity):
    devices, position = (lax.axis_size(axis), lax.axis_index(axis))
    everything = jax.tree.map(lambda part: lax.all_gather(part, axis), value)
    start = jax.tree.map(
        lambda part, zero: jnp.broadcast_to(jnp.asarray(zero, part.dtype), part.shape),
        value,
        identity,
    )

    def hop(k, before):
        reached = k < position
        new = combine(before, jax.tree.map(lambda part: part[k], everything))
        return jax.tree.map(lambda a, b: jnp.where(reached, a, b), new, before)

    return lax.fori_loop(0, devices, hop, start)


def route_slots(id_rows):
    count = id_rows.shape[1]
    same = id_rows[:, :, None] == id_rows[:, None, :]
    before = lax.broadcasted_iota(jnp.int32, (count, count), 1) < lax.broadcasted_iota(
        jnp.int32, (count, count), 0
    )
    return jnp.sum((same & before[None]).astype(jnp.int32), axis=2)


def select_matrix(id_rows, slot_rows, owners, capacity):
    routes = id_rows.shape[1]
    places = jnp.arange(capacity, dtype=jnp.int32)
    hits = (id_rows[:, None, None, :] == owners[None, :, None, None]) & (
        slot_rows[:, None, None, :] == places[None, None, :, None]
    )
    to_token = (
        jnp.arange(routes, dtype=jnp.int32)[:, None] // 2
        == jnp.arange(routes // 2, dtype=jnp.int32)[None, :]
    ).astype(jnp.float32)
    return jnp.einsum("bepr,rt->bept", hits.astype(jnp.float32), to_token)


def on_any_mesh(
    queries,
    key_rows,
    value_rows,
    decay_rate,
    out_weight,
    residual,
    moe_gain,
    expert_ids,
    gate_weight,
    up_weight,
):
    highest = lax.Precision.HIGHEST
    block_len = queries.shape[0]
    heads_here = decay_rate.shape[0]
    width_here = queries.shape[1]
    head_size = width_here // heads_here
    exp_count = lax.axis_size("exp")
    tok_count = block_len // exp_count
    capacity = max(2, 3 * tok_count // exp_count)
    query_here = queries.reshape(block_len, heads_here, head_size)
    key_here = key_rows.reshape(block_len, heads_here, head_size)
    value_here = value_rows.reshape(block_len, heads_here, head_size)
    position = jnp.arange(block_len, dtype=jnp.float32)
    offset = position[:, None] - position[None, :]
    masked = jnp.where(
        (offset >= 0)[None],
        jnp.exp(-decay_rate[:, None, None] * jnp.maximum(offset, 0.0)[None]),
        0.0,
    )
    inner = jnp.exp(-decay_rate[None, :] * position[:, None])
    tail = jnp.exp(-decay_rate[None, :] * (block_len - position[:, None]))
    whole = jnp.exp(-decay_rate * block_len)
    scores = jnp.einsum("ihd,jhd->hij", query_here, key_here, preferred_element_type=jnp.float32)
    weighted = (scores * masked).astype(jnp.bfloat16)
    local_part = jnp.einsum(
        "hij,jhd->ihd", weighted, value_here, preferred_element_type=jnp.float32
    )
    fresh = jnp.einsum(
        "jhd,jhe->hde",
        key_here.astype(jnp.float32) * tail[:, :, None],
        value_here.astype(jnp.float32),
        precision=highest,
    )

    def combine(earlier, later):
        return (earlier[0] * later[0], later[0][:, None, None] * earlier[1] + later[1])

    unused, state_in = entering(
        (whole, fresh), "ctx", combine, (jnp.ones_like(whole), jnp.zeros_like(fresh))
    )
    carried = (
        jnp.einsum("ihd,hde->ihe", query_here.astype(jnp.float32), state_in, precision=highest)
        * inner[:, :, None]
    )
    attended = local_part + carried
    scale_rows = lax.rsqrt(jnp.mean(attended * attended, axis=-1, keepdims=True) + 1e-05)
    head_out = (attended * scale_rows).astype(jnp.bfloat16).reshape(block_len, width_here)
    partial_rows = jnp.dot(
        head_out,
        lax.all_gather(out_weight, "ctx", axis=1, tiled=True),
        preferred_element_type=jnp.float32,
    )
    attn = lax.psum_scatter(partial_rows, "exp", scatter_dimension=0, tiled=True)
    mixed = (residual.astype(jnp.float32) + attn).astype(jnp.bfloat16)
    mixed_f = mixed.astype(jnp.float32)
    normed = (
        mixed_f * lax.rsqrt(jnp.mean(mixed_f * mixed_f, axis=-1, keepdims=True) + 1e-05) * moe_gain
    ).astype(jnp.bfloat16)
    id_rows = expert_ids.reshape(1, 2 * tok_count)
    slot_rows = route_slots(id_rows)
    picks = select_matrix(id_rows, slot_rows, jnp.arange(exp_count, dtype=jnp.int32), capacity)[0]
    picks = picks.reshape(exp_count * capacity, tok_count).astype(jnp.bfloat16)
    buffer = jnp.dot(picks, normed, preferred_element_type=jnp.float32).astype(jnp.bfloat16)
    received = lax.all_to_all(buffer, "exp", split_axis=0, concat_axis=0, tiled=True)
    gate_here = gate_weight[0]
    up_here = up_weight[0]
    contract = (((1,), (1,)), ((), ()))
    piece = lax.all_gather(received, "ctx", axis=0, tiled=True)
    gated = lax.dot_general(gate_here, piece, contract, preferred_element_type=jnp.float32)
    lifted = lax.dot_general(up_here, piece, contract, preferred_element_type=jnp.float32)
    hidden = (jax.nn.silu(gated) * lifted).astype(jnp.bfloat16)
    return (mixed, hidden[None])


def solution(mesh):
    in_specs = (
        P("ctx", "exp"),
        P("ctx", "exp"),
        P("ctx", "exp"),
        P("exp"),
        P("exp", "ctx"),
        P(("ctx", "exp"), None),
        P(),
        P(("ctx", "exp"), None),
        P("exp", "ctx", None),
        P("exp", "ctx", None),
    )
    out_specs = (P(("ctx", "exp"), None), P("exp", "ctx", None))
    square, line = mesh.shape["ctx"] == GROUPS * CORES, mesh.shape["exp"] == 4

    def per_device(*args):
        tokens, model = args[5].shape
        fits = square and line and 2 * tokens == LANES and args[3].shape[0] % CORES == 0
        fits = fits and model % (GROUPS * CORES * LANES) == 0
        return (on_square if fits else on_any_mesh)(*args)

    return jax.shard_map(
        per_device, mesh=mesh, in_specs=in_specs, out_specs=out_specs, check_vma=False
    )
```
